32 devices in a mesh: lat: 8 (over y, x, core), var: 4 (over z).
Axes of the slice: x: 2, y: 2, z: 4, core: 2. Of those that a mesh axis runs over, the one named last changes fastest.
Arguments:
- patches: bfloat16 [48, 96, 1024], P('lat', 'var'), may hold values from -6 to 6
- norm_gain: float32 [1024], replicated, may hold values from 0.25 to 1.75
- input_proj: bfloat16 [1024, 3072], replicated, may hold values from -7 to 7
- output_proj: bfloat16 [1024, 1024], replicated, may hold values from -0.1875 to 0.1875
- level_scale: float32 [40, 1024], P('var'), may hold values from 0.1 to 1.9
- level_shift: float32 [40, 1024], P('var'), may hold values from -3 to 3
- head_weight: bfloat16 [40, 1024, 320], P('var', 'lat'), may hold values from -0.1875 to 0.1875
- targets: bfloat16 [40, 48, 96, 320], P('var', 'lat'), may hold values from -6 to 6
- level_counts: int32 [4], replicated, may hold values from 13 to 37
- tile_dataset: int32 [8, 4], P('lat'), may hold values from 0 to 3
- slot_level: int32 [40], P('var'), may hold values from 0 to 39, as said below
Outputs:
- latent: bfloat16 [48, 96, 1024], P('lat', 'var')
- grad_latent: bfloat16 [48, 96, 1024], P('lat', 'var')
- grad_head: float32 [40, 1024, 320], P('var', 'lat')
The draws below stay inside these ranges and needn't reach their ends.
Inputs may be any that keep to these rules, and one draw needn't show every extreme that they name: `slot_level`: for each j, slots j * 10 to (j + 1) * 10 - 1 hold the levels j * 10 to (j + 1) * 10 - 1 in some order.
All inputs are finite; a program needn't handle non-finite values.
Results may differ from the reference program's by a relative error of at most 0.012.
Values may be sent and summed in bfloat16 or wider, within the bound.
No kernel may reach another device: no remote copies, remote signals or barrier semaphores. Data moves between devices by JAX's collectives and lax.ppermute only.
A program may use at most 128 MiB of HBM per device.

```python
import math
import jax
import jax.numpy as jnp
from jax import lax

D = 1024
HEADS = 16
WH = 6
WW = 12
BR = 6
BC = 24
OUT = 320
LEVELS = 37
LV_PAD = 40
DATASETS = 4
LPO = 10
NLAT_P = 48
NLON_P = 96
N_LAT = 8
N_VAR = 4


def draw_input_proj(key, part):
    base = jax.random.normal(key, (D, 3 * D), jnp.float32) / math.sqrt(D)
    base = jnp.clip(base, -6.0 / math.sqrt(D), 6.0 / math.sqrt(D))
    return base.astype(jnp.bfloat16)


def one_block(block_key):
    return jax.random.permutation(block_key, LPO).astype(jnp.int32)


def draw_slot_level(key, part):
    block_keys = jax.random.split(jax.random.fold_in(key, 23), N_VAR)
    orders = jax.vmap(one_block)(block_keys)
    offsets = jnp.arange(N_VAR, dtype=jnp.int32)[:, None] * LPO
    return (orders + offsets).reshape(LV_PAD)


def with_ends(array, key, smallest, high):
    dims = array.shape
    index_at = [jax.random.randint(jax.random.fold_in(key, axis), (), 0, dims[axis]) for axis in range(len(dims))]
    array = array.at[tuple(index_at)].set(smallest)
    longest = dims.index(max(dims))
    index_at[longest] = (index_at[longest] + 1) % dims[longest]
    return array.at[tuple(index_at)].set(high)


def shard_levels(stream_key, shape, pieces, smallest, top_value):
    level, own = 1.0, jax.random.fold_in(stream_key, 6)
    for axis_at, shards_of in pieces:
        steps = jnp.exp(jax.random.uniform(jax.random.fold_in(own, axis_at), (shards_of,), jnp.float32, smallest / len(pieces), top_value / len(pieces)))
        level = level * jnp.repeat(steps, shape[axis_at] // shards_of).reshape([-1 if axis == axis_at else 1 for axis in range(len(shape))])
    return level


def bell_draw(own_key, shape, scale, reach, cuts=(), held_as=jnp.bfloat16):
    level = shard_levels(own_key, shape, cuts, -0.22, 0.18) if cuts else 1.0
    array = jax.random.normal(own_key, shape, jnp.float32) * scale * level
    return jnp.minimum(jnp.maximum(array, -reach), reach).astype(held_as)


def setup_inputs(seed: int = 0) -> dict:
    key_of = jax.random.split(jax.random.key(seed), 12)
    patches = bell_draw(key_of[0], (NLAT_P, NLON_P, D), 1.0, 6.0, ((0, 8), (1, 4)))
    norm_gain = jnp.clip(1.0 + 0.15 * jax.random.normal(key_of[1], (D,), jnp.float32), 0.25, 1.75)
    input_proj = draw_input_proj(jax.random.fold_in(key_of[11], 71), 0)
    output_proj = bell_draw(key_of[3], (D, D), D ** -0.5, 0.1875)
    level_scale = jnp.clip(1.0 + 0.18 * jax.random.normal(key_of[4], (LV_PAD, D), jnp.float32), 0.1, 1.9)
    level_shift = bell_draw(key_of[5], (LV_PAD, D), 0.5, 3.0, ((0, 4),), jnp.float32)
    head_weight = bell_draw(key_of[6], (LV_PAD, D, OUT), D ** -0.5, 0.1875, ((0, 4), (1, 8)))
    targets = bell_draw(key_of[7], (LV_PAD, NLAT_P, NLON_P, OUT), 1.0, 6.0, ((0, 4), (1, 8)))
    level_counts = with_ends(jax.random.randint(key_of[8], (DATASETS,), 13, LEVELS + 1), jax.random.fold_in(key_of[8], 1), 13, LEVELS).astype(jnp.int32)
    tile_dataset = with_ends(jax.random.randint(key_of[9], (N_LAT, N_VAR), 0, DATASETS), jax.random.fold_in(key_of[9], 1), 0, DATASETS - 1).astype(jnp.int32)
    slot_level = draw_slot_level(jax.random.fold_in(key_of[11], 71), 0)
    return dict(patches=patches, norm_gain=norm_gain, input_proj=input_proj, output_proj=output_proj, level_scale=level_scale, level_shift=level_shift, head_weight=head_weight, targets=targets, level_counts=level_counts, tile_dataset=tile_dataset, slot_level=slot_level)


EPS = 1e-05

def layer_norm(values, gain):
    wide = values.astype(jnp.float32)
    average = lax.optimization_barrier(jnp.mean(wide, axis=-1, keepdims=True))
    centred = wide - average
    variance = lax.optimization_barrier(jnp.mean(centred * centred, axis=-1, keepdims=True))
    return (centred * lax.rsqrt(variance + EPS) * gain).astype(jnp.bfloat16)

def reference(patches, norm_gain, input_proj, output_proj, level_scale, level_shift, head_weight, targets, level_counts, tile_dataset, slot_level):
    nlat, nlon, width = patches.shape
    head_size = width // HEADS
    half_rows = WH // 2
    half_cols = WW // 2
    normed = layer_norm(patches, norm_gain)
    qkv = jnp.dot(normed.reshape(-1, width), input_proj, preferred_element_type=jnp.float32).astype(jnp.bfloat16)
    qkv = qkv.reshape(nlat, nlon, 3 * width)
    padded = jnp.pad(qkv, ((half_rows, WH - half_rows), (0, 0), (0, 0)))
    rolled = jnp.roll(padded, half_cols, axis=1)
    rows_pad = nlat + WH
    win_rows = rows_pad // WH
    win_cols = nlon // WW
    windows = rolled.reshape(win_rows, WH, win_cols, WW, 3, HEADS, head_size)
    windows = windows.transpose(0, 2, 1, 3, 4, 5, 6).reshape(win_rows * win_cols, WH * WW, 3, HEADS, head_size)
    query_win = windows[:, :, 0].astype(jnp.float32)
    key_win = windows[:, :, 1].astype(jnp.float32)
    value_win = windows[:, :, 2].astype(jnp.float32)
    row_ids = jnp.arange(rows_pad)
    row_valid = (row_ids >= half_rows) & (row_ids < half_rows + nlat)
    key_mask = jnp.broadcast_to(row_valid.reshape(win_rows, 1, WH, 1), (win_rows, win_cols, WH, WW)).reshape(win_rows * win_cols, WH * WW)
    scores = jnp.einsum('wqhd,wkhd->whqk', query_win, key_win) / math.sqrt(head_size)
    scores = jnp.where(key_mask[:, None, None, :], scores, -jnp.inf)
    peak = lax.optimization_barrier(jnp.max(scores, axis=-1, keepdims=True))
    weights = jnp.exp(scores - peak)
    probs = (weights / lax.optimization_barrier(jnp.sum(weights, axis=-1, keepdims=True))).astype(jnp.bfloat16)
    mixed = jnp.einsum('whqk,wkhd->wqhd', probs.astype(jnp.float32), value_win)
    mixed = mixed.reshape(win_rows, win_cols, WH, WW, width).transpose(0, 2, 1, 3, 4).reshape(rows_pad, nlon, width)
    mixed = jnp.roll(mixed, -half_cols, axis=1)[half_rows:half_rows + nlat]
    attn = mixed.astype(jnp.bfloat16)
    update = jnp.dot(attn.reshape(-1, width), output_proj, preferred_element_type=jnp.float32).reshape(nlat, nlon, width)
    latent = (patches.astype(jnp.float32) + update).astype(jnp.bfloat16)
    tile_levels = level_counts[tile_dataset]
    live = (slot_level[:, None, None] < tile_levels[None]).astype(jnp.float32)
    live_grid = jnp.repeat(jnp.repeat(live, BR, axis=1), BC, axis=2)
    latent_wide = latent.astype(jnp.float32)
    head_norm = 1.0 / math.sqrt(NLAT_P * NLON_P)

    def per_slot(carry, slot_inputs):
        scale, shift, weight, target, mask = slot_inputs
        rows = (latent_wide * scale + shift).astype(jnp.bfloat16).reshape(-1, width)
        predicted = jnp.dot(rows, weight, preferred_element_type=jnp.float32)
        errors = ((predicted - target.reshape(-1, OUT).astype(jnp.float32)) * mask.reshape(-1, 1)).astype(jnp.bfloat16)
        back_grad = jnp.dot(errors, weight.T, preferred_element_type=jnp.float32) * scale
        grad_slot = jnp.dot(rows.T, errors, preferred_element_type=jnp.float32) * head_norm
        return (carry + back_grad, grad_slot)
    start = jnp.zeros((nlat * nlon, width), jnp.float32)
    total, grad_head = lax.scan(per_slot, start, (level_scale, level_shift, head_weight, targets, live_grid))
    grad_latent = total.reshape(nlat, nlon, width).astype(jnp.bfloat16)
    return (latent, grad_latent, grad_head)
```

```python
import functools
import math

import jax
import jax.numpy as jnp
import numpy as np
from jax import lax
from jax.experimental import pallas as pl
from jax.experimental.pallas import tpu as pltpu
from jax.sharding import PartitionSpec as P

HEADS = 16
WH = 6
WW = 12
EPS = 1e-05
HR = WH // 2
HC = WW // 2
QP = 48
LEFT = 8
VMEM_LIMIT = 48 * 1024 * 1024
F32 = jnp.float32
BF16 = jnp.bfloat16


def source_base(cols):
    own = 0
    left = own + WH * cols
    above = left + WH * LEFT
    above_left = above + HR * cols
    below = above_left + HR * LEFT
    below_left = below + HR * cols
    total = below_left + HR * LEFT
    return own, left, above, above_left, below, below_left, total


def gather_maps(cols):
    own, left, above, above_left, below, below_left, total = source_base(cols)
    win_cols = cols // WW
    windows = 2 * win_cols

    def source(part, win_row, row, col):
        if part == 0:
            r = win_row * HR + row
            return left + r * LEFT + col if col < HC else own + r * cols + col - HC
        if win_row == 0:
            return above_left + row * LEFT + col if col < HC else above + row * cols + col - HC
        return below_left + row * LEFT + col if col < HC else below + row * cols + col - HC

    into = np.zeros((windows * 2 * QP, total), np.float32)
    keep = np.zeros((WH * cols, total), np.float32)
    back = np.zeros((WH * cols, windows * QP), np.float32)
    for win in range(windows):
        win_row, win_col = divmod(win, win_cols)
        for part in range(2):
            for row in range(HR):
                for c in range(WW):
                    at = source(part, win_row, row, win_col * WW + c)
                    slot = row * WW + c
                    into[win * 2 * QP + part * QP + slot, at] = 1
                    if part == 0:
                        natural = (win_row * HR + row) * cols + win_col * WW + c
                        keep[natural, at] = 1
                        back[natural, win * QP + slot] = 1
    return into, keep, back


def attention_kernel(
    bands,
    place,
    own,
    left,
    above,
    above_left,
    below,
    below_left,
    gain,
    into,
    keep,
    back,
    proj_in,
    proj_out,
    out,
    raw,
    qkv,
    attn,
):
    cols, width = own.shape[1], own.shape[2]
    bases = source_base(cols)
    windows = 2 * (cols // WW)
    head_size = width // HEADS
    quad = 256 // head_size
    for base, ref in zip(bases, (own, left, above, above_left, below, below_left)):
        count = ref.shape[0]
        if ref.shape[1] == cols:
            raw[base : base + count * cols, :] = ref[...].astype(F32).reshape(count * cols, width)
        else:
            for r in range(count):
                raw[base + r * LEFT : base + (r + 1) * LEFT, :] = jnp.zeros((LEFT, width), F32)
                raw[base + r * LEFT : base + r * LEFT + HC, :] = ref[r].astype(F32)
    wide = raw[...]
    average = jnp.mean(wide, axis=-1, keepdims=True)
    centred = wide - average
    variance = jnp.mean(centred * centred, axis=-1, keepdims=True)
    normed = (centred * lax.rsqrt(variance + EPS) * gain[...]).astype(BF16)
    win_x = jnp.dot(into[...], normed, preferred_element_type=F32).astype(BF16)
    step = 512
    for j in range(3 * width // step):
        part = slice(j * step, (j + 1) * step)
        qkv[:, part] = jnp.dot(win_x, proj_in[:, part], preferred_element_type=F32).astype(BF16)
    lane = lax.broadcasted_iota(jnp.int32, (1, 256), 1) // head_size
    heads = [jnp.where(lane == h, 1.0, 0.0) for h in range(quad)]
    key_id = lax.broadcasted_iota(jnp.int32, (1, 2 * QP), 1)
    scale = 1.0 / math.sqrt(head_size)
    for win in range(windows):
        win_row = win // (cols // WW)
        edge = 0 if win_row == 0 else bands - 1
        has_halo = place[0] != edge
        halo_keys = jnp.logical_and(key_id >= QP, key_id < QP + HR * WW)
        valid = jnp.logical_or(key_id < HR * WW, jnp.logical_and(halo_keys, has_halo))
        bias = jnp.where(valid, 0.0, -1e30)
        row0 = win * 2 * QP
        for g in range(width // 256):
            lanes = slice(g * 256, (g + 1) * 256)
            query = qkv[row0 : row0 + QP, lanes].astype(F32) * scale
            stacked = jnp.concatenate([query * h for h in heads], axis=0).astype(BF16)
            key = qkv[row0 : row0 + 2 * QP, width + g * 256 : width + (g + 1) * 256]
            value = qkv[row0 : row0 + 2 * QP, 2 * width + g * 256 : 2 * width + (g + 1) * 256]
            scores = (
                lax.dot_general(
                    stacked, key, (((1,), (1,)), ((), ())), preferred_element_type=F32
                )
                + bias
            )
            weights = jnp.exp(scores - jnp.max(scores, axis=-1, keepdims=True))
            probs = (weights / jnp.sum(weights, axis=-1, keepdims=True)).astype(BF16)
            mixed = jnp.dot(probs, value, preferred_element_type=F32)
            chosen = mixed[0:QP] * heads[0]
            for h in range(1, quad):
                chosen = chosen + mixed[h * QP : (h + 1) * QP] * heads[h]
            attn[win * QP : (win + 1) * QP, lanes] = chosen.astype(BF16)
    ordered = jnp.dot(back[...], attn[...], preferred_element_type=F32).astype(BF16)
    update = jnp.dot(ordered, proj_out[...], preferred_element_type=F32)
    residual = jnp.dot(keep[...], raw[...].astype(BF16), preferred_element_type=F32)
    out[...] = (residual + update).astype(BF16)


def attention(place, pieces, gain, proj_in, proj_out, bands):
    rows, cols, width = pieces[0].shape
    into, keep, back = gather_maps(cols)
    total = source_base(cols)[-1]
    windows = 2 * (cols // WW)
    vmem = pl.BlockSpec(memory_space=pltpu.VMEM)
    return pl.pallas_call(
        functools.partial(attention_kernel, bands),
        out_shape=jax.ShapeDtypeStruct((rows * cols, width), BF16),
        in_specs=[pl.BlockSpec(memory_space=pltpu.SMEM)] + [vmem] * 12,
        out_specs=vmem,
        scratch_shapes=[
            pltpu.VMEM((total, width), F32),
            pltpu.VMEM((windows * 2 * QP, 3 * width), BF16),
            pltpu.VMEM((windows * QP, width), BF16),
        ],
        compiler_params=pltpu.CompilerParams(vmem_limit_bytes=VMEM_LIMIT),
        cost_estimate=pl.CostEstimate(
            flops=6_000_000_000, bytes_accessed=12_000_000, transcendentals=400_000
        ),
        name="window_attention",
    )(
        place,
        *pieces,
        gain.reshape(1, width),
        jnp.asarray(into, BF16),
        jnp.asarray(keep, BF16),
        jnp.asarray(back, BF16),
        proj_in,
        proj_out,
    )


def band_map(tiles, cols):
    wide = tiles * cols
    chosen = np.zeros((WH * wide, WH * wide), np.float32)
    for r in range(WH):
        for c in range(wide):
            tile, at = divmod((c + HC) % wide, cols)
            chosen[r * wide + c, tile * WH * cols + r * cols + at] = 1
    return chosen


def band_kernel(tiles, cols, place, chosen, *refs):
    pieces, (band, latent, laid, wide) = refs[:tiles], refs[tiles:]
    size = WH * cols
    var = place[1]
    for s in range(tiles):
        tile = lax.rem(var + tiles - s, tiles)
        laid[pl.ds(pl.multiple_of(tile * size, 16), size), :] = pieces[s][...]
    wide[...] = jnp.dot(chosen[...], laid[...], preferred_element_type=F32)
    band[...] = wide[...].astype(BF16)
    for r in range(WH):
        start = pl.multiple_of(r * tiles * cols + var * cols, 8)
        latent[r] = wide[pl.ds(start, cols), :].astype(BF16)


def band_latents(place, pieces, cols):
    tiles = len(pieces)
    width = pieces[0].shape[1]
    total = WH * tiles * cols
    vmem = pl.BlockSpec(memory_space=pltpu.VMEM)
    return pl.pallas_call(
        functools.partial(band_kernel, tiles, cols),
        out_shape=(
            jax.ShapeDtypeStruct((total, width), BF16),
            jax.ShapeDtypeStruct((WH, cols, width), BF16),
        ),
        in_specs=[pl.BlockSpec(memory_space=pltpu.SMEM)] + [vmem] * (tiles + 1),
        out_specs=(vmem, vmem),
        scratch_shapes=[pltpu.VMEM((total, width), BF16), pltpu.VMEM((total, width), F32)],
        compiler_params=pltpu.CompilerParams(vmem_limit_bytes=VMEM_LIMIT),
        cost_estimate=pl.CostEstimate(
            flops=2 * total * total * width, bytes_accessed=4_000_000, transcendentals=0
        ),
        name="band_latents",
    )(place, jnp.asarray(band_map(tiles, cols), BF16), *pieces)


def slot_kernel(
    first_slot, lats, outer_bit, tile_count, place, counts, datasets, levels, tile_of, band, scale, shift,
    weight, target, *refs
):
    keep, send, err, turned = refs[-4:]
    slot = first_slot + pl.program_id(0)
    rows = (band[...].astype(F32) * scale[0] + shift[0]).astype(BF16)
    predicted = jnp.dot(rows, weight[0], preferred_element_type=F32)
    total, outs = predicted.shape
    diff = predicted - target[0].astype(F32).reshape(total, outs)
    tile = tile_of[...]
    live = jnp.zeros(tile.shape, F32)
    for t in range(tile_count):
        alive = levels[slot] < counts[datasets[0, t]]
        live = live + jnp.where(jnp.logical_and(tile == t, alive), 1.0, 0.0)
    errors = (diff * live).astype(BF16)
    err[0] = errors
    turned[...] = lax.dot_general(
        errors, rows, (((0,), (0,)), ((), ())), preferred_element_type=F32
    ).astype(BF16)
    piece = turned.shape[1] // lats
    for q in range(lats):
        core, x, y = q & 1, (q >> 1) & 1, (q >> 2) & 1
        outer, inner = (x, y) if outer_bit == 2 else (y, x)
        start = pl.multiple_of(jnp.bitwise_xor(place[0], q) * piece, piece)
        to = send if core else keep
        to[outer, inner, 0] = turned[:, pl.ds(start, piece)]


def slot_chunk(first_slot, count, outer_bit, lats, place, small, tile_of, band, scale, shift, heads, targets, errors):
    total, width = band.shape
    slots, _, outs = heads.shape
    piece = width // lats
    smem = pl.BlockSpec(memory_space=pltpu.SMEM)
    halves = jax.ShapeDtypeStruct((2, 2, count, outs, piece), BF16)
    half_spec = pl.BlockSpec((2, 2, 1, outs, piece), lambda k: (0, 0, k, 0, 0))
    in_specs = [
        smem, smem, smem, smem,
        pl.BlockSpec((total, 1), lambda k: (0, 0)),
        pl.BlockSpec((total, width), lambda k: (0, 0)),
        pl.BlockSpec((1, 1, width), lambda k: (k + first_slot, 0, 0)),
        pl.BlockSpec((1, 1, width), lambda k: (k + first_slot, 0, 0)),
        pl.BlockSpec((1, width, outs), lambda k: (k + first_slot, 0, 0)),
        pl.BlockSpec((1,) + targets.shape[1:], lambda k: (k + first_slot, 0, 0, 0)),
    ]
    args = [place, *small, tile_of, band, scale, shift, heads, targets]
    aliases = {}
    if errors is not None:
        in_specs.append(pl.BlockSpec(memory_space=pl.ANY))
        aliases = {len(args): 2}
        args.append(errors)
    return pl.pallas_call(
        functools.partial(slot_kernel, first_slot, lats, outer_bit, total // (WH * tile_cols(targets, small))),
        grid=(count,),
        out_shape=(halves, halves, jax.ShapeDtypeStruct((slots, total, outs), BF16)),
        in_specs=in_specs,
        out_specs=(
            half_spec,
            half_spec,
            pl.BlockSpec((1, total, outs), lambda k: (k + first_slot, 0, 0)),
        ),
        scratch_shapes=[pltpu.VMEM((outs, width), BF16)],
        input_output_aliases=aliases,
        compiler_params=pltpu.CompilerParams(vmem_limit_bytes=VMEM_LIMIT),
        cost_estimate=pl.CostEstimate(
            flops=count * 8 * total * width * outs, bytes_accessed=count * 2_500_000, transcendentals=0
        ),
        name="slot_errors",
    )(*args)


def tile_cols(targets, small):
    return targets.shape[2] // small[1].shape[1]


def back_kernel(tiles, cols, place, err, weight, scale, out, total):
    slot = pl.program_id(0)
    term = (
        lax.dot_general(err[0], weight[0], (((1,), (1,)), ((), ())), preferred_element_type=F32)
        * scale[0]
    )

    @pl.when(slot == 0)
    def _():
        total[...] = term

    @pl.when(slot > 0)
    def _():
        total[...] += term

    @pl.when(slot == pl.num_programs(0) - 1)
    def _():
        for s in range(tiles):
            tile = lax.rem(place[1] + s, tiles)
            for r in range(WH):
                start = pl.multiple_of(r * tiles * cols + tile * cols, 8)
                out[s, r] = total[pl.ds(start, cols), :].astype(BF16)


def back_terms(place, errors, heads, scale, tiles, cols):
    slots, total, outs = errors.shape
    width = heads.shape[1]
    shape = (tiles, WH, cols, width)
    return pl.pallas_call(
        functools.partial(back_kernel, tiles, cols),
        grid=(slots,),
        out_shape=jax.ShapeDtypeStruct(shape, BF16),
        in_specs=[
            pl.BlockSpec(memory_space=pltpu.SMEM),
            pl.BlockSpec((1, total, outs), lambda k: (k, 0, 0)),
            pl.BlockSpec((1, width, outs), lambda k: (k, 0, 0)),
            pl.BlockSpec((1, 1, width), lambda k: (k, 0, 0)),
        ],
        out_specs=pl.BlockSpec(shape, lambda k: (0, 0, 0, 0)),
        scratch_shapes=[pltpu.VMEM((total, width), F32)],
        compiler_params=pltpu.CompilerParams(vmem_limit_bytes=VMEM_LIMIT),
        cost_estimate=pl.CostEstimate(
            flops=slots * 4 * total * width * outs, bytes_accessed=12_000_000, transcendentals=0
        ),
        name="latent_terms",
    )(place, errors, heads, scale)


def join_kernel(norm, *refs):
    out = refs[-1]
    pairs = refs[:-1]
    slot = 0
    for kept, came in zip(pairs[0::2], pairs[1::2]):
        for k in range(kept.shape[0]):
            total = (kept[k].astype(F32) + came[k].astype(F32)) * norm
            out[slot] = total.T
            slot += 1


def join_heads(pairs, norm):
    flat = [array for pair in pairs for array in pair]
    slots = sum(kept.shape[0] for kept, _ in pairs)
    _, outs, piece = flat[0].shape
    vmem = pl.BlockSpec(memory_space=pltpu.VMEM)
    return pl.pallas_call(
        functools.partial(join_kernel, norm),
        out_shape=jax.ShapeDtypeStruct((slots, piece, outs), F32),
        in_specs=[vmem] * len(flat),
        out_specs=vmem,
        compiler_params=pltpu.CompilerParams(vmem_limit_bytes=VMEM_LIMIT),
        cost_estimate=pl.CostEstimate(flops=1_000_000, bytes_accessed=4_000_000, transcendentals=0),
        name="join_heads",
    )(*flat)


def fast_local(
    patches, norm_gain, input_proj, output_proj, level_scale, level_shift, head_weight, targets,
    level_counts, tile_dataset, slot_level,
):
    rows, cols, width = patches.shape
    lats, tiles = lax.axis_size("lat"), lax.axis_size("var")
    slots, _, outs = head_weight.shape
    lat, var = lax.axis_index("lat"), lax.axis_index("var")
    place = jnp.stack([lat, var]).astype(jnp.int32)
    heads_full = lax.all_gather(head_weight, "lat", axis=1, tiled=True)

    right = [(i, (i + 1) % tiles) for i in range(tiles)]
    up = [(i, i + 1) for i in range(lats - 1)]
    down = [(i + 1, i) for i in range(lats - 1)]
    both = lambda pairs: [(a * tiles + c, b * tiles + d) for a, b in pairs for c, d in right]
    low, high = patches[HR:], patches[:HR]
    above = lax.ppermute(low, "lat", up)
    below = lax.ppermute(high, "lat", down)
    left = lax.ppermute(patches[:, cols - HC :], "var", right)
    above_left = lax.ppermute(low[:, cols - HC :], ("lat", "var"), both(up))
    below_left = lax.ppermute(high[:, cols - HC :], ("lat", "var"), both(down))
    mine = attention(
        place, (patches, left, above, above_left, below, below_left), norm_gain, input_proj, output_proj, lats
    )
    pieces = [mine]
    for s in range(1, tiles):
        pieces.append(lax.ppermute(mine, "var", [(i, (i + s) % tiles) for i in range(tiles)]))
    band, latent = band_latents(place, pieces, cols)

    tile_of = jnp.asarray(np.arange(rows * tiles * cols)[:, None] % (tiles * cols) // cols, jnp.int32)
    scale3, shift3 = level_scale.reshape(slots, 1, width), level_shift.reshape(slots, 1, width)
    small = (level_counts, tile_dataset, slot_level)
    flip = lambda array, bit: lax.ppermute(array, "lat", [(i, i ^ bit) for i in range(lats)])
    add = lambda a, b: (a.astype(F32) + b.astype(F32)).astype(BF16)
    count = 2
    errors, pairs = None, []
    for index in range(slots // count):
        outer_bit = 2 if index % 2 == 0 else 4
        keep, send, errors = slot_chunk(
            index * count, count, outer_bit, lats, place, small, tile_of, band, scale3, shift3,
            heads_full, targets, errors,
        )
        came = flip(send, 1)
        keep, send = add(keep[0], came[0]), add(keep[1], came[1])
        came = flip(send, outer_bit)
        keep, send = add(keep[0], came[0]), add(keep[1], came[1])
        pairs.append((keep, flip(send, 6 - outer_bit)))
    terms = back_terms(place, errors, heads_full, scale3, tiles, cols)
    total = terms[0].astype(F32)
    for s in range(1, tiles):
        came = lax.ppermute(terms[s], "var", [(i, (i + s) % tiles) for i in range(tiles)])
        total = total + came.astype(F32)
    grad_latent = total.astype(BF16)
    grad_head = join_heads(pairs, 1.0 / math.sqrt(lats * rows * tiles * cols))
    return (latent, grad_latent, grad_head)


def padded(array, sides, width, wrap):
    for axis, dim in sides:
        size, length = (lax.axis_size(axis), array.shape[dim])
        up = [(i, (i + 1) % size) for i in range(size if wrap else size - 1)]
        down = [(j, i) for i, j in up]
        last = lax.slice_in_dim(array, length - width, length, axis=dim)
        initial = lax.slice_in_dim(array, 0, width, axis=dim)
        before = lax.ppermute(last, axis, up)
        after = lax.ppermute(initial, axis, down)
        array = jnp.concatenate([before, array, after], axis=dim)
    return array


def layer_norm(values, gain):
    wide = values.astype(jnp.float32)
    average = jnp.mean(wide, axis=-1, keepdims=True)
    centred = wide - average
    variance = jnp.mean(centred * centred, axis=-1, keepdims=True)
    return (centred * lax.rsqrt(variance + EPS) * gain).astype(jnp.bfloat16)


def window_attention(query_ext, keyval, row_valid, heads):
    ext_rows, ext_cols, width = query_ext.shape
    head_size = width // heads
    win_rows = ext_rows // WH
    win_cols = ext_cols // WW

    def split(values, parts):
        shaped = values.reshape(win_rows, WH, win_cols, WW, parts, heads, head_size)
        return shaped.transpose(0, 2, 1, 3, 4, 5, 6).reshape(
            win_rows * win_cols, WH * WW, parts, heads, head_size
        )

    query_win = split(query_ext, 1)[:, :, 0]
    pairs = split(keyval, 2)
    key_win = pairs[:, :, 0]
    value_win = pairs[:, :, 1]
    key_mask = jnp.broadcast_to(
        row_valid.reshape(win_rows, 1, WH, 1), (win_rows, win_cols, WH, WW)
    ).reshape(win_rows * win_cols, WH * WW)
    scores = jnp.einsum(
        "wqhd,wkhd->whqk", query_win, key_win, preferred_element_type=jnp.float32
    ) / math.sqrt(head_size)
    scores = jnp.where(key_mask[:, None, None, :], scores, -jnp.inf)
    peak = jnp.max(scores, axis=-1, keepdims=True)
    weights = jnp.exp(scores - peak)
    probs = (weights / jnp.sum(weights, axis=-1, keepdims=True)).astype(jnp.bfloat16)
    mixed = jnp.einsum("whqk,wkhd->wqhd", probs, value_win, preferred_element_type=jnp.float32)
    return (
        mixed.reshape(win_rows, win_cols, WH, WW, width)
        .transpose(0, 2, 1, 3, 4)
        .reshape(ext_rows, ext_cols, width)
    )


def slot_terms(piece, target_rows, live_cols, level_scale, level_shift, heads_full):
    piece_wide = piece.astype(jnp.float32)
    rows = (
        piece_wide[None] * level_scale[:, None, None, :] + level_shift[:, None, None, :]
    ).astype(jnp.bfloat16)
    predicted = jnp.einsum("krnd,kdo->krno", rows, heads_full, preferred_element_type=jnp.float32)
    errors = ((predicted - target_rows.astype(jnp.float32)) * live_cols[:, None, :, None]).astype(
        jnp.bfloat16
    )
    back_grad = jnp.einsum("krno,kdo->krnd", errors, heads_full, preferred_element_type=jnp.float32)
    piece_grad = jnp.sum(back_grad * level_scale[:, None, None, :], axis=0)
    head_add = jnp.einsum("krnd,krno->dko", rows, errors, preferred_element_type=jnp.float32)
    return (piece_grad, head_add)


def local(
    patches,
    norm_gain,
    input_proj,
    output_proj,
    level_scale,
    level_shift,
    head_weight,
    targets,
    level_counts,
    tile_dataset,
    slot_level,
):
    band_rows, band_cols, width = patches.shape
    half_rows = WH // 2
    half_cols = WW // 2
    lat_count = lax.axis_size("lat")
    var_count = lax.axis_size("var")
    lat_place = lax.axis_index("lat")
    ext_rows = band_rows + WH
    ext_cols = band_cols + WW
    extended = padded(patches, (("lat", 0),), half_rows, False)
    extended = padded(extended, (("var", 1),), half_cols, True)
    normed_ext = layer_norm(extended, norm_gain)
    keyval = jnp.dot(
        normed_ext.reshape(-1, width), input_proj[:, width:], preferred_element_type=jnp.float32
    )
    keyval = keyval.astype(jnp.bfloat16).reshape(ext_rows, ext_cols, 2 * width)
    normed = normed_ext[half_rows : half_rows + band_rows, half_cols : half_cols + band_cols]
    queries = jnp.dot(
        normed.reshape(-1, width), input_proj[:, :width], preferred_element_type=jnp.float32
    )
    queries = queries.astype(jnp.bfloat16).reshape(band_rows, band_cols, width)
    query_ext = jnp.pad(queries, ((half_rows, WH - half_rows), (half_cols, WW - half_cols), (0, 0)))
    global_row = lat_place * band_rows - half_rows + jnp.arange(ext_rows, dtype=jnp.int32)
    row_valid = (global_row >= 0) & (global_row < lat_count * band_rows)
    mixed = window_attention(query_ext, keyval, row_valid, HEADS)
    attn = mixed[half_rows : half_rows + band_rows, half_cols : half_cols + band_cols].astype(
        jnp.bfloat16
    )
    update = jnp.dot(
        attn.reshape(-1, width), output_proj, preferred_element_type=jnp.float32
    ).reshape(band_rows, band_cols, width)
    latent = (patches.astype(jnp.float32) + update).astype(jnp.bfloat16)
    dataset_row = tile_dataset[0]
    dataset_ids = jnp.arange(level_counts.shape[0], dtype=jnp.int32)
    tile_levels = jnp.sum(
        jnp.where(dataset_row[:, None] == dataset_ids[None, :], level_counts[None, :], 0), axis=1
    )
    live_tiles = (slot_level[None, :] < tile_levels[:, None]).astype(jnp.float32)
    heads_full = lax.all_gather(head_weight, "lat", axis=1, tiled=True)
    tile_ids = jnp.arange(var_count, dtype=jnp.int32)
    piece = lax.all_gather(latent, "var", axis=1, tiled=True)
    piece_cols = piece.shape[1]
    column_tile = jnp.arange(piece_cols, dtype=jnp.int32) // band_cols
    onehot = (column_tile[:, None] == tile_ids[None, :]).astype(jnp.float32)
    column_live = jnp.dot(onehot, live_tiles)
    piece_grad, head_add = slot_terms(
        piece, targets, column_live.T, level_scale, level_shift, heads_full
    )
    latent_terms = piece_grad
    latent_terms, head_terms = (latent_terms, head_add)
    grad_latent = lax.psum_scatter(
        latent_terms.astype(jnp.bfloat16), "var", scatter_dimension=1, tiled=True
    )
    head_terms = head_terms * (1.0 / math.sqrt(lat_count * band_rows * var_count * band_cols))
    mine = lax.psum_scatter(
        head_terms.astype(jnp.bfloat16), "lat", scatter_dimension=0, tiled=True
    ).astype(jnp.float32)
    grad_head = jnp.transpose(mine, (1, 0, 2))
    return (latent, grad_latent, grad_head)


def solution(mesh):
    in_specs = (
        P("lat", "var", None),
        P(),
        P(),
        P(),
        P("var", None),
        P("var", None),
        P("var", "lat", None),
        P("var", "lat", None, None),
        P(),
        P("lat", None),
        P("var"),
    )
    fast = mesh.shape["lat"] == 8 and mesh.shape["var"] == 4
    body = fast_local if fast else local
    out_specs = (P("lat", "var", None), P("lat", "var", None), P("var", "lat", None))
    return jax.shard_map(body, mesh=mesh, in_specs=in_specs, out_specs=out_specs, check_vma=False)
```

```python
import functools
import math

import jax
import jax.numpy as jnp
import numpy as np
from jax import lax
from jax.experimental import pallas as pl
from jax.experimental.pallas import tpu as pltpu
from jax.sharding import PartitionSpec as P

HEADS = 16
WH = 6
WW = 12
EPS = 1e-05
HR = WH // 2
HC = WW // 2
QP = 48
LEFT = 8
VMEM_LIMIT = 48 * 1024 * 1024
F32 = jnp.float32
BF16 = jnp.bfloat16


def source_base(cols):
    own = 0
    left = own + WH * cols
    above = left + WH * LEFT
    above_left = above + HR * cols
    below = above_left + HR * LEFT
    below_left = below + HR * cols
    total = below_left + HR * LEFT
    return own, left, above, above_left, below, below_left, total


def gather_maps(cols):
    own, left, above, above_left, below, below_left, total = source_base(cols)
    win_cols = cols // WW
    windows = 2 * win_cols

    def source(part, win_row, row, col):
        if part == 0:
            r = win_row * HR + row
            return left + r * LEFT + col if col < HC else own + r * cols + col - HC
        if win_row == 0:
            return above_left + row * LEFT + col if col < HC else above + row * cols + col - HC
        return below_left + row * LEFT + col if col < HC else below + row * cols + col - HC

    into = np.zeros((windows * 2 * QP, total), np.float32)
    keep = np.zeros((WH * cols, total), np.float32)
    back = np.zeros((WH * cols, windows * QP), np.float32)
    for win in range(windows):
        win_row, win_col = divmod(win, win_cols)
        for part in range(2):
            for row in range(HR):
                for c in range(WW):
                    at = source(part, win_row, row, win_col * WW + c)
                    slot = row * WW + c
                    into[win * 2 * QP + part * QP + slot, at] = 1
                    if part == 0:
                        natural = (win_row * HR + row) * cols + win_col * WW + c
                        keep[natural, at] = 1
                        back[natural, win * QP + slot] = 1
    return into, keep, back


def attention_kernel(
    bands,
    place,
    left,
    above,
    above_left,
    below,
    below_left,
    own_hbm,
    gain,
    maps_hbm,
    in_hbm,
    out_hbm,
    out,
    raw,
    qkv,
    attn,
    own,
    maps,
    proj_in,
    proj_out,
    sems,
):
    moves = [
        pltpu.make_async_copy(src, dst, sems.at[i])
        for i, (src, dst) in enumerate(
            ((own_hbm, own), (maps_hbm, maps), (in_hbm, proj_in), (out_hbm, proj_out))
        )
    ]
    for move in moves:
        move.start()
    cols, width = own.shape[1], own.shape[2]
    bases = source_base(cols)
    total = bases[-1]
    win_cols = cols // WW
    windows = 2 * win_cols
    slots = windows * 2 * QP
    head_size = width // HEADS
    quad = 256 // head_size
    for base, ref in zip(bases, (own, left, above, above_left, below, below_left)):
        count = ref.shape[0]
        if ref is own:
            moves[0].wait()
        if ref.shape[1] == cols:
            raw[base : base + count * cols, :] = ref[...].astype(F32).reshape(count * cols, width)
        else:
            for r in range(count):
                raw[base + r * LEFT : base + (r + 1) * LEFT, :] = jnp.zeros((LEFT, width), F32)
                raw[base + r * LEFT : base + r * LEFT + HC, :] = ref[r].astype(F32)
    wide = raw[...]
    average = jnp.mean(wide, axis=-1, keepdims=True)
    centred = wide - average
    variance = jnp.mean(centred * centred, axis=-1, keepdims=True)
    normed = (centred * lax.rsqrt(variance + EPS) * gain[...]).astype(BF16)
    moves[1].wait()
    win_x = jnp.dot(maps[0:slots, :], normed, preferred_element_type=F32).astype(BF16)
    moves[2].wait()
    step = 512
    for j in range(3 * width // step):
        part = slice(j * step, (j + 1) * step)
        qkv[:, part] = jnp.dot(win_x, proj_in[:, part], preferred_element_type=F32).astype(BF16)
    lane = lax.broadcasted_iota(jnp.int32, (1, 256), 1) // head_size
    heads = [jnp.where(lane == h, 1.0, 0.0) for h in range(quad)]
    key_id = lax.broadcasted_iota(jnp.int32, (1, 2 * QP), 1)
    scale = 1.0 / math.sqrt(head_size)
    for win in range(windows):
        win_row = win // win_cols
        edge = 0 if win_row == 0 else bands - 1
        has_halo = place[0] != edge
        halo_keys = jnp.logical_and(key_id >= QP, key_id < QP + HR * WW)
        valid = jnp.logical_or(key_id < HR * WW, jnp.logical_and(halo_keys, has_halo))
        bias = jnp.where(valid, 0.0, -1e30)
        row0 = win * 2 * QP
        for g in range(width // 256):
            lanes = slice(g * 256, (g + 1) * 256)
            query = qkv[row0 : row0 + QP, lanes].astype(F32) * scale
            stacked = jnp.concatenate([query * h for h in heads], axis=0).astype(BF16)
            key = qkv[row0 : row0 + 2 * QP, width + g * 256 : width + (g + 1) * 256]
            value = qkv[row0 : row0 + 2 * QP, 2 * width + g * 256 : 2 * width + (g + 1) * 256]
            scores = (
                lax.dot_general(
                    stacked, key, (((1,), (1,)), ((), ())), preferred_element_type=F32
                )
                + bias
            )
            weights = jnp.exp(scores - jnp.max(scores, axis=-1, keepdims=True))
            probs = (weights / jnp.sum(weights, axis=-1, keepdims=True)).astype(BF16)
            mixed = jnp.dot(probs, value, preferred_element_type=F32)
            chosen = mixed[0:QP] * heads[0]
            for h in range(1, quad):
                chosen = chosen + mixed[h * QP : (h + 1) * QP] * heads[h]
            attn[win * QP : (win + 1) * QP, lanes] = chosen.astype(BF16)
    size = WH * cols
    keep = maps[slots : slots + size, :]
    back = maps[slots + size : slots + 2 * size, 0 : windows * QP]
    ordered = jnp.dot(back, attn[...], preferred_element_type=F32).astype(BF16)
    residual = jnp.dot(keep, raw[...].astype(BF16), preferred_element_type=F32)
    moves[3].wait()
    update = jnp.dot(ordered, proj_out[...], preferred_element_type=F32)
    out[...] = (residual + update).astype(BF16)


def attention(place, patches, pieces, gain, proj_in, proj_out, bands):
    rows, cols, width = patches.shape
    into, keep, back = gather_maps(cols)
    total = source_base(cols)[-1]
    windows = 2 * (cols // WW)
    back = np.pad(back, ((0, 0), (0, total - back.shape[1])))
    maps = np.concatenate([into, keep, back])
    vmem = pl.BlockSpec(memory_space=pltpu.VMEM)
    hbm = pl.BlockSpec(memory_space=pltpu.HBM)
    return pl.pallas_call(
        functools.partial(attention_kernel, bands),
        out_shape=jax.ShapeDtypeStruct((rows * cols, width), BF16),
        in_specs=[pl.BlockSpec(memory_space=pltpu.SMEM)] + [vmem] * 5 + [hbm, vmem, hbm, hbm, hbm],
        out_specs=vmem,
        scratch_shapes=[
            pltpu.VMEM((total, width), F32),
            pltpu.VMEM((windows * 2 * QP, 3 * width), BF16),
            pltpu.VMEM((windows * QP, width), BF16),
            pltpu.VMEM(patches.shape, BF16),
            pltpu.VMEM(maps.shape, BF16),
            pltpu.VMEM(proj_in.shape, BF16),
            pltpu.VMEM(proj_out.shape, BF16),
            pltpu.SemaphoreType.DMA((4,)),
        ],
        compiler_params=pltpu.CompilerParams(vmem_limit_bytes=VMEM_LIMIT),
        cost_estimate=pl.CostEstimate(
            flops=6_000_000_000, bytes_accessed=12_000_000, transcendentals=400_000
        ),
        name="window_attention",
    )(
        place,
        *pieces,
        patches,
        gain.reshape(1, width),
        jnp.asarray(maps, BF16),
        proj_in,
        proj_out,
    )


def band_map(tiles, cols):
    wide = tiles * cols
    chosen = np.zeros((WH * wide, WH * wide), np.float32)
    for r in range(WH):
        for c in range(wide):
            tile, at = divmod((c + HC) % wide, cols)
            chosen[r * wide + c, tile * WH * cols + r * cols + at] = 1
    return chosen


def band_kernel(tiles, cols, place, chosen, *refs):
    pieces, (band, latent, laid, wide) = refs[:tiles], refs[tiles:]
    size = WH * cols
    var = place[1]
    for s in range(tiles):
        tile = lax.rem(var + tiles - s, tiles)
        laid[pl.ds(pl.multiple_of(tile * size, 16), size), :] = pieces[s][...]
    wide[...] = jnp.dot(chosen[...], laid[...], preferred_element_type=F32)
    band[...] = wide[...].astype(BF16)
    for r in range(WH):
        start = pl.multiple_of(r * tiles * cols + var * cols, 8)
        latent[r] = wide[pl.ds(start, cols), :].astype(BF16)


def band_latents(place, pieces, cols):
    tiles = len(pieces)
    width = pieces[0].shape[1]
    total = WH * tiles * cols
    vmem = pl.BlockSpec(memory_space=pltpu.VMEM)
    return pl.pallas_call(
        functools.partial(band_kernel, tiles, cols),
        out_shape=(
            jax.ShapeDtypeStruct((total, width), BF16),
            jax.ShapeDtypeStruct((WH, cols, width), BF16),
        ),
        in_specs=[pl.BlockSpec(memory_space=pltpu.SMEM)] + [vmem] * (tiles + 1),
        out_specs=(vmem, vmem),
        scratch_shapes=[pltpu.VMEM((total, width), BF16), pltpu.VMEM((total, width), F32)],
        compiler_params=pltpu.CompilerParams(vmem_limit_bytes=VMEM_LIMIT),
        cost_estimate=pl.CostEstimate(
            flops=2 * total * total * width, bytes_accessed=4_000_000, transcendentals=0
        ),
        name="band_latents",
    )(place, jnp.asarray(band_map(tiles, cols), BF16), *pieces)


LANES = 384


def scale_kernel(gathered, scale, shift, scaled, bias):
    lats, _, outs, piece = gathered.shape
    weight = jnp.concatenate([gathered[l, 0] for l in range(lats)], axis=1)
    scaled[0, 0:outs, :] = (weight.astype(F32) * scale[0]).astype(BF16)
    scaled[0, outs:, :] = jnp.zeros((scaled.shape[1] - outs, lats * piece), BF16)
    rest = jnp.broadcast_to(shift[0], (8, lats * piece))
    row = lax.broadcasted_iota(jnp.int32, rest.shape, 0)
    split = jnp.zeros(rest.shape, F32)
    for i in range(3):
        part = rest.astype(BF16).astype(F32)
        split = jnp.where(row == i, part, split)
        rest = rest - part
    terms = lax.dot_general(
        split.astype(BF16), weight, (((1,), (1,)), ((), ())), preferred_element_type=F32
    )
    bias[0] = jnp.sum(terms, axis=0, keepdims=True)


def scaled_heads(gathered, scale, shift):
    lats, slots, outs, piece = gathered.shape
    width = lats * piece
    return pl.pallas_call(
        scale_kernel,
        grid=(slots,),
        out_shape=(
            jax.ShapeDtypeStruct((slots, LANES, width), BF16),
            jax.ShapeDtypeStruct((slots, 1, outs), F32),
        ),
        in_specs=[
            pl.BlockSpec((lats, 1, outs, piece), lambda k: (0, k, 0, 0)),
            pl.BlockSpec((1, 1, width), lambda k: (k, 0, 0)),
            pl.BlockSpec((1, 1, width), lambda k: (k, 0, 0)),
        ],
        out_specs=(
            pl.BlockSpec((1, LANES, width), lambda k: (k, 0, 0)),
            pl.BlockSpec((1, 1, outs), lambda k: (k, 0, 0)),
        ),
        compiler_params=pltpu.CompilerParams(vmem_limit_bytes=VMEM_LIMIT),
        cost_estimate=pl.CostEstimate(
            flops=100_000_000, bytes_accessed=16_000_000, transcendentals=0
        ),
        name="scaled_heads",
    )(gathered, scale, shift)


def slot_kernel(
    first_slot, lats, outer_bit, tiles, place, counts, datasets, levels, tile_of, band, scale, shift,
    bias, weight, target, *refs
):
    keep, send, err, turned = refs[-4:]
    count, outs = target.shape[0], target.shape[-1]
    total, width = band.shape
    piece = width // lats
    latent = band[...]
    predicted = lax.dot_general(
        latent, weight[...].reshape(count * LANES, width), (((1,), (1,)), ((), ())),
        preferred_element_type=F32,
    )
    tile = tile_of[...]
    for k in range(count):
        live = jnp.zeros(tile.shape, F32)
        for t in range(tiles):
            alive = levels[first_slot + k] < counts[datasets[0, t]]
            live = live + jnp.where(jnp.logical_and(tile == t, alive), 1.0, 0.0)
        mine = predicted[:, k * LANES : k * LANES + outs]
        diff = mine + bias[k] - target[k].astype(F32).reshape(total, outs)
        err[:, k * LANES : k * LANES + outs] = (diff * live).astype(BF16)
        err[:, k * LANES + outs : (k + 1) * LANES] = jnp.zeros((total, LANES - outs), BF16)
        errors = err[:, k * LANES : (k + 1) * LANES]
        sums = jnp.sum(errors.astype(F32), axis=0, keepdims=True)
        column = jnp.transpose(jnp.broadcast_to(sums, (128, LANES)))[0:outs]
        grad = lax.dot_general(
            errors, latent, (((0,), (0,)), ((), ())), preferred_element_type=F32
        )[0:outs]
        for j in range(lats):
            lanes = slice(j * piece, (j + 1) * piece)
            turned[:, lanes] = (
                grad[:, lanes] * scale[k][:, lanes] + column[:, 0:piece] * shift[k][:, lanes]
            ).astype(BF16)
        for q in range(lats):
            core, x, y = q & 1, (q >> 1) & 1, (q >> 2) & 1
            outer, inner = (x, y) if outer_bit == 2 else (y, x)
            start = pl.multiple_of(jnp.bitwise_xor(place[0], q) * piece, piece)
            to = send if core else keep
            to[outer, inner, k] = turned[:, pl.ds(start, piece)]


def slot_chunk(index, count, outer_bit, lats, place, small, tile_of, band, scale, shift, bias, heads, targets, errors, after):
    total, width = band.shape
    slots, _, _, outs = targets.shape
    tiles = small[1].shape[1]
    piece = width // lats
    smem = pl.BlockSpec(memory_space=pltpu.SMEM)
    halves = jax.ShapeDtypeStruct((2, 2, count, outs, piece), BF16)
    half_spec = pl.BlockSpec(halves.shape, lambda i: (0, 0, 0, 0, 0))
    in_specs = [
        smem, smem, smem, smem,
        pl.BlockSpec((total, 1), lambda i: (0, 0)),
        pl.BlockSpec((total, width), lambda i: (0, 0)),
        pl.BlockSpec((count, 1, width), lambda i: (index, 0, 0)),
        pl.BlockSpec((count, 1, width), lambda i: (index, 0, 0)),
        pl.BlockSpec((count, 1, outs), lambda i: (index, 0, 0)),
        pl.BlockSpec((count, LANES, width), lambda i: (index, 0, 0)),
        pl.BlockSpec((count,) + targets.shape[1:], lambda i: (index, 0, 0, 0)),
    ]
    args = [place, *small, tile_of, band, scale, shift, bias, heads, targets]
    aliases = {}
    if errors is not None:
        aliases = {len(args): 2}
        args.append(errors)
    args.extend(after)
    in_specs.extend([pl.BlockSpec(memory_space=pl.ANY)] * (len(args) - len(in_specs)))
    return pl.pallas_call(
        functools.partial(slot_kernel, index * count, lats, outer_bit, tiles),
        grid=(1,),
        out_shape=(halves, halves, jax.ShapeDtypeStruct((total, slots * LANES), BF16)),
        in_specs=in_specs,
        out_specs=(
            half_spec,
            half_spec,
            pl.BlockSpec((total, count * LANES), lambda i: (0, index)),
        ),
        scratch_shapes=[pltpu.VMEM((outs, width), BF16)],
        input_output_aliases=aliases,
        compiler_params=pltpu.CompilerParams(vmem_limit_bytes=VMEM_LIMIT),
        cost_estimate=pl.CostEstimate(
            flops=count * 8 * total * width * outs, bytes_accessed=count * 2_500_000, transcendentals=0
        ),
        name="slot_errors",
    )(*args)


def back_kernel(tiles, cols, place, err, weight, *refs):
    out, total = refs[-2:]
    step = pl.program_id(0)
    width = weight.shape[-1]
    term = jnp.dot(err[...], weight[...].reshape(-1, width), preferred_element_type=F32)

    @pl.when(step == 0)
    def _():
        total[...] = term

    @pl.when(step > 0)
    def _():
        total[...] += term

    @pl.when(step == pl.num_programs(0) - 1)
    def _():
        for s in range(tiles):
            tile = lax.rem(place[1] + s, tiles)
            for r in range(WH):
                start = pl.multiple_of(r * tiles * cols + tile * cols, 8)
                out[s, r] = total[pl.ds(start, cols), :].astype(BF16)


def back_terms(place, errors, heads, count, tiles, cols, after):
    total = errors.shape[0]
    slots, _, width = heads.shape
    shape = (tiles, WH, cols, width)
    return pl.pallas_call(
        functools.partial(back_kernel, tiles, cols),
        grid=(slots // count,),
        out_shape=jax.ShapeDtypeStruct(shape, BF16),
        in_specs=[
            pl.BlockSpec(memory_space=pltpu.SMEM),
            pl.BlockSpec((total, count * LANES), lambda i: (0, i)),
            pl.BlockSpec((count, LANES, width), lambda i: (i, 0, 0)),
        ]
        + [pl.BlockSpec(memory_space=pl.ANY)] * len(after),
        out_specs=pl.BlockSpec(shape, lambda i: (0, 0, 0, 0)),
        scratch_shapes=[pltpu.VMEM((total, width), F32)],
        compiler_params=pltpu.CompilerParams(vmem_limit_bytes=VMEM_LIMIT),
        cost_estimate=pl.CostEstimate(
            flops=slots * 2 * total * width * LANES, bytes_accessed=12_000_000, transcendentals=0
        ),
        name="latent_terms",
    )(place, errors, heads, *after)


def join_kernel(norm, *refs):
    out = refs[-1]
    pairs = refs[:-1]
    slot = 0
    for kept, came in zip(pairs[0::2], pairs[1::2]):
        for k in range(kept.shape[0]):
            out[slot] = (kept[k].astype(F32) + came[k].astype(F32)) * norm
            slot += 1


def join_heads(pairs, norm):
    flat = [array for pair in pairs for array in pair]
    slots = sum(kept.shape[0] for kept, _ in pairs)
    _, outs, piece = flat[0].shape
    vmem = pl.BlockSpec(memory_space=pltpu.VMEM)
    return pl.pallas_call(
        functools.partial(join_kernel, norm),
        out_shape=jax.ShapeDtypeStruct((slots, outs, piece), F32),
        in_specs=[vmem] * len(flat),
        out_specs=vmem,
        compiler_params=pltpu.CompilerParams(vmem_limit_bytes=VMEM_LIMIT),
        cost_estimate=pl.CostEstimate(flops=1_000_000, bytes_accessed=4_000_000, transcendentals=0),
        name="join_heads",
    )(*flat)


def fast_local(
    patches, norm_gain, input_proj, output_proj, level_scale, level_shift, head_weight, targets,
    level_counts, tile_dataset, slot_level,
):
    rows, cols, width = patches.shape
    lats, tiles = lax.axis_size("lat"), lax.axis_size("var")
    slots = head_weight.shape[0]
    lat, var = lax.axis_index("lat"), lax.axis_index("var")
    place = jnp.stack([lat, var]).astype(jnp.int32)
    gathered = lax.all_gather(jnp.transpose(head_weight, (0, 2, 1)), "lat", axis=0, tiled=False)

    right = [(i, (i + 1) % tiles) for i in range(tiles)]
    up = [(i, i + 1) for i in range(lats - 1)]
    down = [(i + 1, i) for i in range(lats - 1)]
    both = lambda pairs: [(a * tiles + c, b * tiles + d) for a, b in pairs for c, d in right]
    low, high = patches[HR:], patches[:HR]
    above = lax.ppermute(low, "lat", up)
    below = lax.ppermute(high, "lat", down)
    left = lax.ppermute(patches[:, cols - HC :], "var", right)
    above_left = lax.ppermute(low[:, cols - HC :], ("lat", "var"), both(up))
    below_left = lax.ppermute(high[:, cols - HC :], ("lat", "var"), both(down))
    mine = attention(
        place, patches, (left, above, above_left, below, below_left), norm_gain, input_proj, output_proj, lats
    )
    pieces = [mine]
    for s in range(1, tiles):
        pieces.append(lax.ppermute(mine, "var", [(i, (i + s) % tiles) for i in range(tiles)]))
    band, latent = band_latents(place, pieces, cols)

    tile_of = jnp.asarray(np.arange(rows * tiles * cols)[:, None] % (tiles * cols) // cols, jnp.int32)
    scale3, shift3 = level_scale.reshape(slots, 1, width), level_shift.reshape(slots, 1, width)
    small = (level_counts, tile_dataset, slot_level)
    heads_full, bias = scaled_heads(gathered, scale3, shift3)
    flip = lambda array, bit: lax.ppermute(array, "lat", [(i, i ^ bit) for i in range(lats)])
    add = lambda a, b: (a.astype(F32) + b.astype(F32)).astype(BF16)
    count = 2
    chunks = slots // count
    kept, sent, errors = {}, {}, None

    def advance(index, stage):
        if index < 0 or index >= chunks:
            return []
        outer = 2 if index % 2 == 0 else 4
        came = flip(sent[index], (1, outer)[stage])
        kept[index], sent[index] = add(kept[index][0], came[0]), add(kept[index][1], came[1])
        return [sent[index]]

    for index in range(chunks):
        after = advance(index - 3, 1) + advance(index - 2, 0)
        kept[index], sent[index], errors = slot_chunk(
            index, count, 2 if index % 2 == 0 else 4, lats, place, small, tile_of, band, scale3, shift3,
            bias, heads_full, targets, errors, after,
        )
    after = advance(chunks - 3, 1) + advance(chunks - 2, 0)
    terms = back_terms(place, errors, heads_full, count, tiles, cols, after)
    advance(chunks - 1, 0)
    advance(chunks - 2, 1)
    advance(chunks - 1, 1)
    pairs = [
        (kept[i], flip(sent[i], 4 if i % 2 == 0 else 2)) for i in range(chunks)
    ]
    total = terms[0].astype(F32)
    for s in range(1, tiles):
        came = lax.ppermute(terms[s], "var", [(i, (i + s) % tiles) for i in range(tiles)])
        total = total + came.astype(F32)
    grad_latent = total.astype(BF16)
    grad_head = join_heads(pairs, 1.0 / math.sqrt(lats * rows * tiles * cols))
    return (latent, grad_latent, jnp.transpose(grad_head, (0, 2, 1)))


def padded(array, sides, width, wrap):
    for axis, dim in sides:
        size, length = (lax.axis_size(axis), array.shape[dim])
        up = [(i, (i + 1) % size) for i in range(size if wrap else size - 1)]
        down = [(j, i) for i, j in up]
        last = lax.slice_in_dim(array, length - width, length, axis=dim)
        initial = lax.slice_in_dim(array, 0, width, axis=dim)
        before = lax.ppermute(last, axis, up)
        after = lax.ppermute(initial, axis, down)
        array = jnp.concatenate([before, array, after], axis=dim)
    return array


def layer_norm(values, gain):
    wide = values.astype(jnp.float32)
    average = jnp.mean(wide, axis=-1, keepdims=True)
    centred = wide - average
    variance = jnp.mean(centred * centred, axis=-1, keepdims=True)
    return (centred * lax.rsqrt(variance + EPS) * gain).astype(jnp.bfloat16)


def window_attention(query_ext, keyval, row_valid, heads):
    ext_rows, ext_cols, width = query_ext.shape
    head_size = width // heads
    win_rows = ext_rows // WH
    win_cols = ext_cols // WW

    def split(values, parts):
        shaped = values.reshape(win_rows, WH, win_cols, WW, parts, heads, head_size)
        return shaped.transpose(0, 2, 1, 3, 4, 5, 6).reshape(
            win_rows * win_cols, WH * WW, parts, heads, head_size
        )

    query_win = split(query_ext, 1)[:, :, 0]
    pairs = split(keyval, 2)
    key_win = pairs[:, :, 0]
    value_win = pairs[:, :, 1]
    key_mask = jnp.broadcast_to(
        row_valid.reshape(win_rows, 1, WH, 1), (win_rows, win_cols, WH, WW)
    ).reshape(win_rows * win_cols, WH * WW)
    scores = jnp.einsum(
        "wqhd,wkhd->whqk", query_win, key_win, preferred_element_type=jnp.float32
    ) / math.sqrt(head_size)
    scores = jnp.where(key_mask[:, None, None, :], scores, -jnp.inf)
    peak = jnp.max(scores, axis=-1, keepdims=True)
    weights = jnp.exp(scores - peak)
    probs = (weights / jnp.sum(weights, axis=-1, keepdims=True)).astype(jnp.bfloat16)
    mixed = jnp.einsum("whqk,wkhd->wqhd", probs, value_win, preferred_element_type=jnp.float32)
    return (
        mixed.reshape(win_rows, win_cols, WH, WW, width)
        .transpose(0, 2, 1, 3, 4)
        .reshape(ext_rows, ext_cols, width)
    )


def slot_terms(piece, target_rows, live_cols, level_scale, level_shift, heads_full):
    piece_wide = piece.astype(jnp.float32)
    rows = (
        piece_wide[None] * level_scale[:, None, None, :] + level_shift[:, None, None, :]
    ).astype(jnp.bfloat16)
    predicted = jnp.einsum("krnd,kdo->krno", rows, heads_full, preferred_element_type=jnp.float32)
    errors = ((predicted - target_rows.astype(jnp.float32)) * live_cols[:, None, :, None]).astype(
        jnp.bfloat16
    )
    back_grad = jnp.einsum("krno,kdo->krnd", errors, heads_full, preferred_element_type=jnp.float32)
    piece_grad = jnp.sum(back_grad * level_scale[:, None, None, :], axis=0)
    head_add = jnp.einsum("krnd,krno->dko", rows, errors, preferred_element_type=jnp.float32)
    return (piece_grad, head_add)


def local(
    patches,
    norm_gain,
    input_proj,
    output_proj,
    level_scale,
    level_shift,
    head_weight,
    targets,
    level_counts,
    tile_dataset,
    slot_level,
):
    band_rows, band_cols, width = patches.shape
    half_rows = WH // 2
    half_cols = WW // 2
    lat_count = lax.axis_size("lat")
    var_count = lax.axis_size("var")
    lat_place = lax.axis_index("lat")
    ext_rows = band_rows + WH
    ext_cols = band_cols + WW
    extended = padded(patches, (("lat", 0),), half_rows, False)
    extended = padded(extended, (("var", 1),), half_cols, True)
    normed_ext = layer_norm(extended, norm_gain)
    keyval = jnp.dot(
        normed_ext.reshape(-1, width), input_proj[:, width:], preferred_element_type=jnp.float32
    )
    keyval = keyval.astype(jnp.bfloat16).reshape(ext_rows, ext_cols, 2 * width)
    normed = normed_ext[half_rows : half_rows + band_rows, half_cols : half_cols + band_cols]
    queries = jnp.dot(
        normed.reshape(-1, width), input_proj[:, :width], preferred_element_type=jnp.float32
    )
    queries = queries.astype(jnp.bfloat16).reshape(band_rows, band_cols, width)
    query_ext = jnp.pad(queries, ((half_rows, WH - half_rows), (half_cols, WW - half_cols), (0, 0)))
    global_row = lat_place * band_rows - half_rows + jnp.arange(ext_rows, dtype=jnp.int32)
    row_valid = (global_row >= 0) & (global_row < lat_count * band_rows)
    mixed = window_attention(query_ext, keyval, row_valid, HEADS)
    attn = mixed[half_rows : half_rows + band_rows, half_cols : half_cols + band_cols].astype(
        jnp.bfloat16
    )
    update = jnp.dot(
        attn.reshape(-1, width), output_proj, preferred_element_type=jnp.float32
    ).reshape(band_rows, band_cols, width)
    latent = (patches.astype(jnp.float32) + update).astype(jnp.bfloat16)
    dataset_row = tile_dataset[0]
    dataset_ids = jnp.arange(level_counts.shape[0], dtype=jnp.int32)
    tile_levels = jnp.sum(
        jnp.where(dataset_row[:, None] == dataset_ids[None, :], level_counts[None, :], 0), axis=1
    )
    live_tiles = (slot_level[None, :] < tile_levels[:, None]).astype(jnp.float32)
    heads_full = lax.all_gather(head_weight, "lat", axis=1, tiled=True)
    tile_ids = jnp.arange(var_count, dtype=jnp.int32)
    piece = lax.all_gather(latent, "var", axis=1, tiled=True)
    piece_cols = piece.shape[1]
    column_tile = jnp.arange(piece_cols, dtype=jnp.int32) // band_cols
    onehot = (column_tile[:, None] == tile_ids[None, :]).astype(jnp.float32)
    column_live = jnp.dot(onehot, live_tiles)
    piece_grad, head_add = slot_terms(
        piece, targets, column_live.T, level_scale, level_shift, heads_full
    )
    latent_terms = piece_grad
    latent_terms, head_terms = (latent_terms, head_add)
    grad_latent = lax.psum_scatter(
        latent_terms.astype(jnp.bfloat16), "var", scatter_dimension=1, tiled=True
    )
    head_terms = head_terms * (1.0 / math.sqrt(lat_count * band_rows * var_count * band_cols))
    mine = lax.psum_scatter(
        head_terms.astype(jnp.bfloat16), "lat", scatter_dimension=0, tiled=True
    ).astype(jnp.float32)
    grad_head = jnp.transpose(mine, (1, 0, 2))
    return (latent, grad_latent, grad_head)


def solution(mesh):
    in_specs = (
        P("lat", "var", None),
        P(),
        P(),
        P(),
        P("var", None),
        P("var", None),
        P("var", "lat", None),
        P("var", "lat", None, None),
        P(),
        P("lat", None),
        P("var"),
    )
    fast = mesh.shape["lat"] == 8 and mesh.shape["var"] == 4
    body = fast_local if fast else local
    out_specs = (P("lat", "var", None), P("lat", "var", None), P("var", "lat", None))
    return jax.shard_map(body, mesh=mesh, in_specs=in_specs, out_specs=out_specs, check_vma=False)
```

```python
import functools
import math

import jax
import jax.numpy as jnp
import numpy as np
from jax import lax
from jax.experimental import pallas as pl
from jax.experimental.pallas import tpu as pltpu
from jax.sharding import PartitionSpec as P

HEADS = 16
WH = 6
WW = 12
EPS = 1e-05
HR = WH // 2
HC = WW // 2
QP = 48
LEFT = 8
VMEM_LIMIT = 48 * 1024 * 1024
F32 = jnp.float32
BF16 = jnp.bfloat16


def source_base(cols):
    own = 0
    left = own + WH * cols
    above = left + WH * LEFT
    above_left = above + HR * cols
    below = above_left + HR * LEFT
    below_left = below + HR * cols
    total = below_left + HR * LEFT
    return own, left, above, above_left, below, below_left, total


def gather_maps(cols):
    own, left, above, above_left, below, below_left, total = source_base(cols)
    win_cols = cols // WW
    windows = 2 * win_cols

    def source(part, win_row, row, col):
        if part == 0:
            r = win_row * HR + row
            return left + r * LEFT + col if col < HC else own + r * cols + col - HC
        if win_row == 0:
            return above_left + row * LEFT + col if col < HC else above + row * cols + col - HC
        return below_left + row * LEFT + col if col < HC else below + row * cols + col - HC

    into = np.zeros((windows * 2 * QP, total), np.float32)
    keep = np.zeros((WH * cols, total), np.float32)
    back = np.zeros((WH * cols, windows * QP), np.float32)
    for win in range(windows):
        win_row, win_col = divmod(win, win_cols)
        for part in range(2):
            for row in range(HR):
                for c in range(WW):
                    at = source(part, win_row, row, win_col * WW + c)
                    slot = row * WW + c
                    into[win * 2 * QP + part * QP + slot, at] = 1
                    if part == 0:
                        natural = (win_row * HR + row) * cols + win_col * WW + c
                        keep[natural, at] = 1
                        back[natural, win * QP + slot] = 1
    return into, keep, back


def attention_kernel(
    bands,
    place,
    left,
    above,
    above_left,
    below,
    below_left,
    own_hbm,
    gain,
    maps_hbm,
    in_hbm,
    out_hbm,
    out,
    raw,
    qkv,
    attn,
    own,
    maps,
    proj_in,
    proj_out,
    sems,
):
    moves = [
        pltpu.make_async_copy(src, dst, sems.at[i])
        for i, (src, dst) in enumerate(
            ((own_hbm, own), (maps_hbm, maps), (in_hbm, proj_in), (out_hbm, proj_out))
        )
    ]
    for move in moves:
        move.start()
    cols, width = own.shape[1], own.shape[2]
    bases = source_base(cols)
    total = bases[-1]
    win_cols = cols // WW
    windows = 2 * win_cols
    slots = windows * 2 * QP
    head_size = width // HEADS
    quad = 256 // head_size
    for base, ref in zip(bases, (own, left, above, above_left, below, below_left)):
        count = ref.shape[0]
        if ref is own:
            moves[0].wait()
        if ref.shape[1] == cols:
            raw[base : base + count * cols, :] = ref[...].astype(F32).reshape(count * cols, width)
        else:
            for r in range(count):
                raw[base + r * LEFT : base + (r + 1) * LEFT, :] = jnp.zeros((LEFT, width), F32)
                raw[base + r * LEFT : base + r * LEFT + HC, :] = ref[r].astype(F32)
    wide = raw[...]
    average = jnp.mean(wide, axis=-1, keepdims=True)
    centred = wide - average
    variance = jnp.mean(centred * centred, axis=-1, keepdims=True)
    normed = (centred * lax.rsqrt(variance + EPS) * gain[...]).astype(BF16)
    moves[1].wait()
    win_x = jnp.dot(maps[0:slots, :], normed, preferred_element_type=F32).astype(BF16)
    moves[2].wait()
    step = 512
    for j in range(3 * width // step):
        part = slice(j * step, (j + 1) * step)
        qkv[:, part] = jnp.dot(win_x, proj_in[:, part], preferred_element_type=F32).astype(BF16)
    lane = lax.broadcasted_iota(jnp.int32, (1, 256), 1) // head_size
    heads = [jnp.where(lane == h, 1.0, 0.0) for h in range(quad)]
    key_id = lax.broadcasted_iota(jnp.int32, (1, 2 * QP), 1)
    scale = 1.0 / math.sqrt(head_size)
    for win in range(windows):
        win_row = win // win_cols
        edge = 0 if win_row == 0 else bands - 1
        has_halo = place[0] != edge
        halo_keys = jnp.logical_and(key_id >= QP, key_id < QP + HR * WW)
        valid = jnp.logical_or(key_id < HR * WW, jnp.logical_and(halo_keys, has_halo))
        bias = jnp.where(valid, 0.0, -1e30)
        row0 = win * 2 * QP
        for g in range(width // 256):
            lanes = slice(g * 256, (g + 1) * 256)
            query = qkv[row0 : row0 + QP, lanes].astype(F32) * scale
            stacked = jnp.concatenate([query * h for h in heads], axis=0).astype(BF16)
            key = qkv[row0 : row0 + 2 * QP, width + g * 256 : width + (g + 1) * 256]
            value = qkv[row0 : row0 + 2 * QP, 2 * width + g * 256 : 2 * width + (g + 1) * 256]
            scores = (
                lax.dot_general(
                    stacked, key, (((1,), (1,)), ((), ())), preferred_element_type=F32
                )
                + bias
            )
            weights = jnp.exp(scores - jnp.max(scores, axis=-1, keepdims=True))
            probs = (weights / jnp.sum(weights, axis=-1, keepdims=True)).astype(BF16)
            mixed = jnp.dot(probs, value, preferred_element_type=F32)
            chosen = mixed[0:QP] * heads[0]
            for h in range(1, quad):
                chosen = chosen + mixed[h * QP : (h + 1) * QP] * heads[h]
            attn[win * QP : (win + 1) * QP, lanes] = chosen.astype(BF16)
    size = WH * cols
    keep = maps[slots : slots + size, :]
    back = maps[slots + size : slots + 2 * size, 0 : windows * QP]
    ordered = jnp.dot(back, attn[...], preferred_element_type=F32).astype(BF16)
    residual = jnp.dot(keep, raw[...].astype(BF16), preferred_element_type=F32)
    moves[3].wait()
    update = jnp.dot(ordered, proj_out[...], preferred_element_type=F32)
    out[...] = (residual + update).astype(BF16)


def attention(place, patches, pieces, gain, proj_in, proj_out, bands):
    rows, cols, width = patches.shape
    into, keep, back = gather_maps(cols)
    total = source_base(cols)[-1]
    windows = 2 * (cols // WW)
    back = np.pad(back, ((0, 0), (0, total - back.shape[1])))
    maps = np.concatenate([into, keep, back])
    vmem = pl.BlockSpec(memory_space=pltpu.VMEM)
    hbm = pl.BlockSpec(memory_space=pltpu.HBM)
    return pl.pallas_call(
        functools.partial(attention_kernel, bands),
        out_shape=jax.ShapeDtypeStruct((rows * cols, width), BF16),
        in_specs=[pl.BlockSpec(memory_space=pltpu.SMEM)] + [vmem] * 5 + [hbm, vmem, hbm, hbm, hbm],
        out_specs=vmem,
        scratch_shapes=[
            pltpu.VMEM((total, width), F32),
            pltpu.VMEM((windows * 2 * QP, 3 * width), BF16),
            pltpu.VMEM((windows * QP, width), BF16),
            pltpu.VMEM(patches.shape, BF16),
            pltpu.VMEM(maps.shape, BF16),
            pltpu.VMEM(proj_in.shape, BF16),
            pltpu.VMEM(proj_out.shape, BF16),
            pltpu.SemaphoreType.DMA((4,)),
        ],
        compiler_params=pltpu.CompilerParams(vmem_limit_bytes=VMEM_LIMIT),
        cost_estimate=pl.CostEstimate(
            flops=6_000_000_000, bytes_accessed=12_000_000, transcendentals=400_000
        ),
        name="window_attention",
    )(
        place,
        *pieces,
        patches,
        gain.reshape(1, width),
        jnp.asarray(maps, BF16),
        proj_in,
        proj_out,
    )


def band_map(tiles, cols):
    wide = tiles * cols
    chosen = np.zeros((WH * wide, WH * wide), np.float32)
    for r in range(WH):
        for c in range(wide):
            tile, at = divmod((c + HC) % wide, cols)
            chosen[r * wide + c, tile * WH * cols + r * cols + at] = 1
    return chosen


def band_kernel(tiles, cols, place, chosen, *refs):
    pieces, (band, latent, laid, wide) = refs[:tiles], refs[tiles:]
    size = WH * cols
    var = place[1]
    for s in range(tiles):
        tile = lax.rem(var + tiles - s, tiles)
        laid[pl.ds(pl.multiple_of(tile * size, 16), size), :] = pieces[s][...]
    wide[...] = jnp.dot(chosen[...], laid[...], preferred_element_type=F32)
    band[...] = wide[...].astype(BF16)
    for r in range(WH):
        start = pl.multiple_of(r * tiles * cols + var * cols, 8)
        latent[r] = wide[pl.ds(start, cols), :].astype(BF16)


def band_latents(place, pieces, cols):
    tiles = len(pieces)
    width = pieces[0].shape[1]
    total = WH * tiles * cols
    vmem = pl.BlockSpec(memory_space=pltpu.VMEM)
    return pl.pallas_call(
        functools.partial(band_kernel, tiles, cols),
        out_shape=(
            jax.ShapeDtypeStruct((total, width), BF16),
            jax.ShapeDtypeStruct((WH, cols, width), BF16),
        ),
        in_specs=[pl.BlockSpec(memory_space=pltpu.SMEM)] + [vmem] * (tiles + 1),
        out_specs=(vmem, vmem),
        scratch_shapes=[pltpu.VMEM((total, width), BF16), pltpu.VMEM((total, width), F32)],
        compiler_params=pltpu.CompilerParams(vmem_limit_bytes=VMEM_LIMIT),
        cost_estimate=pl.CostEstimate(
            flops=2 * total * total * width, bytes_accessed=4_000_000, transcendentals=0
        ),
        name="band_latents",
    )(place, jnp.asarray(band_map(tiles, cols), BF16), *pieces)


def slot_kernel(first_slot, lats, tiles, final, place, counts, datasets, levels, tile_of, band, scale, shift, gathered, target, *refs):
    keep, send, out = refs[-8:-5] if final else refs[-7:-4]
    rows, errs, turned = refs[-4:-2], refs[-2], refs[-1]
    total = refs[-5] if final else out
    step = pl.program_id(0)
    outs = target.shape[-1]
    places, width = band.shape
    piece = width // lats

    @pl.when(step == 0)
    def _():
        total[...] = refs[0][...] if final else jnp.zeros_like(total)

    tile = tile_of[...]
    for k in range(2):
        rows[k][...] = (band[...].astype(F32) * scale[k] + shift[k]).astype(BF16)
    for k in range(2):
        weight = jnp.concatenate([gathered[l, k] for l in range(lats)], axis=1)
        predicted = lax.dot_general(
            rows[k][...], weight, (((1,), (1,)), ((), ())), preferred_element_type=F32
        )
        live = jnp.zeros(tile.shape, F32)
        for t in range(tiles):
            alive = levels[first_slot + 2 * step + k] < counts[datasets[0, t]]
            live = live + jnp.where(jnp.logical_and(tile == t, alive), 1.0, 0.0)
        diff = predicted - target[k].astype(F32).reshape(places, outs)
        errs[k] = (diff * live).astype(BF16)
    for k in range(2):
        turned[k] = lax.dot_general(
            errs[k], rows[k][...], (((0,), (0,)), ((), ())), preferred_element_type=F32
        ).astype(BF16)
        for q in range(lats):
            core, x, y = q & 1, (q >> 1) & 1, (q >> 2) & 1
            outer, inner = (x, y) if k == 0 else (y, x)
            start = pl.multiple_of(jnp.bitwise_xor(place[0], q) * piece, piece)
            to = send if core else keep
            to[k, outer, inner, 0] = turned[k, :, pl.ds(start, piece)]
    for l in range(0, lats, 2):
        lanes = slice(l * piece, (l + 2) * piece)
        term = 0.0
        for k in range(2):
            weight = jnp.concatenate([gathered[l, k], gathered[l + 1, k]], axis=1)
            term = term + jnp.dot(errs[k], weight, preferred_element_type=F32) * scale[k][:, lanes]
        total[:, lanes] += term

    if final:

        @pl.when(step == pl.num_programs(0) - 1)
        def _():
            cols = out.shape[2]
            for s in range(tiles):
                at = lax.rem(place[1] + s, tiles)
                for r in range(WH):
                    start = pl.multiple_of(r * tiles * cols + at * cols, 8)
                    out[s, r] = total[pl.ds(start, cols), :].astype(BF16)


def slot_group(pair, pairs, lats, place, small, tile_of, band, scale, shift, gathered, targets, before):
    places, width = band.shape
    outs = targets.shape[-1]
    tiles = small[1].shape[1]
    piece = width // lats
    smem = pl.BlockSpec(memory_space=pltpu.SMEM)
    halves = jax.ShapeDtypeStruct((2, 2, 2, pairs, outs, piece), BF16)
    half_spec = pl.BlockSpec((2, 2, 2, 1, outs, piece), lambda i: (0, 0, 0, i, 0, 0))
    in_specs = [
        smem, smem, smem, smem,
        pl.BlockSpec((places, 1), lambda i: (0, 0)),
        pl.BlockSpec((places, width), lambda i: (0, 0)),
        pl.BlockSpec((2, 1, width), lambda i: (i + pair, 0, 0)),
        pl.BlockSpec((2, 1, width), lambda i: (i + pair, 0, 0)),
        pl.BlockSpec((lats, 2, outs, piece), lambda i: (0, i + pair, 0, 0)),
        pl.BlockSpec((2,) + targets.shape[1:], lambda i: (i + pair, 0, 0, 0)),
    ]
    args = [place, *small, tile_of, band, scale, shift, gathered, targets]
    final = before is not None
    scratch = [
        pltpu.VMEM((places, width), BF16),
        pltpu.VMEM((places, width), BF16),
        pltpu.VMEM((2, places, outs), BF16),
        pltpu.VMEM((2, outs, width), BF16),
    ]
    sums = jax.ShapeDtypeStruct((places, width), F32)
    if final:
        in_specs.append(pl.BlockSpec((places, width), lambda i: (0, 0)))
        args.append(before)
        scratch.insert(0, pltpu.VMEM(sums.shape, F32))
        sums = jax.ShapeDtypeStruct((tiles, WH, places // (WH * tiles), width), BF16)
    return pl.pallas_call(
        functools.partial(slot_kernel, 2 * pair, lats, tiles, final),
        grid=(pairs,),
        out_shape=(halves, halves, sums),
        in_specs=in_specs,
        out_specs=(half_spec, half_spec, pl.BlockSpec(sums.shape, lambda i: (0,) * len(sums.shape))),
        scratch_shapes=scratch,
        compiler_params=pltpu.CompilerParams(vmem_limit_bytes=VMEM_LIMIT),
        cost_estimate=pl.CostEstimate(
            flops=pairs * 12 * places * width * outs, bytes_accessed=pairs * 5_000_000, transcendentals=0
        ),
        name="slot_group",
    )(*args)


def join_kernel(norm, *refs):
    out = refs[-1]
    pairs = refs[:-1]
    slot = 0
    for i in range(0, len(pairs), 4):
        for k in range(pairs[i].shape[0]):
            for kept, came in (pairs[i : i + 2], pairs[i + 2 : i + 4]):
                out[slot] = (kept[k].astype(F32) + came[k].astype(F32)) * norm
                slot += 1


def join_heads(pairs, norm):
    flat = [array for pair in pairs for array in pair]
    slots = sum(kept.shape[0] for kept, _ in pairs)
    _, outs, piece = flat[0].shape
    vmem = pl.BlockSpec(memory_space=pltpu.VMEM)
    return pl.pallas_call(
        functools.partial(join_kernel, norm),
        out_shape=jax.ShapeDtypeStruct((slots, outs, piece), F32),
        in_specs=[vmem] * len(flat),
        out_specs=vmem,
        compiler_params=pltpu.CompilerParams(vmem_limit_bytes=VMEM_LIMIT),
        cost_estimate=pl.CostEstimate(flops=1_000_000, bytes_accessed=4_000_000, transcendentals=0),
        name="join_heads",
    )(*flat)


def fast_local(
    patches, norm_gain, input_proj, output_proj, level_scale, level_shift, head_weight, targets,
    level_counts, tile_dataset, slot_level,
):
    rows, cols, width = patches.shape
    lats, tiles = lax.axis_size("lat"), lax.axis_size("var")
    slots = head_weight.shape[0]
    lat, var = lax.axis_index("lat"), lax.axis_index("var")
    place = jnp.stack([lat, var]).astype(jnp.int32)
    gathered = lax.all_gather(jnp.transpose(head_weight, (0, 2, 1)), "lat", axis=0, tiled=False)

    right = [(i, (i + 1) % tiles) for i in range(tiles)]
    up = [(i, i + 1) for i in range(lats - 1)]
    down = [(i + 1, i) for i in range(lats - 1)]
    both = lambda pairs: [(a * tiles + c, b * tiles + d) for a, b in pairs for c, d in right]
    low, high = patches[HR:], patches[:HR]
    above = lax.ppermute(low, "lat", up)
    below = lax.ppermute(high, "lat", down)
    left = lax.ppermute(patches[:, cols - HC :], "var", right)
    above_left = lax.ppermute(low[:, cols - HC :], ("lat", "var"), both(up))
    below_left = lax.ppermute(high[:, cols - HC :], ("lat", "var"), both(down))
    mine = attention(
        place, patches, (left, above, above_left, below, below_left), norm_gain, input_proj, output_proj, lats
    )
    pieces = [mine]
    for s in range(1, tiles):
        pieces.append(lax.ppermute(mine, "var", [(i, (i + s) % tiles) for i in range(tiles)]))
    band, latent = band_latents(place, pieces, cols)

    tile_of = jnp.asarray(np.arange(rows * tiles * cols)[:, None] % (tiles * cols) // cols, jnp.int32)
    scale3, shift3 = level_scale.reshape(slots, 1, width), level_shift.reshape(slots, 1, width)
    small = (level_counts, tile_dataset, slot_level)
    flip = lambda array, bit: lax.ppermute(array, "lat", [(i, i ^ bit) for i in range(lats)])
    add = lambda a, b: (a.astype(F32) + b.astype(F32)).astype(BF16)
    common = (lats, place, small, tile_of, band, scale3, shift3, gathered, targets)
    most = slots // 4 + 1
    keep_a, send_a, so_far = slot_group(0, most, *common, None)
    keep_b, send_b, terms = slot_group(most, slots // 2 - most, *common, so_far)
    pairs = []
    for keep, send in ((keep_a, send_a), (keep_b, send_b)):
        came = flip(send, 1)
        bits = (2, 4)
        kept = [add(keep[k, 0], came[k, 0]) for k in range(2)]
        sent = [flip(add(keep[k, 1], came[k, 1]), bits[k]) for k in range(2)]
        for k in range(2):
            last = flip(add(kept[k][1], sent[k][1]), bits[1 - k])
            pairs.append((add(kept[k][0], sent[k][0]), last))
    total = terms[0].astype(F32)
    for s in range(1, tiles):
        came = lax.ppermute(terms[s], "var", [(i, (i + s) % tiles) for i in range(tiles)])
        total = total + came.astype(F32)
    grad_latent = total.astype(BF16)
    grad_head = join_heads(pairs, 1.0 / math.sqrt(lats * rows * tiles * cols))
    return (latent, grad_latent, jnp.transpose(grad_head, (0, 2, 1)))


def padded(array, sides, width, wrap):
    for axis, dim in sides:
        size, length = (lax.axis_size(axis), array.shape[dim])
        up = [(i, (i + 1) % size) for i in range(size if wrap else size - 1)]
        down = [(j, i) for i, j in up]
        last = lax.slice_in_dim(array, length - width, length, axis=dim)
        initial = lax.slice_in_dim(array, 0, width, axis=dim)
        before = lax.ppermute(last, axis, up)
        after = lax.ppermute(initial, axis, down)
        array = jnp.concatenate([before, array, after], axis=dim)
    return array


def layer_norm(values, gain):
    wide = values.astype(jnp.float32)
    average = jnp.mean(wide, axis=-1, keepdims=True)
    centred = wide - average
    variance = jnp.mean(centred * centred, axis=-1, keepdims=True)
    return (centred * lax.rsqrt(variance + EPS) * gain).astype(jnp.bfloat16)


def window_attention(query_ext, keyval, row_valid, heads):
    ext_rows, ext_cols, width = query_ext.shape
    head_size = width // heads
    win_rows = ext_rows // WH
    win_cols = ext_cols // WW

    def split(values, parts):
        shaped = values.reshape(win_rows, WH, win_cols, WW, parts, heads, head_size)
        return shaped.transpose(0, 2, 1, 3, 4, 5, 6).reshape(
            win_rows * win_cols, WH * WW, parts, heads, head_size
        )

    query_win = split(query_ext, 1)[:, :, 0]
    pairs = split(keyval, 2)
    key_win = pairs[:, :, 0]
    value_win = pairs[:, :, 1]
    key_mask = jnp.broadcast_to(
        row_valid.reshape(win_rows, 1, WH, 1), (win_rows, win_cols, WH, WW)
    ).reshape(win_rows * win_cols, WH * WW)
    scores = jnp.einsum(
        "wqhd,wkhd->whqk", query_win, key_win, preferred_element_type=jnp.float32
    ) / math.sqrt(head_size)
    scores = jnp.where(key_mask[:, None, None, :], scores, -jnp.inf)
    peak = jnp.max(scores, axis=-1, keepdims=True)
    weights = jnp.exp(scores - peak)
    probs = (weights / jnp.sum(weights, axis=-1, keepdims=True)).astype(jnp.bfloat16)
    mixed = jnp.einsum("whqk,wkhd->wqhd", probs, value_win, preferred_element_type=jnp.float32)
    return (
        mixed.reshape(win_rows, win_cols, WH, WW, width)
        .transpose(0, 2, 1, 3, 4)
        .reshape(ext_rows, ext_cols, width)
    )


def slot_terms(piece, target_rows, live_cols, level_scale, level_shift, heads_full):
    piece_wide = piece.astype(jnp.float32)
    rows = (
        piece_wide[None] * level_scale[:, None, None, :] + level_shift[:, None, None, :]
    ).astype(jnp.bfloat16)
    predicted = jnp.einsum("krnd,kdo->krno", rows, heads_full, preferred_element_type=jnp.float32)
    errors = ((predicted - target_rows.astype(jnp.float32)) * live_cols[:, None, :, None]).astype(
        jnp.bfloat16
    )
    back_grad = jnp.einsum("krno,kdo->krnd", errors, heads_full, preferred_element_type=jnp.float32)
    piece_grad = jnp.sum(back_grad * level_scale[:, None, None, :], axis=0)
    head_add = jnp.einsum("krnd,krno->dko", rows, errors, preferred_element_type=jnp.float32)
    return (piece_grad, head_add)


def local(
    patches,
    norm_gain,
    input_proj,
    output_proj,
    level_scale,
    level_shift,
    head_weight,
    targets,
    level_counts,
    tile_dataset,
    slot_level,
):
    band_rows, band_cols, width = patches.shape
    half_rows = WH // 2
    half_cols = WW // 2
    lat_count = lax.axis_size("lat")
    var_count = lax.axis_size("var")
    lat_place = lax.axis_index("lat")
    ext_rows = band_rows + WH
    ext_cols = band_cols + WW
    extended = padded(patches, (("lat", 0),), half_rows, False)
    extended = padded(extended, (("var", 1),), half_cols, True)
    normed_ext = layer_norm(extended, norm_gain)
    keyval = jnp.dot(
        normed_ext.reshape(-1, width), input_proj[:, width:], preferred_element_type=jnp.float32
    )
    keyval = keyval.astype(jnp.bfloat16).reshape(ext_rows, ext_cols, 2 * width)
    normed = normed_ext[half_rows : half_rows + band_rows, half_cols : half_cols + band_cols]
    queries = jnp.dot(
        normed.reshape(-1, width), input_proj[:, :width], preferred_element_type=jnp.float32
    )
    queries = queries.astype(jnp.bfloat16).reshape(band_rows, band_cols, width)
    query_ext = jnp.pad(queries, ((half_rows, WH - half_rows), (half_cols, WW - half_cols), (0, 0)))
    global_row = lat_place * band_rows - half_rows + jnp.arange(ext_rows, dtype=jnp.int32)
    row_valid = (global_row >= 0) & (global_row < lat_count * band_rows)
    mixed = window_attention(query_ext, keyval, row_valid, HEADS)
    attn = mixed[half_rows : half_rows + band_rows, half_cols : half_cols + band_cols].astype(
        jnp.bfloat16
    )
    update = jnp.dot(
        attn.reshape(-1, width), output_proj, preferred_element_type=jnp.float32
    ).reshape(band_rows, band_cols, width)
    latent = (patches.astype(jnp.float32) + update).astype(jnp.bfloat16)
    dataset_row = tile_dataset[0]
    dataset_ids = jnp.arange(level_counts.shape[0], dtype=jnp.int32)
    tile_levels = jnp.sum(
        jnp.where(dataset_row[:, None] == dataset_ids[None, :], level_counts[None, :], 0), axis=1
    )
    live_tiles = (slot_level[None, :] < tile_levels[:, None]).astype(jnp.float32)
    heads_full = lax.all_gather(head_weight, "lat", axis=1, tiled=True)
    tile_ids = jnp.arange(var_count, dtype=jnp.int32)
    piece = lax.all_gather(latent, "var", axis=1, tiled=True)
    piece_cols = piece.shape[1]
    column_tile = jnp.arange(piece_cols, dtype=jnp.int32) // band_cols
    onehot = (column_tile[:, None] == tile_ids[None, :]).astype(jnp.float32)
    column_live = jnp.dot(onehot, live_tiles)
    piece_grad, head_add = slot_terms(
        piece, targets, column_live.T, level_scale, level_shift, heads_full
    )
    latent_terms = piece_grad
    latent_terms, head_terms = (latent_terms, head_add)
    grad_latent = lax.psum_scatter(
        latent_terms.astype(jnp.bfloat16), "var", scatter_dimension=1, tiled=True
    )
    head_terms = head_terms * (1.0 / math.sqrt(lat_count * band_rows * var_count * band_cols))
    mine = lax.psum_scatter(
        head_terms.astype(jnp.bfloat16), "lat", scatter_dimension=0, tiled=True
    ).astype(jnp.float32)
    grad_head = jnp.transpose(mine, (1, 0, 2))
    return (latent, grad_latent, grad_head)


def solution(mesh):
    in_specs = (
        P("lat", "var", None),
        P(),
        P(),
        P(),
        P("var", None),
        P("var", None),
        P("var", "lat", None),
        P("var", "lat", None, None),
        P(),
        P("lat", None),
        P("var"),
    )
    fast = mesh.shape["lat"] == 8 and mesh.shape["var"] == 4
    body = fast_local if fast else local
    out_specs = (P("lat", "var", None), P("lat", "var", None), P("var", "lat", None))
    return jax.shard_map(body, mesh=mesh, in_specs=in_specs, out_specs=out_specs, check_vma=False)
```

```python
import functools
import math

import jax
import jax.numpy as jnp
import numpy as np
from jax import lax
from jax.experimental import pallas as pl
from jax.experimental.pallas import tpu as pltpu
from jax.sharding import PartitionSpec as P

HEADS = 16
WH = 6
WW = 12
EPS = 1e-05
HR = WH // 2
HC = WW // 2
QP = 48
LEFT = 8
VMEM_LIMIT = 48 * 1024 * 1024
F32 = jnp.float32
BF16 = jnp.bfloat16


def source_base(cols):
    own = 0
    left = own + WH * cols
    above = left + WH * LEFT
    above_left = above + HR * cols
    below = above_left + HR * LEFT
    below_left = below + HR * cols
    total = below_left + HR * LEFT
    return own, left, above, above_left, below, below_left, total


def gather_maps(cols):
    own, left, above, above_left, below, below_left, total = source_base(cols)
    win_cols = cols // WW
    windows = 2 * win_cols

    def source(part, win_row, row, col):
        if part == 0:
            r = win_row * HR + row
            return left + r * LEFT + col if col < HC else own + r * cols + col - HC
        if win_row == 0:
            return above_left + row * LEFT + col if col < HC else above + row * cols + col - HC
        return below_left + row * LEFT + col if col < HC else below + row * cols + col - HC

    into = np.zeros((windows * 2 * QP, total), np.float32)
    keep = np.zeros((WH * cols, total), np.float32)
    back = np.zeros((WH * cols, windows * QP), np.float32)
    for win in range(windows):
        win_row, win_col = divmod(win, win_cols)
        for part in range(2):
            for row in range(HR):
                for c in range(WW):
                    at = source(part, win_row, row, win_col * WW + c)
                    slot = row * WW + c
                    into[win * 2 * QP + part * QP + slot, at] = 1
                    if part == 0:
                        natural = (win_row * HR + row) * cols + win_col * WW + c
                        keep[natural, at] = 1
                        back[natural, win * QP + slot] = 1
    return into, keep, back


def attention_kernel(
    bands,
    place,
    left,
    above,
    above_left,
    below,
    below_left,
    own_hbm,
    gain,
    maps_hbm,
    in_hbm,
    out_hbm,
    out,
    raw,
    qkv,
    attn,
    own,
    maps,
    proj_in,
    proj_out,
    sems,
):
    moves = [
        pltpu.make_async_copy(src, dst, sems.at[i])
        for i, (src, dst) in enumerate(
            ((own_hbm, own), (maps_hbm, maps), (in_hbm, proj_in), (out_hbm, proj_out))
        )
    ]
    for move in moves:
        move.start()
    cols, width = own.shape[1], own.shape[2]
    bases = source_base(cols)
    total = bases[-1]
    win_cols = cols // WW
    windows = 2 * win_cols
    slots = windows * 2 * QP
    head_size = width // HEADS
    quad = 256 // head_size
    for base, ref in zip(bases, (own, left, above, above_left, below, below_left)):
        count = ref.shape[0]
        if ref is own:
            moves[0].wait()
        if ref.shape[1] == cols:
            raw[base : base + count * cols, :] = ref[...].astype(F32).reshape(count * cols, width)
        else:
            for r in range(count):
                raw[base + r * LEFT : base + (r + 1) * LEFT, :] = jnp.zeros((LEFT, width), F32)
                raw[base + r * LEFT : base + r * LEFT + HC, :] = ref[r].astype(F32)
    wide = raw[...]
    average = jnp.mean(wide, axis=-1, keepdims=True)
    centred = wide - average
    variance = jnp.mean(centred * centred, axis=-1, keepdims=True)
    normed = (centred * lax.rsqrt(variance + EPS) * gain[...]).astype(BF16)
    moves[1].wait()
    win_x = jnp.dot(maps[0:slots, :], normed, preferred_element_type=F32).astype(BF16)
    moves[2].wait()
    step = 512
    for j in range(3 * width // step):
        part = slice(j * step, (j + 1) * step)
        qkv[:, part] = jnp.dot(win_x, proj_in[:, part], preferred_element_type=F32).astype(BF16)
    lane = lax.broadcasted_iota(jnp.int32, (1, 256), 1) // head_size
    heads = [jnp.where(lane == h, 1.0, 0.0) for h in range(quad)]
    key_id = lax.broadcasted_iota(jnp.int32, (1, 2 * QP), 1)
    scale = 1.0 / math.sqrt(head_size)
    for win in range(windows):
        win_row = win // win_cols
        edge = 0 if win_row == 0 else bands - 1
        has_halo = place[0] != edge
        halo_keys = jnp.logical_and(key_id >= QP, key_id < QP + HR * WW)
        valid = jnp.logical_or(key_id < HR * WW, jnp.logical_and(halo_keys, has_halo))
        bias = jnp.where(valid, 0.0, -1e30)
        row0 = win * 2 * QP
        for g in range(width // 256):
            lanes = slice(g * 256, (g + 1) * 256)
            query = qkv[row0 : row0 + QP, lanes].astype(F32) * scale
            stacked = jnp.concatenate([query * h for h in heads], axis=0).astype(BF16)
            key = qkv[row0 : row0 + 2 * QP, width + g * 256 : width + (g + 1) * 256]
            value = qkv[row0 : row0 + 2 * QP, 2 * width + g * 256 : 2 * width + (g + 1) * 256]
            scores = (
                lax.dot_general(
                    stacked, key, (((1,), (1,)), ((), ())), preferred_element_type=F32
                )
                + bias
            )
            weights = jnp.exp(scores - jnp.max(scores, axis=-1, keepdims=True))
            probs = (weights / jnp.sum(weights, axis=-1, keepdims=True)).astype(BF16)
            mixed = jnp.dot(probs, value, preferred_element_type=F32)
            chosen = mixed[0:QP] * heads[0]
            for h in range(1, quad):
                chosen = chosen + mixed[h * QP : (h + 1) * QP] * heads[h]
            attn[win * QP : (win + 1) * QP, lanes] = chosen.astype(BF16)
    size = WH * cols
    keep = maps[slots : slots + size, :]
    back = maps[slots + size : slots + 2 * size, 0 : windows * QP]
    ordered = jnp.dot(back, attn[...], preferred_element_type=F32).astype(BF16)
    residual = jnp.dot(keep, raw[...].astype(BF16), preferred_element_type=F32)
    moves[3].wait()
    update = jnp.dot(ordered, proj_out[...], preferred_element_type=F32)
    out[...] = (residual + update).astype(BF16)


def attention(place, patches, pieces, gain, proj_in, proj_out, bands):
    rows, cols, width = patches.shape
    into, keep, back = gather_maps(cols)
    total = source_base(cols)[-1]
    windows = 2 * (cols // WW)
    back = np.pad(back, ((0, 0), (0, total - back.shape[1])))
    maps = np.concatenate([into, keep, back])
    vmem = pl.BlockSpec(memory_space=pltpu.VMEM)
    hbm = pl.BlockSpec(memory_space=pltpu.HBM)
    return pl.pallas_call(
        functools.partial(attention_kernel, bands),
        out_shape=jax.ShapeDtypeStruct((rows * cols, width), BF16),
        in_specs=[pl.BlockSpec(memory_space=pltpu.SMEM)] + [vmem] * 5 + [hbm, vmem, hbm, hbm, hbm],
        out_specs=vmem,
        scratch_shapes=[
            pltpu.VMEM((total, width), F32),
            pltpu.VMEM((windows * 2 * QP, 3 * width), BF16),
            pltpu.VMEM((windows * QP, width), BF16),
            pltpu.VMEM(patches.shape, BF16),
            pltpu.VMEM(maps.shape, BF16),
            pltpu.VMEM(proj_in.shape, BF16),
            pltpu.VMEM(proj_out.shape, BF16),
            pltpu.SemaphoreType.DMA((4,)),
        ],
        compiler_params=pltpu.CompilerParams(vmem_limit_bytes=53 * 1024 * 1024),
        cost_estimate=pl.CostEstimate(
            flops=6_000_000_000, bytes_accessed=12_000_000, transcendentals=400_000
        ),
        name="window_attention",
    )(
        place,
        *pieces,
        patches,
        gain.reshape(1, width),
        jnp.asarray(maps, BF16),
        proj_in,
        proj_out,
    )


def band_map(tiles, cols):
    wide = tiles * cols
    chosen = np.zeros((WH * wide, WH * wide), np.float32)
    for r in range(WH):
        for c in range(wide):
            tile, at = divmod((c + HC) % wide, cols)
            chosen[r * wide + c, tile * WH * cols + r * cols + at] = 1
    return chosen


def band_kernel(tiles, cols, place, chosen, *refs):
    pieces, (band, latent, laid, wide) = refs[:tiles], refs[tiles:]
    size = WH * cols
    var = place[1]
    for s in range(tiles):
        tile = lax.rem(var + tiles - s, tiles)
        laid[pl.ds(pl.multiple_of(tile * size, 16), size), :] = pieces[s][...]
    wide[...] = jnp.dot(chosen[...], laid[...], preferred_element_type=F32)
    band[...] = wide[...].astype(BF16)
    for r in range(WH):
        start = pl.multiple_of(r * tiles * cols + var * cols, 8)
        latent[r] = wide[pl.ds(start, cols), :].astype(BF16)


def band_latents(place, pieces, cols):
    tiles = len(pieces)
    width = pieces[0].shape[1]
    total = WH * tiles * cols
    vmem = pl.BlockSpec(memory_space=pltpu.VMEM)
    return pl.pallas_call(
        functools.partial(band_kernel, tiles, cols),
        out_shape=(
            jax.ShapeDtypeStruct((total, width), BF16),
            jax.ShapeDtypeStruct((WH, cols, width), BF16),
        ),
        in_specs=[pl.BlockSpec(memory_space=pltpu.SMEM)] + [vmem] * (tiles + 1),
        out_specs=(vmem, vmem),
        scratch_shapes=[pltpu.VMEM((total, width), BF16), pltpu.VMEM((total, width), F32)],
        compiler_params=pltpu.CompilerParams(vmem_limit_bytes=VMEM_LIMIT),
        cost_estimate=pl.CostEstimate(
            flops=2 * total * total * width, bytes_accessed=4_000_000, transcendentals=0
        ),
        name="band_latents",
    )(place, jnp.asarray(band_map(tiles, cols), BF16), *pieces)


def slot_errors(slot, tiles, counts, datasets, levels, tile, rows, weight, target):
    predicted = lax.dot_general(
        rows, weight, (((1,), (1,)), ((), ())), preferred_element_type=F32
    )
    live = jnp.zeros(tile.shape, F32)
    for t in range(tiles):
        alive = levels[slot] < counts[datasets[0, t]]
        live = live + jnp.where(jnp.logical_and(tile == t, alive), 1.0, 0.0)
    diff = predicted - target.astype(F32).reshape(predicted.shape)
    return (diff * live).astype(BF16)


def head_halves(k, lats, lat, errors, rows, turned, keep, send):
    turned[k] = lax.dot_general(
        errors, rows, (((0,), (0,)), ((), ())), preferred_element_type=F32
    ).astype(BF16)
    piece = turned.shape[-1] // lats
    for q in range(lats):
        core, x, y = q & 1, (q >> 1) & 1, (q >> 2) & 1
        outer, inner = (x, y) if k == 0 else (y, x)
        start = pl.multiple_of(jnp.bitwise_xor(lat, q) * piece, piece)
        to = send if core else keep
        to[k, outer, inner, 0] = turned[k, :, pl.ds(start, piece)]


def scaled_rows(band, scale, shift, rows):
    for k in range(2):
        rows[k][...] = (band[...].astype(F32) * scale[k] + shift[k]).astype(BF16)


def add_back(lats, errs, gathered, scale, total):
    piece = gathered.shape[-1]
    for l in range(0, lats, 2):
        lanes = slice(l * piece, (l + 2) * piece)
        term = 0.0
        for k in range(2):
            weight = jnp.concatenate([gathered[l, k], gathered[l + 1, k]], axis=1)
            term = term + jnp.dot(errs[k], weight, preferred_element_type=F32) * scale[k][:, lanes]
        total[:, lanes] += term


def first_kernel(lats, tiles, place, counts, datasets, levels, tile_of, band, scale, shift, gathered, target,
                 keep, send, total, rows0, rows1, errs, turned):
    rows = (rows0, rows1)
    step = pl.program_id(0)

    @pl.when(step == 0)
    def _():
        total[...] = jnp.zeros_like(total)

    tile = tile_of[...]
    scaled_rows(band, scale, shift, rows)
    for k in range(2):
        weight = jnp.concatenate([gathered[l, k] for l in range(lats)], axis=1)
        errs[k] = slot_errors(
            2 * step + k, tiles, counts, datasets, levels, tile, rows[k][...], weight, target[k]
        )
    for k in range(2):
        head_halves(k, lats, place[0], errs[k], rows[k][...], turned, keep, send)
    add_back(lats, errs, gathered, scale, total)


def second_kernel(first_slot, lats, tiles, place, counts, datasets, levels, tile_of, band, scale, shift,
                  gathered, target, before, errs, out, total, rows0, rows1):
    rows = (rows0, rows1)
    step = pl.program_id(0)

    @pl.when(step == 0)
    def _():
        total[...] = before[...]

    tile = tile_of[...]
    scaled_rows(band, scale, shift, rows)
    for k in range(2):
        weight = jnp.concatenate([gathered[l, k] for l in range(lats)], axis=1)
        errs[k] = slot_errors(
            first_slot + 2 * step + k, tiles, counts, datasets, levels, tile, rows[k][...], weight, target[k]
        )
    add_back(lats, errs, gathered, scale, total)

    @pl.when(step == pl.num_programs(0) - 1)
    def _():
        cols = out.shape[2]
        for s in range(tiles):
            for r in range(WH):
                start = (r * tiles + s) * cols
                out[s, r] = total[start : start + cols, :].astype(BF16)


def heads_kernel(lats, place, band, scale, shift, errs, *refs):
    keep, send, rows0, rows1, turned = refs[-5:]
    rows = (rows0, rows1)
    scaled_rows(band, scale, shift, rows)
    for k in range(2):
        head_halves(k, lats, place[0], errs[k], rows[k][...], turned, keep, send)


def slot_specs(pair, lats, band, outs):
    places, width = band.shape
    piece = width // lats
    return dict(
        smem=pl.BlockSpec(memory_space=pltpu.SMEM),
        tile_of=pl.BlockSpec((places, 1), lambda i: (0, 0)),
        band=pl.BlockSpec((places, width), lambda i: (0, 0)),
        level=pl.BlockSpec((2, 1, width), lambda i: (i + pair, 0, 0)),
        heads=pl.BlockSpec((lats, 2, outs, piece), lambda i: (0, i + pair, 0, 0)),
        halves=pl.BlockSpec((2, 2, 2, 1, outs, piece), lambda i: (0, 0, 0, i, 0, 0)),
        errs=pl.BlockSpec((2, places, outs), lambda i: (i, 0, 0)),
        rows=pltpu.VMEM((places, width), BF16),
        turned=pltpu.VMEM((2, outs, width), BF16),
    )


def slot_cost(pairs, products, places, width, outs):
    return pl.CostEstimate(
        flops=pairs * 4 * products * places * width * outs, bytes_accessed=pairs * 4_000_000, transcendentals=0
    )


def first_slots(pairs, lats, place, small, tile_of, band, scale, shift, gathered, targets):
    places, width = band.shape
    outs = targets.shape[-1]
    sp = slot_specs(0, lats, band, outs)
    halves = jax.ShapeDtypeStruct((2, 2, 2, pairs, outs, width // lats), BF16)
    target = pl.BlockSpec((2,) + targets.shape[1:], lambda i: (i, 0, 0, 0))
    return pl.pallas_call(
        functools.partial(first_kernel, lats, small[1].shape[1]),
        grid=(pairs,),
        out_shape=(halves, halves, jax.ShapeDtypeStruct((places, width), F32)),
        in_specs=[sp["smem"]] * 4
        + [sp["tile_of"], sp["band"], sp["level"], sp["level"], sp["heads"], target],
        out_specs=(sp["halves"], sp["halves"], sp["band"]),
        scratch_shapes=[sp["rows"], sp["rows"], pltpu.VMEM((2, places, outs), BF16), sp["turned"]],
        compiler_params=pltpu.CompilerParams(vmem_limit_bytes=VMEM_LIMIT),
        cost_estimate=slot_cost(pairs, 3, places, width, outs),
        name="first_slots",
    )(place, *small, tile_of, band, scale, shift, gathered, targets)


def second_slots(pair, pairs, lats, place, small, tile_of, band, scale, shift, gathered, targets, before):
    places, width = band.shape
    outs = targets.shape[-1]
    tiles = small[1].shape[1]
    sp = slot_specs(pair, lats, band, outs)
    target = pl.BlockSpec((2,) + targets.shape[1:], lambda i: (i + pair, 0, 0, 0))
    terms = (tiles, WH, places // (WH * tiles), width)
    return pl.pallas_call(
        functools.partial(second_kernel, 2 * pair, lats, tiles),
        grid=(pairs,),
        out_shape=(
            jax.ShapeDtypeStruct((2 * pairs, places, outs), BF16),
            jax.ShapeDtypeStruct(terms, BF16),
        ),
        in_specs=[sp["smem"]] * 4
        + [sp["tile_of"], sp["band"], sp["level"], sp["level"], sp["heads"], target, sp["band"]],
        out_specs=(sp["errs"], pl.BlockSpec(terms, lambda i: (0, 0, 0, 0))),
        scratch_shapes=[pltpu.VMEM((places, width), F32), sp["rows"], sp["rows"]],
        compiler_params=pltpu.CompilerParams(vmem_limit_bytes=VMEM_LIMIT),
        cost_estimate=slot_cost(pairs, 2, places, width, outs),
        name="second_slots",
    )(place, *small, tile_of, band, scale, shift, gathered, targets, before)


def second_heads(pair, pairs, lats, place, band, scale, shift, errs, after):
    places, width = band.shape
    outs = errs.shape[-1]
    sp = slot_specs(pair, lats, band, outs)
    halves = jax.ShapeDtypeStruct((2, 2, 2, pairs, outs, width // lats), BF16)
    return pl.pallas_call(
        functools.partial(heads_kernel, lats),
        grid=(pairs,),
        out_shape=(halves, halves),
        in_specs=[sp["smem"], sp["band"], sp["level"], sp["level"], sp["errs"]]
        + [pl.BlockSpec(memory_space=pl.ANY)] * len(after),
        out_specs=(sp["halves"], sp["halves"]),
        scratch_shapes=[sp["rows"], sp["rows"], sp["turned"]],
        compiler_params=pltpu.CompilerParams(vmem_limit_bytes=VMEM_LIMIT),
        cost_estimate=slot_cost(pairs, 1, places, width, outs),
        name="second_heads",
    )(place, band, scale, shift, errs, *after)


def join_kernel(norm, *refs):
    out = refs[-1]
    pairs = refs[:-1]
    slot = 0
    for i in range(0, len(pairs), 4):
        for k in range(pairs[i].shape[0]):
            for kept, came in (pairs[i : i + 2], pairs[i + 2 : i + 4]):
                out[slot] = (kept[k].astype(F32) + came[k].astype(F32)) * norm
                slot += 1


def join_heads(pairs, norm):
    flat = [array for pair in pairs for array in pair]
    slots = sum(kept.shape[0] for kept, _ in pairs)
    _, outs, piece = flat[0].shape
    vmem = pl.BlockSpec(memory_space=pltpu.VMEM)
    return pl.pallas_call(
        functools.partial(join_kernel, norm),
        out_shape=jax.ShapeDtypeStruct((slots, outs, piece), F32),
        in_specs=[vmem] * len(flat),
        out_specs=vmem,
        compiler_params=pltpu.CompilerParams(vmem_limit_bytes=VMEM_LIMIT),
        cost_estimate=pl.CostEstimate(flops=1_000_000, bytes_accessed=4_000_000, transcendentals=0),
        name="join_heads",
    )(*flat)


def fast_local(
    patches, norm_gain, input_proj, output_proj, level_scale, level_shift, head_weight, targets,
    level_counts, tile_dataset, slot_level,
):
    rows, cols, width = patches.shape
    lats, tiles = lax.axis_size("lat"), lax.axis_size("var")
    slots = head_weight.shape[0]
    lat, var = lax.axis_index("lat"), lax.axis_index("var")
    place = jnp.stack([lat, var]).astype(jnp.int32)
    gathered = lax.all_gather(jnp.transpose(head_weight, (0, 2, 1)), "lat", axis=0, tiled=False)

    right = [(i, (i + 1) % tiles) for i in range(tiles)]
    up = [(i, i + 1) for i in range(lats - 1)]
    down = [(i + 1, i) for i in range(lats - 1)]
    both = lambda pairs: [(a * tiles + c, b * tiles + d) for a, b in pairs for c, d in right]
    low, high = patches[HR:], patches[:HR]
    above = lax.ppermute(low, "lat", up)
    below = lax.ppermute(high, "lat", down)
    left = lax.ppermute(patches[:, cols - HC :], "var", right)
    above_left = lax.ppermute(low[:, cols - HC :], ("lat", "var"), both(up))
    below_left = lax.ppermute(high[:, cols - HC :], ("lat", "var"), both(down))
    mine = attention(
        place, patches, (left, above, above_left, below, below_left), norm_gain, input_proj, output_proj, lats
    )
    pieces = [mine]
    for s in range(1, tiles):
        pieces.append(lax.ppermute(mine, "var", [(i, (i + s) % tiles) for i in range(tiles)]))
    band, latent = band_latents(place, pieces, cols)

    tile_of = jnp.asarray(np.arange(rows * tiles * cols)[:, None] % (tiles * cols) // cols, jnp.int32)
    scale3, shift3 = level_scale.reshape(slots, 1, width), level_shift.reshape(slots, 1, width)
    small = (level_counts, tile_dataset, slot_level)
    flip = lambda array, bit: lax.ppermute(array, "lat", [(i, i ^ bit) for i in range(lats)])
    add = lambda a, b: (a.astype(F32) + b.astype(F32)).astype(BF16)
    common = (lats, place, small, tile_of, band, scale3, shift3, gathered, targets)
    most = slots // 4 + 1
    rest = slots // 2 - most
    bits = (2, 4)

    def halve(keep, send):
        came = flip(send, 1)
        return (
            [add(keep[k, 0], came[k, 0]) for k in range(2)],
            [add(keep[k, 1], came[k, 1]) for k in range(2)],
        )

    keep, send, so_far = first_slots(most, *common)
    errs, terms = second_slots(most, rest, *common, so_far)
    kept_a, sent_a = halve(keep, send)
    keep, send = second_heads(most, rest, lats, place, band, scale3, shift3, errs, sent_a)
    kept_b, sent_b = halve(keep, send)
    grad_latent = lax.psum_scatter(terms, "var", scatter_dimension=0, tiled=False)
    pairs = []
    for kept, sent in ((kept_a, sent_a), (kept_b, sent_b)):
        came = [flip(sent[k], bits[k]) for k in range(2)]
        for k in range(2):
            last = flip(add(kept[k][1], came[k][1]), bits[1 - k])
            pairs.append((add(kept[k][0], came[k][0]), last))
    grad_head = join_heads(pairs, 1.0 / math.sqrt(lats * rows * tiles * cols))
    return (latent, grad_latent, jnp.transpose(grad_head, (0, 2, 1)))


def padded(array, sides, width, wrap):
    for axis, dim in sides:
        size, length = (lax.axis_size(axis), array.shape[dim])
        up = [(i, (i + 1) % size) for i in range(size if wrap else size - 1)]
        down = [(j, i) for i, j in up]
        last = lax.slice_in_dim(array, length - width, length, axis=dim)
        initial = lax.slice_in_dim(array, 0, width, axis=dim)
        before = lax.ppermute(last, axis, up)
        after = lax.ppermute(initial, axis, down)
        array = jnp.concatenate([before, array, after], axis=dim)
    return array


def layer_norm(values, gain):
    wide = values.astype(jnp.float32)
    average = jnp.mean(wide, axis=-1, keepdims=True)
    centred = wide - average
    variance = jnp.mean(centred * centred, axis=-1, keepdims=True)
    return (centred * lax.rsqrt(variance + EPS) * gain).astype(jnp.bfloat16)


def window_attention(query_ext, keyval, row_valid, heads):
    ext_rows, ext_cols, width = query_ext.shape
    head_size = width // heads
    win_rows = ext_rows // WH
    win_cols = ext_cols // WW

    def split(values, parts):
        shaped = values.reshape(win_rows, WH, win_cols, WW, parts, heads, head_size)
        return shaped.transpose(0, 2, 1, 3, 4, 5, 6).reshape(
            win_rows * win_cols, WH * WW, parts, heads, head_size
        )

    query_win = split(query_ext, 1)[:, :, 0]
    pairs = split(keyval, 2)
    key_win = pairs[:, :, 0]
    value_win = pairs[:, :, 1]
    key_mask = jnp.broadcast_to(
        row_valid.reshape(win_rows, 1, WH, 1), (win_rows, win_cols, WH, WW)
    ).reshape(win_rows * win_cols, WH * WW)
    scores = jnp.einsum(
        "wqhd,wkhd->whqk", query_win, key_win, preferred_element_type=jnp.float32
    ) / math.sqrt(head_size)
    scores = jnp.where(key_mask[:, None, None, :], scores, -jnp.inf)
    peak = jnp.max(scores, axis=-1, keepdims=True)
    weights = jnp.exp(scores - peak)
    probs = (weights / jnp.sum(weights, axis=-1, keepdims=True)).astype(jnp.bfloat16)
    mixed = jnp.einsum("whqk,wkhd->wqhd", probs, value_win, preferred_element_type=jnp.float32)
    return (
        mixed.reshape(win_rows, win_cols, WH, WW, width)
        .transpose(0, 2, 1, 3, 4)
        .reshape(ext_rows, ext_cols, width)
    )


def slot_terms(piece, target_rows, live_cols, level_scale, level_shift, heads_full):
    piece_wide = piece.astype(jnp.float32)
    rows = (
        piece_wide[None] * level_scale[:, None, None, :] + level_shift[:, None, None, :]
    ).astype(jnp.bfloat16)
    predicted = jnp.einsum("krnd,kdo->krno", rows, heads_full, preferred_element_type=jnp.float32)
    errors = ((predicted - target_rows.astype(jnp.float32)) * live_cols[:, None, :, None]).astype(
        jnp.bfloat16
    )
    back_grad = jnp.einsum("krno,kdo->krnd", errors, heads_full, preferred_element_type=jnp.float32)
    piece_grad = jnp.sum(back_grad * level_scale[:, None, None, :], axis=0)
    head_add = jnp.einsum("krnd,krno->dko", rows, errors, preferred_element_type=jnp.float32)
    return (piece_grad, head_add)


def local(
    patches,
    norm_gain,
    input_proj,
    output_proj,
    level_scale,
    level_shift,
    head_weight,
    targets,
    level_counts,
    tile_dataset,
    slot_level,
):
    band_rows, band_cols, width = patches.shape
    half_rows = WH // 2
    half_cols = WW // 2
    lat_count = lax.axis_size("lat")
    var_count = lax.axis_size("var")
    lat_place = lax.axis_index("lat")
    ext_rows = band_rows + WH
    ext_cols = band_cols + WW
    extended = padded(patches, (("lat", 0),), half_rows, False)
    extended = padded(extended, (("var", 1),), half_cols, True)
    normed_ext = layer_norm(extended, norm_gain)
    keyval = jnp.dot(
        normed_ext.reshape(-1, width), input_proj[:, width:], preferred_element_type=jnp.float32
    )
    keyval = keyval.astype(jnp.bfloat16).reshape(ext_rows, ext_cols, 2 * width)
    normed = normed_ext[half_rows : half_rows + band_rows, half_cols : half_cols + band_cols]
    queries = jnp.dot(
        normed.reshape(-1, width), input_proj[:, :width], preferred_element_type=jnp.float32
    )
    queries = queries.astype(jnp.bfloat16).reshape(band_rows, band_cols, width)
    query_ext = jnp.pad(queries, ((half_rows, WH - half_rows), (half_cols, WW - half_cols), (0, 0)))
    global_row = lat_place * band_rows - half_rows + jnp.arange(ext_rows, dtype=jnp.int32)
    row_valid = (global_row >= 0) & (global_row < lat_count * band_rows)
    mixed = window_attention(query_ext, keyval, row_valid, HEADS)
    attn = mixed[half_rows : half_rows + band_rows, half_cols : half_cols + band_cols].astype(
        jnp.bfloat16
    )
    update = jnp.dot(
        attn.reshape(-1, width), output_proj, preferred_element_type=jnp.float32
    ).reshape(band_rows, band_cols, width)
    latent = (patches.astype(jnp.float32) + update).astype(jnp.bfloat16)
    dataset_row = tile_dataset[0]
    dataset_ids = jnp.arange(level_counts.shape[0], dtype=jnp.int32)
    tile_levels = jnp.sum(
        jnp.where(dataset_row[:, None] == dataset_ids[None, :], level_counts[None, :], 0), axis=1
    )
    live_tiles = (slot_level[None, :] < tile_levels[:, None]).astype(jnp.float32)
    heads_full = lax.all_gather(head_weight, "lat", axis=1, tiled=True)
    tile_ids = jnp.arange(var_count, dtype=jnp.int32)
    piece = lax.all_gather(latent, "var", axis=1, tiled=True)
    piece_cols = piece.shape[1]
    column_tile = jnp.arange(piece_cols, dtype=jnp.int32) // band_cols
    onehot = (column_tile[:, None] == tile_ids[None, :]).astype(jnp.float32)
    column_live = jnp.dot(onehot, live_tiles)
    piece_grad, head_add = slot_terms(
        piece, targets, column_live.T, level_scale, level_shift, heads_full
    )
    latent_terms = piece_grad
    latent_terms, head_terms = (latent_terms, head_add)
    grad_latent = lax.psum_scatter(
        latent_terms.astype(jnp.bfloat16), "var", scatter_dimension=1, tiled=True
    )
    head_terms = head_terms * (1.0 / math.sqrt(lat_count * band_rows * var_count * band_cols))
    mine = lax.psum_scatter(
        head_terms.astype(jnp.bfloat16), "lat", scatter_dimension=0, tiled=True
    ).astype(jnp.float32)
    grad_head = jnp.transpose(mine, (1, 0, 2))
    return (latent, grad_latent, grad_head)


def solution(mesh):
    in_specs = (
        P("lat", "var", None),
        P(),
        P(),
        P(),
        P("var", None),
        P("var", None),
        P("var", "lat", None),
        P("var", "lat", None, None),
        P(),
        P("lat", None),
        P("var"),
    )
    fast = mesh.shape["lat"] == 8 and mesh.shape["var"] == 4
    body = fast_local if fast else local
    out_specs = (P("lat", "var", None), P("lat", "var", None), P("var", "lat", None))
    return jax.shard_map(body, mesh=mesh, in_specs=in_specs, out_specs=out_specs, check_vma=False)
```

```python
import functools
import math

import jax
import jax.numpy as jnp
import numpy as np
from jax import lax
from jax.experimental import pallas as pl
from jax.experimental.pallas import tpu as pltpu
from jax.sharding import PartitionSpec as P

HEADS = 16
WH = 6
WW = 12
EPS = 1e-05
HR = WH // 2
HC = WW // 2
QP = 48
LEFT = 8
VMEM_LIMIT = 48 * 1024 * 1024
F32 = jnp.float32
BF16 = jnp.bfloat16


def source_base(cols):
    own = 0
    left = own + WH * cols
    above = left + WH * LEFT
    above_left = above + HR * cols
    below = above_left + HR * LEFT
    below_left = below + HR * cols
    total = below_left + HR * LEFT
    return own, left, above, above_left, below, below_left, total


def gather_maps(cols):
    own, left, above, above_left, below, below_left, total = source_base(cols)
    win_cols = cols // WW
    windows = 2 * win_cols

    def source(part, win_row, row, col):
        if part == 0:
            r = win_row * HR + row
            return left + r * LEFT + col if col < HC else own + r * cols + col - HC
        if win_row == 0:
            return above_left + row * LEFT + col if col < HC else above + row * cols + col - HC
        return below_left + row * LEFT + col if col < HC else below + row * cols + col - HC

    into = np.zeros((windows * 2 * QP, total), np.float32)
    keep = np.zeros((WH * cols, total), np.float32)
    back = np.zeros((WH * cols, windows * QP), np.float32)
    for win in range(windows):
        win_row, win_col = divmod(win, win_cols)
        for part in range(2):
            for row in range(HR):
                for c in range(WW):
                    at = source(part, win_row, row, win_col * WW + c)
                    slot = row * WW + c
                    into[win * 2 * QP + part * QP + slot, at] = 1
                    if part == 0:
                        natural = (win_row * HR + row) * cols + win_col * WW + c
                        keep[natural, at] = 1
                        back[natural, win * QP + slot] = 1
    return into, keep, back


def attention_kernel(
    bands,
    place,
    left,
    above,
    above_left,
    below,
    below_left,
    own_hbm,
    gain,
    maps_hbm,
    in_hbm,
    out_hbm,
    out,
    raw,
    qkv,
    attn,
    own,
    maps,
    proj_in,
    proj_out,
    sems,
):
    moves = [
        pltpu.make_async_copy(src, dst, sems.at[i])
        for i, (src, dst) in enumerate(
            ((own_hbm, own), (maps_hbm, maps), (in_hbm, proj_in), (out_hbm, proj_out))
        )
    ]
    for move in moves:
        move.start()
    cols, width = own.shape[1], own.shape[2]
    bases = source_base(cols)
    total = bases[-1]
    win_cols = cols // WW
    windows = 2 * win_cols
    slots = windows * 2 * QP
    head_size = width // HEADS
    quad = 256 // head_size
    for base, ref in zip(bases, (own, left, above, above_left, below, below_left)):
        count = ref.shape[0]
        if ref is own:
            moves[0].wait()
        if ref.shape[1] == cols:
            raw[base : base + count * cols, :] = ref[...].astype(F32).reshape(count * cols, width)
        else:
            for r in range(count):
                raw[base + r * LEFT : base + (r + 1) * LEFT, :] = jnp.zeros((LEFT, width), F32)
                raw[base + r * LEFT : base + r * LEFT + HC, :] = ref[r].astype(F32)
    wide = raw[...]
    average = jnp.mean(wide, axis=-1, keepdims=True)
    centred = wide - average
    variance = jnp.mean(centred * centred, axis=-1, keepdims=True)
    normed = (centred * lax.rsqrt(variance + EPS) * gain[...]).astype(BF16)
    moves[1].wait()
    win_x = jnp.dot(maps[0:slots, :], normed, preferred_element_type=F32).astype(BF16)
    moves[2].wait()
    step = 512
    for j in range(3 * width // step):
        part = slice(j * step, (j + 1) * step)
        qkv[:, part] = jnp.dot(win_x, proj_in[:, part], preferred_element_type=F32).astype(BF16)
    lane = lax.broadcasted_iota(jnp.int32, (1, 256), 1) // head_size
    heads = [jnp.where(lane == h, 1.0, 0.0) for h in range(quad)]
    key_id = lax.broadcasted_iota(jnp.int32, (1, 2 * QP), 1)
    scale = 1.0 / math.sqrt(head_size)
    for win in range(windows):
        win_row = win // win_cols
        edge = 0 if win_row == 0 else bands - 1
        has_halo = place[0] != edge
        halo_keys = jnp.logical_and(key_id >= QP, key_id < QP + HR * WW)
        valid = jnp.logical_or(key_id < HR * WW, jnp.logical_and(halo_keys, has_halo))
        bias = jnp.where(valid, 0.0, -1e30)
        row0 = win * 2 * QP
        for g in range(width // 256):
            lanes = slice(g * 256, (g + 1) * 256)
            query = qkv[row0 : row0 + QP, lanes].astype(F32) * scale
            stacked = jnp.concatenate([query * h for h in heads], axis=0).astype(BF16)
            key = qkv[row0 : row0 + 2 * QP, width + g * 256 : width + (g + 1) * 256]
            value = qkv[row0 : row0 + 2 * QP, 2 * width + g * 256 : 2 * width + (g + 1) * 256]
            scores = (
                lax.dot_general(
                    stacked, key, (((1,), (1,)), ((), ())), preferred_element_type=F32
                )
                + bias
            )
            weights = jnp.exp(scores - jnp.max(scores, axis=-1, keepdims=True))
            probs = (weights / jnp.sum(weights, axis=-1, keepdims=True)).astype(BF16)
            mixed = jnp.dot(probs, value, preferred_element_type=F32)
            chosen = mixed[0:QP] * heads[0]
            for h in range(1, quad):
                chosen = chosen + mixed[h * QP : (h + 1) * QP] * heads[h]
            attn[win * QP : (win + 1) * QP, lanes] = chosen.astype(BF16)
    size = WH * cols
    keep = maps[slots : slots + size, :]
    back = maps[slots + size : slots + 2 * size, 0 : windows * QP]
    ordered = jnp.dot(back, attn[...], preferred_element_type=F32).astype(BF16)
    residual = jnp.dot(keep, raw[...].astype(BF16), preferred_element_type=F32)
    moves[3].wait()
    update = jnp.dot(ordered, proj_out[...], preferred_element_type=F32)
    out[...] = (residual + update).astype(BF16)


def attention(place, patches, pieces, gain, proj_in, proj_out, bands):
    rows, cols, width = patches.shape
    into, keep, back = gather_maps(cols)
    total = source_base(cols)[-1]
    windows = 2 * (cols // WW)
    back = np.pad(back, ((0, 0), (0, total - back.shape[1])))
    maps = np.concatenate([into, keep, back])
    vmem = pl.BlockSpec(memory_space=pltpu.VMEM)
    hbm = pl.BlockSpec(memory_space=pltpu.HBM)
    return pl.pallas_call(
        functools.partial(attention_kernel, bands),
        out_shape=jax.ShapeDtypeStruct((rows * cols, width), BF16),
        in_specs=[pl.BlockSpec(memory_space=pltpu.SMEM)] + [vmem] * 5 + [hbm, vmem, hbm, hbm, hbm],
        out_specs=vmem,
        scratch_shapes=[
            pltpu.VMEM((total, width), F32),
            pltpu.VMEM((windows * 2 * QP, 3 * width), BF16),
            pltpu.VMEM((windows * QP, width), BF16),
            pltpu.VMEM(patches.shape, BF16),
            pltpu.VMEM(maps.shape, BF16),
            pltpu.VMEM(proj_in.shape, BF16),
            pltpu.VMEM(proj_out.shape, BF16),
            pltpu.SemaphoreType.DMA((4,)),
        ],
        compiler_params=pltpu.CompilerParams(vmem_limit_bytes=53 * 1024 * 1024),
        cost_estimate=pl.CostEstimate(
            flops=6_000_000_000, bytes_accessed=12_000_000, transcendentals=400_000
        ),
        name="window_attention",
    )(
        place,
        *pieces,
        patches,
        gain.reshape(1, width),
        jnp.asarray(maps, BF16),
        proj_in,
        proj_out,
    )


def band_map(tiles, cols):
    wide = tiles * cols
    chosen = np.zeros((WH * wide, WH * wide), np.float32)
    for r in range(WH):
        for c in range(wide):
            tile, at = divmod((c + HC) % wide, cols)
            chosen[r * wide + c, tile * WH * cols + r * cols + at] = 1
    return chosen


def band_kernel(tiles, cols, place, chosen, *refs):
    pieces, (band, latent, laid, wide) = refs[:tiles], refs[tiles:]
    size = WH * cols
    var = place[1]
    for s in range(tiles):
        tile = lax.rem(var + tiles - s, tiles)
        laid[pl.ds(pl.multiple_of(tile * size, 16), size), :] = pieces[s][...]
    wide[...] = jnp.dot(chosen[...], laid[...], preferred_element_type=F32)
    band[...] = wide[...].astype(BF16)
    for r in range(WH):
        start = pl.multiple_of(r * tiles * cols + var * cols, 8)
        latent[r] = wide[pl.ds(start, cols), :].astype(BF16)


def band_latents(place, pieces, cols):
    tiles = len(pieces)
    width = pieces[0].shape[1]
    total = WH * tiles * cols
    vmem = pl.BlockSpec(memory_space=pltpu.VMEM)
    return pl.pallas_call(
        functools.partial(band_kernel, tiles, cols),
        out_shape=(
            jax.ShapeDtypeStruct((total, width), BF16),
            jax.ShapeDtypeStruct((WH, cols, width), BF16),
        ),
        in_specs=[pl.BlockSpec(memory_space=pltpu.SMEM)] + [vmem] * (tiles + 1),
        out_specs=(vmem, vmem),
        scratch_shapes=[pltpu.VMEM((total, width), BF16), pltpu.VMEM((total, width), F32)],
        compiler_params=pltpu.CompilerParams(vmem_limit_bytes=VMEM_LIMIT),
        cost_estimate=pl.CostEstimate(
            flops=2 * total * total * width, bytes_accessed=4_000_000, transcendentals=0
        ),
        name="band_latents",
    )(place, jnp.asarray(band_map(tiles, cols), BF16), *pieces)


def slot_errors(level, tile_counts, rows, weight, target):
    predicted = lax.dot_general(
        rows, weight, (((1,), (1,)), ((), ())), preferred_element_type=F32
    )
    live = jnp.where(level < tile_counts, 1.0, 0.0)
    diff = predicted - target.astype(F32).reshape(predicted.shape)
    return (diff * live).astype(BF16)


def head_halves(k, lats, lat, errors, rows, turned, keep, send):
    turned[k] = lax.dot_general(
        errors, rows, (((0,), (0,)), ((), ())), preferred_element_type=F32
    ).astype(BF16)
    piece = turned.shape[-1] // lats
    for q in range(lats):
        core, x, y = q & 1, (q >> 1) & 1, (q >> 2) & 1
        outer, inner = (x, y) if k == 0 else (y, x)
        start = pl.multiple_of(jnp.bitwise_xor(lat, q) * piece, piece)
        to = send if core else keep
        to[k, outer, inner, 0] = turned[k, :, pl.ds(start, piece)]


def scaled_rows(band, scale, shift, slot, rows):
    for k in range(2):
        rows[k][...] = (band[...].astype(F32) * scale[slot + k] + shift[slot + k]).astype(BF16)


def add_back(lats, errs, gathered, scale, slot, total):
    piece = gathered.shape[-1]
    for l in range(0, lats, 2):
        lanes = slice(l * piece, (l + 2) * piece)
        term = 0.0
        for k in range(2):
            weight = jnp.concatenate([gathered[l, k], gathered[l + 1, k]], axis=1)
            factor = scale[slot + k][:, lanes]
            term = term + jnp.dot(errs[k], weight, preferred_element_type=F32) * factor
        total[:, lanes] += term


def slot_kernel(
    first_slot,
    lats,
    tiles,
    final,
    place,
    counts,
    datasets,
    levels,
    tile_of,
    band,
    scale,
    shift,
    gathered,
    target,
    *refs,
):
    if final:
        before, keep, send, out, total, rows0, rows1, errs, turned, tile_counts = refs
    else:
        keep, send, total, rows0, rows1, errs, turned, tile_counts = refs
    rows = (rows0, rows1)
    step, steps = pl.program_id(0), pl.num_programs(0)
    slot = first_slot + 2 * step

    @pl.when(step == 0)
    def _():
        total[...] = before[...] if final else jnp.zeros_like(total)
        tile = tile_of[...]
        wanted = jnp.zeros_like(tile)
        for t in range(tiles):
            wanted = jnp.where(tile == t, counts[datasets[0, t]], wanted)
        tile_counts[...] = wanted
        scaled_rows(band, scale, shift, slot, rows)

    for k in range(2):
        weight = jnp.concatenate([gathered[l, k] for l in range(lats)], axis=1)
        errs[k] = slot_errors(levels[slot + k], tile_counts[...], rows[k][...], weight, target[k])
    for k in range(2):
        head_halves(k, lats, place[0], errs[k], rows[k][...], turned, keep, send)
    scaled_rows(band, scale, shift, first_slot + 2 * jnp.minimum(step + 1, steps - 1), rows)
    add_back(lats, errs, gathered, scale, slot, total)

    if final:

        @pl.when(step == steps - 1)
        def _():
            cols = out.shape[2]
            for s in range(tiles):
                for r in range(WH):
                    start = (r * tiles + s) * cols
                    out[s, r] = total[start : start + cols, :].astype(BF16)


def slot_group(pair, pairs, lats, place, small, tile_of, band, scale, shift, gathered, targets, before):
    places, width = band.shape
    slots, outs = targets.shape[0], targets.shape[-1]
    tiles = small[1].shape[1]
    piece = width // lats
    smem = pl.BlockSpec(memory_space=pltpu.SMEM)
    halves = jax.ShapeDtypeStruct((2, 2, 2, pairs, outs, piece), BF16)
    half_spec = pl.BlockSpec((2, 2, 2, 1, outs, piece), lambda i: (0, 0, 0, i, 0, 0))
    level_spec = pl.BlockSpec((slots, 1, width), lambda i: (0, 0, 0))
    sum_spec = pl.BlockSpec((places, width), lambda i: (0, 0))
    in_specs = [smem] * 4 + [
        pl.BlockSpec((places, 1), lambda i: (0, 0)),
        sum_spec,
        level_spec,
        level_spec,
        pl.BlockSpec((lats, 2, outs, piece), lambda i: (0, i + pair, 0, 0)),
        pl.BlockSpec((2,) + targets.shape[1:], lambda i: (i + pair, 0, 0, 0)),
    ]
    args = [place, *small, tile_of, band, scale, shift, gathered, targets]
    final = before is not None
    scratch = [
        pltpu.VMEM((places, width), BF16),
        pltpu.VMEM((places, width), BF16),
        pltpu.VMEM((2, places, outs), BF16),
        pltpu.VMEM((2, outs, width), BF16),
        pltpu.VMEM((places, 1), jnp.int32),
    ]
    sums = jax.ShapeDtypeStruct((places, width), F32)
    if final:
        in_specs.append(sum_spec)
        args.append(before)
        scratch.insert(0, pltpu.VMEM(sums.shape, F32))
        sums = jax.ShapeDtypeStruct((tiles, WH, places // (WH * tiles), width), BF16)
    return pl.pallas_call(
        functools.partial(slot_kernel, 2 * pair, lats, tiles, final),
        grid=(pairs,),
        out_shape=(halves, halves, sums),
        in_specs=in_specs,
        out_specs=(half_spec, half_spec, pl.BlockSpec(sums.shape, lambda i: (0,) * len(sums.shape))),
        scratch_shapes=scratch,
        compiler_params=pltpu.CompilerParams(vmem_limit_bytes=VMEM_LIMIT),
        cost_estimate=pl.CostEstimate(
            flops=pairs * 12 * places * width * outs, bytes_accessed=pairs * 5_000_000, transcendentals=0
        ),
        name="slot_group",
    )(*args)


def join_kernel(norm, *refs):
    out = refs[-1]
    pairs = refs[:-1]
    slot = 0
    for i in range(0, len(pairs), 4):
        for k in range(pairs[i].shape[0]):
            for kept, came in (pairs[i : i + 2], pairs[i + 2 : i + 4]):
                out[slot] = (kept[k].astype(F32) + came[k].astype(F32)) * norm
                slot += 1


def join_heads(pairs, norm):
    flat = [array for pair in pairs for array in pair]
    slots = sum(kept.shape[0] for kept, _ in pairs)
    _, outs, piece = flat[0].shape
    vmem = pl.BlockSpec(memory_space=pltpu.VMEM)
    return pl.pallas_call(
        functools.partial(join_kernel, norm),
        out_shape=jax.ShapeDtypeStruct((slots, outs, piece), F32),
        in_specs=[vmem] * len(flat),
        out_specs=vmem,
        compiler_params=pltpu.CompilerParams(vmem_limit_bytes=VMEM_LIMIT),
        cost_estimate=pl.CostEstimate(flops=1_000_000, bytes_accessed=4_000_000, transcendentals=0),
        name="join_heads",
    )(*flat)


def fast_local(
    patches, norm_gain, input_proj, output_proj, level_scale, level_shift, head_weight, targets,
    level_counts, tile_dataset, slot_level,
):
    rows, cols, width = patches.shape
    lats, tiles = lax.axis_size("lat"), lax.axis_size("var")
    slots = head_weight.shape[0]
    lat, var = lax.axis_index("lat"), lax.axis_index("var")
    place = jnp.stack([lat, var]).astype(jnp.int32)
    gathered = lax.all_gather(jnp.transpose(head_weight, (0, 2, 1)), "lat", axis=0, tiled=False)

    right = [(i, (i + 1) % tiles) for i in range(tiles)]
    up = [(i, i + 1) for i in range(lats - 1)]
    down = [(i + 1, i) for i in range(lats - 1)]
    both = lambda pairs: [(a * tiles + c, b * tiles + d) for a, b in pairs for c, d in right]
    low, high = patches[HR:], patches[:HR]
    above = lax.ppermute(low, "lat", up)
    below = lax.ppermute(high, "lat", down)
    left = lax.ppermute(patches[:, cols - HC :], "var", right)
    above_left = lax.ppermute(low[:, cols - HC :], ("lat", "var"), both(up))
    below_left = lax.ppermute(high[:, cols - HC :], ("lat", "var"), both(down))
    mine = attention(
        place, patches, (left, above, above_left, below, below_left), norm_gain, input_proj, output_proj, lats
    )
    pieces = [mine]
    for s in range(1, tiles):
        pieces.append(lax.ppermute(mine, "var", [(i, (i + s) % tiles) for i in range(tiles)]))
    band, latent = band_latents(place, pieces, cols)

    tile_of = jnp.asarray(np.arange(rows * tiles * cols)[:, None] % (tiles * cols) // cols, jnp.int32)
    scale3, shift3 = level_scale.reshape(slots, 1, width), level_shift.reshape(slots, 1, width)
    small = (level_counts, tile_dataset, slot_level)
    flip = lambda array, bit: lax.ppermute(array, "lat", [(i, i ^ bit) for i in range(lats)])
    add = lambda a, b: (a.astype(F32) + b.astype(F32)).astype(BF16)
    common = (lats, place, small, tile_of, band, scale3, shift3, gathered, targets)
    most = slots // 4 + 1
    rest = slots // 2 - most
    bits = (2, 4)

    def halve(keep, send):
        came = flip(send, 1)
        return (
            [add(keep[k, 0], came[k, 0]) for k in range(2)],
            [add(keep[k, 1], came[k, 1]) for k in range(2)],
        )

    keep_a, send_a, so_far = slot_group(0, most, *common, None)
    keep_b, send_b, terms = slot_group(most, rest, *common, so_far)
    kept_a, sent_a = halve(keep_a, send_a)
    kept_b, sent_b = halve(keep_b, send_b)
    grad_latent = lax.psum_scatter(terms, "var", scatter_dimension=0, tiled=False)
    pairs = []
    for kept, sent in ((kept_a, sent_a), (kept_b, sent_b)):
        came = [flip(sent[k], bits[k]) for k in range(2)]
        for k in range(2):
            last = flip(add(kept[k][1], came[k][1]), bits[1 - k])
            pairs.append((add(kept[k][0], came[k][0]), last))
    grad_head = join_heads(pairs, 1.0 / math.sqrt(lats * rows * tiles * cols))
    return (latent, grad_latent, jnp.transpose(grad_head, (0, 2, 1)))


def padded(array, sides, width, wrap):
    for axis, dim in sides:
        size, length = (lax.axis_size(axis), array.shape[dim])
        up = [(i, (i + 1) % size) for i in range(size if wrap else size - 1)]
        down = [(j, i) for i, j in up]
        last = lax.slice_in_dim(array, length - width, length, axis=dim)
        initial = lax.slice_in_dim(array, 0, width, axis=dim)
        before = lax.ppermute(last, axis, up)
        after = lax.ppermute(initial, axis, down)
        array = jnp.concatenate([before, array, after], axis=dim)
    return array


def layer_norm(values, gain):
    wide = values.astype(jnp.float32)
    average = jnp.mean(wide, axis=-1, keepdims=True)
    centred = wide - average
    variance = jnp.mean(centred * centred, axis=-1, keepdims=True)
    return (centred * lax.rsqrt(variance + EPS) * gain).astype(jnp.bfloat16)


def window_attention(query_ext, keyval, row_valid, heads):
    ext_rows, ext_cols, width = query_ext.shape
    head_size = width // heads
    win_rows = ext_rows // WH
    win_cols = ext_cols // WW

    def split(values, parts):
        shaped = values.reshape(win_rows, WH, win_cols, WW, parts, heads, head_size)
        return shaped.transpose(0, 2, 1, 3, 4, 5, 6).reshape(
            win_rows * win_cols, WH * WW, parts, heads, head_size
        )

    query_win = split(query_ext, 1)[:, :, 0]
    pairs = split(keyval, 2)
    key_win = pairs[:, :, 0]
    value_win = pairs[:, :, 1]
    key_mask = jnp.broadcast_to(
        row_valid.reshape(win_rows, 1, WH, 1), (win_rows, win_cols, WH, WW)
    ).reshape(win_rows * win_cols, WH * WW)
    scores = jnp.einsum(
        "wqhd,wkhd->whqk", query_win, key_win, preferred_element_type=jnp.float32
    ) / math.sqrt(head_size)
    scores = jnp.where(key_mask[:, None, None, :], scores, -jnp.inf)
    peak = jnp.max(scores, axis=-1, keepdims=True)
    weights = jnp.exp(scores - peak)
    probs = (weights / jnp.sum(weights, axis=-1, keepdims=True)).astype(jnp.bfloat16)
    mixed = jnp.einsum("whqk,wkhd->wqhd", probs, value_win, preferred_element_type=jnp.float32)
    return (
        mixed.reshape(win_rows, win_cols, WH, WW, width)
        .transpose(0, 2, 1, 3, 4)
        .reshape(ext_rows, ext_cols, width)
    )


def slot_terms(piece, target_rows, live_cols, level_scale, level_shift, heads_full):
    piece_wide = piece.astype(jnp.float32)
    rows = (
        piece_wide[None] * level_scale[:, None, None, :] + level_shift[:, None, None, :]
    ).astype(jnp.bfloat16)
    predicted = jnp.einsum("krnd,kdo->krno", rows, heads_full, preferred_element_type=jnp.float32)
    errors = ((predicted - target_rows.astype(jnp.float32)) * live_cols[:, None, :, None]).astype(
        jnp.bfloat16
    )
    back_grad = jnp.einsum("krno,kdo->krnd", errors, heads_full, preferred_element_type=jnp.float32)
    piece_grad = jnp.sum(back_grad * level_scale[:, None, None, :], axis=0)
    head_add = jnp.einsum("krnd,krno->dko", rows, errors, preferred_element_type=jnp.float32)
    return (piece_grad, head_add)


def local(
    patches,
    norm_gain,
    input_proj,
    output_proj,
    level_scale,
    level_shift,
    head_weight,
    targets,
    level_counts,
    tile_dataset,
    slot_level,
):
    band_rows, band_cols, width = patches.shape
    half_rows = WH // 2
    half_cols = WW // 2
    lat_count = lax.axis_size("lat")
    var_count = lax.axis_size("var")
    lat_place = lax.axis_index("lat")
    ext_rows = band_rows + WH
    ext_cols = band_cols + WW
    extended = padded(patches, (("lat", 0),), half_rows, False)
    extended = padded(extended, (("var", 1),), half_cols, True)
    normed_ext = layer_norm(extended, norm_gain)
    keyval = jnp.dot(
        normed_ext.reshape(-1, width), input_proj[:, width:], preferred_element_type=jnp.float32
    )
    keyval = keyval.astype(jnp.bfloat16).reshape(ext_rows, ext_cols, 2 * width)
    normed = normed_ext[half_rows : half_rows + band_rows, half_cols : half_cols + band_cols]
    queries = jnp.dot(
        normed.reshape(-1, width), input_proj[:, :width], preferred_element_type=jnp.float32
    )
    queries = queries.astype(jnp.bfloat16).reshape(band_rows, band_cols, width)
    query_ext = jnp.pad(queries, ((half_rows, WH - half_rows), (half_cols, WW - half_cols), (0, 0)))
    global_row = lat_place * band_rows - half_rows + jnp.arange(ext_rows, dtype=jnp.int32)
    row_valid = (global_row >= 0) & (global_row < lat_count * band_rows)
    mixed = window_attention(query_ext, keyval, row_valid, HEADS)
    attn = mixed[half_rows : half_rows + band_rows, half_cols : half_cols + band_cols].astype(
        jnp.bfloat16
    )
    update = jnp.dot(
        attn.reshape(-1, width), output_proj, preferred_element_type=jnp.float32
    ).reshape(band_rows, band_cols, width)
    latent = (patches.astype(jnp.float32) + update).astype(jnp.bfloat16)
    dataset_row = tile_dataset[0]
    dataset_ids = jnp.arange(level_counts.shape[0], dtype=jnp.int32)
    tile_levels = jnp.sum(
        jnp.where(dataset_row[:, None] == dataset_ids[None, :], level_counts[None, :], 0), axis=1
    )
    live_tiles = (slot_level[None, :] < tile_levels[:, None]).astype(jnp.float32)
    heads_full = lax.all_gather(head_weight, "lat", axis=1, tiled=True)
    tile_ids = jnp.arange(var_count, dtype=jnp.int32)
    piece = lax.all_gather(latent, "var", axis=1, tiled=True)
    piece_cols = piece.shape[1]
    column_tile = jnp.arange(piece_cols, dtype=jnp.int32) // band_cols
    onehot = (column_tile[:, None] == tile_ids[None, :]).astype(jnp.float32)
    column_live = jnp.dot(onehot, live_tiles)
    piece_grad, head_add = slot_terms(
        piece, targets, column_live.T, level_scale, level_shift, heads_full
    )
    latent_terms = piece_grad
    latent_terms, head_terms = (latent_terms, head_add)
    grad_latent = lax.psum_scatter(
        latent_terms.astype(jnp.bfloat16), "var", scatter_dimension=1, tiled=True
    )
    head_terms = head_terms * (1.0 / math.sqrt(lat_count * band_rows * var_count * band_cols))
    mine = lax.psum_scatter(
        head_terms.astype(jnp.bfloat16), "lat", scatter_dimension=0, tiled=True
    ).astype(jnp.float32)
    grad_head = jnp.transpose(mine, (1, 0, 2))
    return (latent, grad_latent, grad_head)


def solution(mesh):
    in_specs = (
        P("lat", "var", None),
        P(),
        P(),
        P(),
        P("var", None),
        P("var", None),
        P("var", "lat", None),
        P("var", "lat", None, None),
        P(),
        P("lat", None),
        P("var"),
    )
    fast = mesh.shape["lat"] == 8 and mesh.shape["var"] == 4
    body = fast_local if fast else local
    out_specs = (P("lat", "var", None), P("lat", "var", None), P("var", "lat", None))
    return jax.shard_map(body, mesh=mesh, in_specs=in_specs, out_specs=out_specs, check_vma=False)
```

```python
import functools
import math

import jax
import jax.numpy as jnp
import numpy as np
from jax import lax
from jax.experimental import pallas as pl
from jax.experimental.pallas import tpu as pltpu
from jax.sharding import PartitionSpec as P

HEADS = 16
WH = 6
WW = 12
EPS = 1e-05
HR = WH // 2
HC = WW // 2
QP = 48
LEFT = 8
VMEM_LIMIT = 48 * 1024 * 1024
F32 = jnp.float32
BF16 = jnp.bfloat16


def source_base(cols):
    own = 0
    left = own + WH * cols
    above = left + WH * LEFT
    above_left = above + HR * cols
    below = above_left + HR * LEFT
    below_left = below + HR * cols
    total = below_left + HR * LEFT
    return own, left, above, above_left, below, below_left, total


def gather_maps(cols):
    own, left, above, above_left, below, below_left, total = source_base(cols)
    win_cols = cols // WW
    windows = 2 * win_cols

    def source(part, win_row, row, col):
        if part == 0:
            r = win_row * HR + row
            return left + r * LEFT + col if col < HC else own + r * cols + col - HC
        if win_row == 0:
            return above_left + row * LEFT + col if col < HC else above + row * cols + col - HC
        return below_left + row * LEFT + col if col < HC else below + row * cols + col - HC

    into = np.zeros((windows * 2 * QP, total), np.float32)
    keep = np.zeros((WH * cols, total), np.float32)
    back = np.zeros((WH * cols, windows * QP), np.float32)
    for win in range(windows):
        win_row, win_col = divmod(win, win_cols)
        for part in range(2):
            for row in range(HR):
                for c in range(WW):
                    at = source(part, win_row, row, win_col * WW + c)
                    slot = row * WW + c
                    into[win * 2 * QP + part * QP + slot, at] = 1
                    if part == 0:
                        natural = (win_row * HR + row) * cols + win_col * WW + c
                        keep[natural, at] = 1
                        back[natural, win * QP + slot] = 1
    return into, keep, back


def attention_kernel(
    bands,
    place,
    left,
    above,
    above_left,
    below,
    below_left,
    own_hbm,
    gain,
    maps_hbm,
    in_hbm,
    out_hbm,
    out,
    raw,
    qkv,
    attn,
    own,
    maps,
    proj_in,
    proj_out,
    sems,
):
    moves = [
        pltpu.make_async_copy(src, dst, sems.at[i])
        for i, (src, dst) in enumerate(
            ((own_hbm, own), (maps_hbm, maps), (in_hbm, proj_in), (out_hbm, proj_out))
        )
    ]
    for move in moves:
        move.start()
    cols, width = own.shape[1], own.shape[2]
    bases = source_base(cols)
    total = bases[-1]
    win_cols = cols // WW
    windows = 2 * win_cols
    slots = windows * 2 * QP
    head_size = width // HEADS
    quad = 256 // head_size
    for base, ref in zip(bases, (own, left, above, above_left, below, below_left)):
        count = ref.shape[0]
        if ref is own:
            moves[0].wait()
        if ref.shape[1] == cols:
            raw[base : base + count * cols, :] = ref[...].astype(F32).reshape(count * cols, width)
        else:
            for r in range(count):
                raw[base + r * LEFT : base + (r + 1) * LEFT, :] = jnp.zeros((LEFT, width), F32)
                raw[base + r * LEFT : base + r * LEFT + HC, :] = ref[r].astype(F32)
    wide = raw[...]
    average = jnp.mean(wide, axis=-1, keepdims=True)
    centred = wide - average
    variance = jnp.mean(centred * centred, axis=-1, keepdims=True)
    normed = (centred * lax.rsqrt(variance + EPS) * gain[...]).astype(BF16)
    moves[1].wait()
    win_x = jnp.dot(maps[0:slots, :], normed, preferred_element_type=F32).astype(BF16)
    moves[2].wait()
    step = 512
    for j in range(3 * width // step):
        part = slice(j * step, (j + 1) * step)
        qkv[:, part] = jnp.dot(win_x, proj_in[:, part], preferred_element_type=F32).astype(BF16)
    lane = lax.broadcasted_iota(jnp.int32, (1, 256), 1) // head_size
    heads = [jnp.where(lane == h, 1.0, 0.0) for h in range(quad)]
    key_id = lax.broadcasted_iota(jnp.int32, (1, 2 * QP), 1)
    scale = 1.0 / math.sqrt(head_size)
    for win in range(windows):
        win_row = win // win_cols
        edge = 0 if win_row == 0 else bands - 1
        has_halo = place[0] != edge
        halo_keys = jnp.logical_and(key_id >= QP, key_id < QP + HR * WW)
        valid = jnp.logical_or(key_id < HR * WW, jnp.logical_and(halo_keys, has_halo))
        bias = jnp.where(valid, 0.0, -1e30)
        row0 = win * 2 * QP
        for g in range(width // 256):
            lanes = slice(g * 256, (g + 1) * 256)
            query = qkv[row0 : row0 + QP, lanes].astype(F32) * scale
            stacked = jnp.concatenate([query * h for h in heads], axis=0).astype(BF16)
            key = qkv[row0 : row0 + 2 * QP, width + g * 256 : width + (g + 1) * 256]
            value = qkv[row0 : row0 + 2 * QP, 2 * width + g * 256 : 2 * width + (g + 1) * 256]
            scores = (
                lax.dot_general(
                    stacked, key, (((1,), (1,)), ((), ())), preferred_element_type=F32
                )
                + bias
            )
            weights = jnp.exp(scores - jnp.max(scores, axis=-1, keepdims=True))
            probs = (weights / jnp.sum(weights, axis=-1, keepdims=True)).astype(BF16)
            mixed = jnp.dot(probs, value, preferred_element_type=F32)
            chosen = mixed[0:QP] * heads[0]
            for h in range(1, quad):
                chosen = chosen + mixed[h * QP : (h + 1) * QP] * heads[h]
            attn[win * QP : (win + 1) * QP, lanes] = chosen.astype(BF16)
    size = WH * cols
    keep = maps[slots : slots + size, :]
    back = maps[slots + size : slots + 2 * size, 0 : windows * QP]
    ordered = jnp.dot(back, attn[...], preferred_element_type=F32).astype(BF16)
    residual = jnp.dot(keep, raw[...].astype(BF16), preferred_element_type=F32)
    moves[3].wait()
    update = jnp.dot(ordered, proj_out[...], preferred_element_type=F32)
    out[...] = (residual + update).astype(BF16)


def attention(place, patches, pieces, gain, proj_in, proj_out, bands):
    rows, cols, width = patches.shape
    into, keep, back = gather_maps(cols)
    total = source_base(cols)[-1]
    windows = 2 * (cols // WW)
    back = np.pad(back, ((0, 0), (0, total - back.shape[1])))
    maps = np.concatenate([into, keep, back])
    vmem = pl.BlockSpec(memory_space=pltpu.VMEM)
    hbm = pl.BlockSpec(memory_space=pltpu.HBM)
    return pl.pallas_call(
        functools.partial(attention_kernel, bands),
        out_shape=jax.ShapeDtypeStruct((rows * cols, width), BF16),
        in_specs=[pl.BlockSpec(memory_space=pltpu.SMEM)] + [vmem] * 5 + [hbm, vmem, hbm, hbm, hbm],
        out_specs=vmem,
        scratch_shapes=[
            pltpu.VMEM((total, width), F32),
            pltpu.VMEM((windows * 2 * QP, 3 * width), BF16),
            pltpu.VMEM((windows * QP, width), BF16),
            pltpu.VMEM(patches.shape, BF16),
            pltpu.VMEM(maps.shape, BF16),
            pltpu.VMEM(proj_in.shape, BF16),
            pltpu.VMEM(proj_out.shape, BF16),
            pltpu.SemaphoreType.DMA((4,)),
        ],
        compiler_params=pltpu.CompilerParams(vmem_limit_bytes=53 * 1024 * 1024),
        cost_estimate=pl.CostEstimate(
            flops=6_000_000_000, bytes_accessed=12_000_000, transcendentals=400_000
        ),
        name="window_attention",
    )(
        place,
        *pieces,
        patches,
        gain.reshape(1, width),
        jnp.asarray(maps, BF16),
        proj_in,
        proj_out,
    )


def band_map(tiles, cols):
    wide = tiles * cols
    chosen = np.zeros((WH * wide, WH * wide), np.float32)
    for r in range(WH):
        for c in range(wide):
            tile, at = divmod((c + HC) % wide, cols)
            chosen[r * wide + c, tile * WH * cols + r * cols + at] = 1
    return chosen


def band_kernel(tiles, cols, place, chosen, *refs):
    pieces, (band, latent, laid, wide) = refs[:tiles], refs[tiles:]
    size = WH * cols
    var = place[1]
    for s in range(tiles):
        tile = lax.rem(var + tiles - s, tiles)
        laid[pl.ds(pl.multiple_of(tile * size, 16), size), :] = pieces[s][...]
    wide[...] = jnp.dot(chosen[...], laid[...], preferred_element_type=F32)
    band[...] = wide[...].astype(BF16)
    for r in range(WH):
        start = pl.multiple_of(r * tiles * cols + var * cols, 8)
        latent[r] = wide[pl.ds(start, cols), :].astype(BF16)


def band_latents(place, pieces, cols):
    tiles = len(pieces)
    width = pieces[0].shape[1]
    total = WH * tiles * cols
    vmem = pl.BlockSpec(memory_space=pltpu.VMEM)
    return pl.pallas_call(
        functools.partial(band_kernel, tiles, cols),
        out_shape=(
            jax.ShapeDtypeStruct((total, width), BF16),
            jax.ShapeDtypeStruct((WH, cols, width), BF16),
        ),
        in_specs=[pl.BlockSpec(memory_space=pltpu.SMEM)] + [vmem] * (tiles + 1),
        out_specs=(vmem, vmem),
        scratch_shapes=[pltpu.VMEM((total, width), BF16), pltpu.VMEM((total, width), F32)],
        compiler_params=pltpu.CompilerParams(vmem_limit_bytes=VMEM_LIMIT),
        cost_estimate=pl.CostEstimate(
            flops=2 * total * total * width, bytes_accessed=4_000_000, transcendentals=0
        ),
        name="band_latents",
    )(place, jnp.asarray(band_map(tiles, cols), BF16), *pieces)


def slot_errors(level, tile_counts, rows, weight, target):
    predicted = lax.dot_general(
        rows, weight, (((1,), (1,)), ((), ())), preferred_element_type=F32
    )
    live = jnp.where(level < tile_counts, 1.0, 0.0)
    diff = predicted - target.astype(F32).reshape(predicted.shape)
    return (diff * live).astype(BF16)


def head_halves(k, lats, lat, errors, rows, turned, keep, send):
    turned[k] = lax.dot_general(
        errors, rows, (((0,), (0,)), ((), ())), preferred_element_type=F32
    ).astype(BF16)
    piece = turned.shape[-1] // lats
    for q in range(lats):
        core, x, y = q & 1, (q >> 1) & 1, (q >> 2) & 1
        outer, inner = (x, y) if k == 0 else (y, x)
        start = pl.multiple_of(jnp.bitwise_xor(lat, q) * piece, piece)
        to = send if core else keep
        to[k, outer, inner, 0] = turned[k, :, pl.ds(start, piece)]


def add_back(lats, errs, gathered, scale, total):
    piece = gathered.shape[-1]
    for l in range(0, lats, 2):
        lanes = slice(l * piece, (l + 2) * piece)
        term = 0.0
        for k in range(2):
            weight = jnp.concatenate([gathered[l, k], gathered[l + 1, k]], axis=1)
            factor = scale[k][:, lanes]
            term = term + jnp.dot(errs[k], weight, preferred_element_type=F32) * factor
        total[:, lanes] += term


def slot_kernel(
    first_slot,
    lats,
    tiles,
    final,
    place,
    counts,
    datasets,
    levels,
    tile_of,
    band,
    scale,
    shift,
    gathered,
    target,
    *refs,
):
    if final:
        before, keep, send, out, total, rows0, rows1, errs, turned, tile_counts = refs
    else:
        keep, send, total, rows0, rows1, errs, turned, tile_counts = refs
    rows = (rows0, rows1)
    step, steps = pl.program_id(0), pl.num_programs(0)
    slot = first_slot + 2 * step

    @pl.when(step == 0)
    def _():
        total[...] = before[...] if final else jnp.zeros_like(total)
        tile = tile_of[...]
        wanted = jnp.zeros_like(tile)
        for t in range(tiles):
            wanted = jnp.where(tile == t, counts[datasets[0, t]], wanted)
        tile_counts[...] = wanted

    for k in range(2):
        rows[k][...] = (band[...].astype(F32) * scale[k] + shift[k]).astype(BF16)
    for k in range(2):
        weight = jnp.concatenate([gathered[l, k] for l in range(lats)], axis=1)
        errs[k] = slot_errors(levels[slot + k], tile_counts[...], rows[k][...], weight, target[k])
    for k in range(2):
        head_halves(k, lats, place[0], errs[k], rows[k][...], turned, keep, send)
    add_back(lats, errs, gathered, scale, total)

    if final:

        @pl.when(step == steps - 1)
        def _():
            cols = out.shape[2]
            for s in range(tiles):
                for r in range(WH):
                    start = (r * tiles + s) * cols
                    out[s, r] = total[start : start + cols, :].astype(BF16)


def slot_group(pair, pairs, lats, place, small, tile_of, band, scale, shift, gathered, targets, before):
    places, width = band.shape
    outs = targets.shape[-1]
    tiles = small[1].shape[1]
    piece = width // lats
    smem = pl.BlockSpec(memory_space=pltpu.SMEM)
    halves = jax.ShapeDtypeStruct((2, 2, 2, pairs, outs, piece), BF16)
    half_spec = pl.BlockSpec((2, 2, 2, 1, outs, piece), lambda i: (0, 0, 0, i, 0, 0))
    level_spec = pl.BlockSpec((2, 1, width), lambda i: (i + pair, 0, 0))
    sum_spec = pl.BlockSpec((places, width), lambda i: (0, 0))
    in_specs = [smem] * 4 + [
        pl.BlockSpec((places, 1), lambda i: (0, 0)),
        sum_spec,
        level_spec,
        level_spec,
        pl.BlockSpec((lats, 2, outs, piece), lambda i: (0, i + pair, 0, 0)),
        pl.BlockSpec((2,) + targets.shape[1:], lambda i: (i + pair, 0, 0, 0)),
    ]
    args = [place, *small, tile_of, band, scale, shift, gathered, targets]
    final = before is not None
    scratch = [
        pltpu.VMEM((places, width), BF16),
        pltpu.VMEM((places, width), BF16),
        pltpu.VMEM((2, places, outs), BF16),
        pltpu.VMEM((2, outs, width), BF16),
        pltpu.VMEM((places, 1), jnp.int32),
    ]
    sums = jax.ShapeDtypeStruct((places, width), F32)
    if final:
        in_specs.append(sum_spec)
        args.append(before)
        scratch.insert(0, pltpu.VMEM(sums.shape, F32))
        sums = jax.ShapeDtypeStruct((tiles, WH, places // (WH * tiles), width), BF16)
    return pl.pallas_call(
        functools.partial(slot_kernel, 2 * pair, lats, tiles, final),
        grid=(pairs,),
        out_shape=(halves, halves, sums),
        in_specs=in_specs,
        out_specs=(half_spec, half_spec, pl.BlockSpec(sums.shape, lambda i: (0,) * len(sums.shape))),
        scratch_shapes=scratch,
        compiler_params=pltpu.CompilerParams(vmem_limit_bytes=45 * 1024 * 1024),
        cost_estimate=pl.CostEstimate(
            flops=pairs * 12 * places * width * outs, bytes_accessed=pairs * 5_000_000, transcendentals=0
        ),
        name="slot_group",
    )(*args)


def halve_kernel(keep, came, *refs):
    outs = refs[-4:]
    for k in range(2):
        for half in range(2):
            total = keep[k, half].astype(F32) + came[k, half].astype(F32)
            outs[2 * half + k][...] = total.astype(BF16)


def halve(keep, came, after):
    part = jax.ShapeDtypeStruct(keep.shape[2:], BF16)
    vmem = pl.BlockSpec(memory_space=pltpu.VMEM)
    out = pl.pallas_call(
        halve_kernel,
        out_shape=(part,) * 4,
        in_specs=[vmem, vmem] + [pl.BlockSpec(memory_space=pl.ANY)] * len(after),
        out_specs=(vmem,) * 4,
        compiler_params=pltpu.CompilerParams(vmem_limit_bytes=24 * 1024 * 1024),
        cost_estimate=pl.CostEstimate(flops=2_000_000, bytes_accessed=6_000_000, transcendentals=0),
        name="halve",
    )(keep, came, *after)
    return out[0:2], out[2:4]


def join_kernel(norm, *refs):
    out = refs[-1]
    pairs = refs[:-1]
    slot = 0
    for i in range(0, len(pairs), 4):
        for k in range(pairs[i].shape[0]):
            for kept, came in (pairs[i : i + 2], pairs[i + 2 : i + 4]):
                out[slot] = (kept[k].astype(F32) + came[k].astype(F32)) * norm
                slot += 1


def join_heads(pairs, norm):
    flat = [array for pair in pairs for array in pair]
    slots = sum(kept.shape[0] for kept, _ in pairs)
    _, outs, piece = flat[0].shape
    vmem = pl.BlockSpec(memory_space=pltpu.VMEM)
    return pl.pallas_call(
        functools.partial(join_kernel, norm),
        out_shape=jax.ShapeDtypeStruct((slots, outs, piece), F32),
        in_specs=[vmem] * len(flat),
        out_specs=vmem,
        compiler_params=pltpu.CompilerParams(vmem_limit_bytes=VMEM_LIMIT),
        cost_estimate=pl.CostEstimate(flops=1_000_000, bytes_accessed=4_000_000, transcendentals=0),
        name="join_heads",
    )(*flat)


def fast_local(
    patches, norm_gain, input_proj, output_proj, level_scale, level_shift, head_weight, targets,
    level_counts, tile_dataset, slot_level,
):
    rows, cols, width = patches.shape
    lats, tiles = lax.axis_size("lat"), lax.axis_size("var")
    slots = head_weight.shape[0]
    lat, var = lax.axis_index("lat"), lax.axis_index("var")
    place = jnp.stack([lat, var]).astype(jnp.int32)
    gathered = lax.all_gather(jnp.transpose(head_weight, (0, 2, 1)), "lat", axis=0, tiled=False)

    right = [(i, (i + 1) % tiles) for i in range(tiles)]
    up = [(i, i + 1) for i in range(lats - 1)]
    down = [(i + 1, i) for i in range(lats - 1)]
    both = lambda pairs: [(a * tiles + c, b * tiles + d) for a, b in pairs for c, d in right]
    low, high = patches[HR:], patches[:HR]
    above = lax.ppermute(low, "lat", up)
    below = lax.ppermute(high, "lat", down)
    left = lax.ppermute(patches[:, cols - HC :], "var", right)
    above_left = lax.ppermute(low[:, cols - HC :], ("lat", "var"), both(up))
    below_left = lax.ppermute(high[:, cols - HC :], ("lat", "var"), both(down))
    mine = attention(
        place, patches, (left, above, above_left, below, below_left), norm_gain, input_proj, output_proj, lats
    )
    pieces = [mine]
    for s in range(1, tiles):
        pieces.append(lax.ppermute(mine, "var", [(i, (i + s) % tiles) for i in range(tiles)]))
    band, latent = band_latents(place, pieces, cols)

    tile_of = jnp.asarray(np.arange(rows * tiles * cols)[:, None] % (tiles * cols) // cols, jnp.int32)
    scale3, shift3 = level_scale.reshape(slots, 1, width), level_shift.reshape(slots, 1, width)
    small = (level_counts, tile_dataset, slot_level)
    flip = lambda array, bit: lax.ppermute(array, "lat", [(i, i ^ bit) for i in range(lats)])
    add = lambda a, b: (a.astype(F32) + b.astype(F32)).astype(BF16)
    common = (lats, place, small, tile_of, band, scale3, shift3, gathered, targets)
    most = slots // 2 - 1
    bits = (2, 4)
    keep_a, send_a, so_far = slot_group(0, most, *common, None)
    keep_b, send_b, terms = slot_group(most, slots // 2 - most, *common, so_far)
    grad_latent = lax.psum_scatter(terms, "var", scatter_dimension=0, tiled=False)
    pairs, came = [], [terms]
    for keep, send in ((keep_a, send_a), (keep_b, send_b)):
        kept, sent = halve(keep, flip(send, 1), came)
        came = [flip(sent[k], bits[k]) for k in range(2)]
        for k in range(2):
            last = flip(add(kept[k][1], came[k][1]), bits[1 - k])
            pairs.append((add(kept[k][0], came[k][0]), last))
    grad_head = join_heads(pairs, 1.0 / math.sqrt(lats * rows * tiles * cols))
    return (latent, grad_latent, jnp.transpose(grad_head, (0, 2, 1)))


def padded(array, sides, width, wrap):
    for axis, dim in sides:
        size, length = (lax.axis_size(axis), array.shape[dim])
        up = [(i, (i + 1) % size) for i in range(size if wrap else size - 1)]
        down = [(j, i) for i, j in up]
        last = lax.slice_in_dim(array, length - width, length, axis=dim)
        initial = lax.slice_in_dim(array, 0, width, axis=dim)
        before = lax.ppermute(last, axis, up)
        after = lax.ppermute(initial, axis, down)
        array = jnp.concatenate([before, array, after], axis=dim)
    return array


def layer_norm(values, gain):
    wide = values.astype(jnp.float32)
    average = jnp.mean(wide, axis=-1, keepdims=True)
    centred = wide - average
    variance = jnp.mean(centred * centred, axis=-1, keepdims=True)
    return (centred * lax.rsqrt(variance + EPS) * gain).astype(jnp.bfloat16)


def window_attention(query_ext, keyval, row_valid, heads):
    ext_rows, ext_cols, width = query_ext.shape
    head_size = width // heads
    win_rows = ext_rows // WH
    win_cols = ext_cols // WW

    def split(values, parts):
        shaped = values.reshape(win_rows, WH, win_cols, WW, parts, heads, head_size)
        return shaped.transpose(0, 2, 1, 3, 4, 5, 6).reshape(
            win_rows * win_cols, WH * WW, parts, heads, head_size
        )

    query_win = split(query_ext, 1)[:, :, 0]
    pairs = split(keyval, 2)
    key_win = pairs[:, :, 0]
    value_win = pairs[:, :, 1]
    key_mask = jnp.broadcast_to(
        row_valid.reshape(win_rows, 1, WH, 1), (win_rows, win_cols, WH, WW)
    ).reshape(win_rows * win_cols, WH * WW)
    scores = jnp.einsum(
        "wqhd,wkhd->whqk", query_win, key_win, preferred_element_type=jnp.float32
    ) / math.sqrt(head_size)
    scores = jnp.where(key_mask[:, None, None, :], scores, -jnp.inf)
    peak = jnp.max(scores, axis=-1, keepdims=True)
    weights = jnp.exp(scores - peak)
    probs = (weights / jnp.sum(weights, axis=-1, keepdims=True)).astype(jnp.bfloat16)
    mixed = jnp.einsum("whqk,wkhd->wqhd", probs, value_win, preferred_element_type=jnp.float32)
    return (
        mixed.reshape(win_rows, win_cols, WH, WW, width)
        .transpose(0, 2, 1, 3, 4)
        .reshape(ext_rows, ext_cols, width)
    )


def slot_terms(piece, target_rows, live_cols, level_scale, level_shift, heads_full):
    piece_wide = piece.astype(jnp.float32)
    rows = (
        piece_wide[None] * level_scale[:, None, None, :] + level_shift[:, None, None, :]
    ).astype(jnp.bfloat16)
    predicted = jnp.einsum("krnd,kdo->krno", rows, heads_full, preferred_element_type=jnp.float32)
    errors = ((predicted - target_rows.astype(jnp.float32)) * live_cols[:, None, :, None]).astype(
        jnp.bfloat16
    )
    back_grad = jnp.einsum("krno,kdo->krnd", errors, heads_full, preferred_element_type=jnp.float32)
    piece_grad = jnp.sum(back_grad * level_scale[:, None, None, :], axis=0)
    head_add = jnp.einsum("krnd,krno->dko", rows, errors, preferred_element_type=jnp.float32)
    return (piece_grad, head_add)


def local(
    patches,
    norm_gain,
    input_proj,
    output_proj,
    level_scale,
    level_shift,
    head_weight,
    targets,
    level_counts,
    tile_dataset,
    slot_level,
):
    band_rows, band_cols, width = patches.shape
    half_rows = WH // 2
    half_cols = WW // 2
    lat_count = lax.axis_size("lat")
    var_count = lax.axis_size("var")
    lat_place = lax.axis_index("lat")
    ext_rows = band_rows + WH
    ext_cols = band_cols + WW
    extended = padded(patches, (("lat", 0),), half_rows, False)
    extended = padded(extended, (("var", 1),), half_cols, True)
    normed_ext = layer_norm(extended, norm_gain)
    keyval = jnp.dot(
        normed_ext.reshape(-1, width), input_proj[:, width:], preferred_element_type=jnp.float32
    )
    keyval = keyval.astype(jnp.bfloat16).reshape(ext_rows, ext_cols, 2 * width)
    normed = normed_ext[half_rows : half_rows + band_rows, half_cols : half_cols + band_cols]
    queries = jnp.dot(
        normed.reshape(-1, width), input_proj[:, :width], preferred_element_type=jnp.float32
    )
    queries = queries.astype(jnp.bfloat16).reshape(band_rows, band_cols, width)
    query_ext = jnp.pad(queries, ((half_rows, WH - half_rows), (half_cols, WW - half_cols), (0, 0)))
    global_row = lat_place * band_rows - half_rows + jnp.arange(ext_rows, dtype=jnp.int32)
    row_valid = (global_row >= 0) & (global_row < lat_count * band_rows)
    mixed = window_attention(query_ext, keyval, row_valid, HEADS)
    attn = mixed[half_rows : half_rows + band_rows, half_cols : half_cols + band_cols].astype(
        jnp.bfloat16
    )
    update = jnp.dot(
        attn.reshape(-1, width), output_proj, preferred_element_type=jnp.float32
    ).reshape(band_rows, band_cols, width)
    latent = (patches.astype(jnp.float32) + update).astype(jnp.bfloat16)
    dataset_row = tile_dataset[0]
    dataset_ids = jnp.arange(level_counts.shape[0], dtype=jnp.int32)
    tile_levels = jnp.sum(
        jnp.where(dataset_row[:, None] == dataset_ids[None, :], level_counts[None, :], 0), axis=1
    )
    live_tiles = (slot_level[None, :] < tile_levels[:, None]).astype(jnp.float32)
    heads_full = lax.all_gather(head_weight, "lat", axis=1, tiled=True)
    tile_ids = jnp.arange(var_count, dtype=jnp.int32)
    piece = lax.all_gather(latent, "var", axis=1, tiled=True)
    piece_cols = piece.shape[1]
    column_tile = jnp.arange(piece_cols, dtype=jnp.int32) // band_cols
    onehot = (column_tile[:, None] == tile_ids[None, :]).astype(jnp.float32)
    column_live = jnp.dot(onehot, live_tiles)
    piece_grad, head_add = slot_terms(
        piece, targets, column_live.T, level_scale, level_shift, heads_full
    )
    latent_terms = piece_grad
    latent_terms, head_terms = (latent_terms, head_add)
    grad_latent = lax.psum_scatter(
        latent_terms.astype(jnp.bfloat16), "var", scatter_dimension=1, tiled=True
    )
    head_terms = head_terms * (1.0 / math.sqrt(lat_count * band_rows * var_count * band_cols))
    mine = lax.psum_scatter(
        head_terms.astype(jnp.bfloat16), "lat", scatter_dimension=0, tiled=True
    ).astype(jnp.float32)
    grad_head = jnp.transpose(mine, (1, 0, 2))
    return (latent, grad_latent, grad_head)


def solution(mesh):
    in_specs = (
        P("lat", "var", None),
        P(),
        P(),
        P(),
        P("var", None),
        P("var", None),
        P("var", "lat", None),
        P("var", "lat", None, None),
        P(),
        P("lat", None),
        P("var"),
    )
    fast = mesh.shape["lat"] == 8 and mesh.shape["var"] == 4
    body = fast_local if fast else local
    out_specs = (P("lat", "var", None), P("lat", "var", None), P("var", "lat", None))
    return jax.shard_map(body, mesh=mesh, in_specs=in_specs, out_specs=out_specs, check_vma=False)
```

```python
import functools
import math

import jax
import jax.numpy as jnp
import numpy as np
from jax import lax
from jax.experimental import pallas as pl
from jax.experimental.pallas import tpu as pltpu
from jax.sharding import PartitionSpec as P

HEADS = 16
WH = 6
WW = 12
EPS = 1e-05
HR = WH // 2
HC = WW // 2
QP = 48
VMEM_LIMIT = 48 * 1024 * 1024
F32 = jnp.float32
BF16 = jnp.bfloat16


def gather_maps(cols):
    win_cols = cols // WW
    windows = 2 * win_cols
    into = np.zeros((windows * 2 * QP, 2 * WH * cols), np.float32)
    back = np.zeros((WH * cols, windows * QP), np.float32)
    for win in range(windows):
        win_row, win_col = divmod(win, win_cols)
        for row in range(HR):
            for c in range(WW):
                own = (win_row * HR + row) * cols + win_col * WW + c
                slot = row * WW + c
                into[win * 2 * QP + slot, own] = 1
                into[win * 2 * QP + QP + slot, WH * cols + own] = 1
                back[own, win * QP + slot] = 1
    return into, back


def attention_kernel(
    bands,
    place,
    own,
    above,
    below,
    gain,
    maps_hbm,
    in_hbm,
    out_hbm,
    out,
    raw,
    qkv,
    attn,
    maps,
    proj_in,
    proj_out,
    sems,
):
    moves = [
        pltpu.make_async_copy(src, dst, sems.at[i])
        for i, (src, dst) in enumerate(((maps_hbm, maps), (in_hbm, proj_in), (out_hbm, proj_out)))
    ]
    for move in moves:
        move.start()
    cols, width = own.shape[1], own.shape[2]
    win_cols = cols // WW
    windows = 2 * win_cols
    slots = windows * 2 * QP
    head_size = width // HEADS
    quad = 256 // head_size
    size = WH * cols
    start = 0
    for ref in (own, above, below):
        count = ref.shape[0] * cols
        raw[start : start + count, :] = ref[...].astype(F32).reshape(count, width)
        start += count
    wide = raw[...]
    average = jnp.mean(wide, axis=-1, keepdims=True)
    centred = wide - average
    variance = jnp.mean(centred * centred, axis=-1, keepdims=True)
    normed = (centred * lax.rsqrt(variance + EPS) * gain[...]).astype(BF16)
    moves[0].wait()
    win_x = jnp.dot(maps[0:slots, :], normed, preferred_element_type=F32).astype(BF16)
    moves[1].wait()
    step = 512
    for j in range(3 * width // step):
        part = slice(j * step, (j + 1) * step)
        qkv[:, part] = jnp.dot(win_x, proj_in[:, part], preferred_element_type=F32).astype(BF16)
    lane = lax.broadcasted_iota(jnp.int32, (1, 256), 1) // head_size
    heads = [jnp.where(lane == h, 1.0, 0.0) for h in range(quad)]
    key_id = lax.broadcasted_iota(jnp.int32, (1, 2 * QP), 1)
    scale = 1.0 / math.sqrt(head_size)
    for win in range(windows):
        win_row = win // win_cols
        edge = 0 if win_row == 0 else bands - 1
        has_halo = place[0] != edge
        halo_keys = jnp.logical_and(key_id >= QP, key_id < QP + HR * WW)
        valid = jnp.logical_or(key_id < HR * WW, jnp.logical_and(halo_keys, has_halo))
        bias = jnp.where(valid, 0.0, -1e30)
        row0 = win * 2 * QP
        for g in range(width // 256):
            lanes = slice(g * 256, (g + 1) * 256)
            query = qkv[row0 : row0 + QP, lanes].astype(F32) * scale
            stacked = jnp.concatenate([query * h for h in heads], axis=0).astype(BF16)
            key = qkv[row0 : row0 + 2 * QP, width + g * 256 : width + (g + 1) * 256]
            value = qkv[row0 : row0 + 2 * QP, 2 * width + g * 256 : 2 * width + (g + 1) * 256]
            scores = (
                lax.dot_general(
                    stacked, key, (((1,), (1,)), ((), ())), preferred_element_type=F32
                )
                + bias
            )
            weights = jnp.exp(scores - jnp.max(scores, axis=-1, keepdims=True))
            probs = (weights / jnp.sum(weights, axis=-1, keepdims=True)).astype(BF16)
            mixed = jnp.dot(probs, value, preferred_element_type=F32)
            chosen = mixed[0:QP] * heads[0]
            for h in range(1, quad):
                chosen = chosen + mixed[h * QP : (h + 1) * QP] * heads[h]
            attn[win * QP : (win + 1) * QP, lanes] = chosen.astype(BF16)
    back = maps[slots : slots + size, 0 : windows * QP]
    ordered = jnp.dot(back, attn[...], preferred_element_type=F32).astype(BF16)
    moves[2].wait()
    update = jnp.dot(ordered, proj_out[...], preferred_element_type=F32)
    out[...] = (raw[0:size, :] + update).astype(BF16)


def attention(place, pieces, gain, proj_in, proj_out, bands):
    rows, cols, width = pieces[0].shape
    into, back = gather_maps(cols)
    total = into.shape[1]
    windows = 2 * (cols // WW)
    back = np.pad(back, ((0, 0), (0, total - back.shape[1])))
    maps = np.concatenate([into, back])
    vmem = pl.BlockSpec(memory_space=pltpu.VMEM)
    hbm = pl.BlockSpec(memory_space=pltpu.HBM)
    return pl.pallas_call(
        functools.partial(attention_kernel, bands),
        out_shape=jax.ShapeDtypeStruct((rows * cols, width), BF16),
        in_specs=[pl.BlockSpec(memory_space=pltpu.SMEM)] + [vmem] * 4 + [hbm] * 3,
        out_specs=vmem,
        scratch_shapes=[
            pltpu.VMEM((total, width), F32),
            pltpu.VMEM((windows * 2 * QP, 3 * width), BF16),
            pltpu.VMEM((windows * QP, width), BF16),
            pltpu.VMEM(maps.shape, BF16),
            pltpu.VMEM(proj_in.shape, BF16),
            pltpu.VMEM(proj_out.shape, BF16),
            pltpu.SemaphoreType.DMA((3,)),
        ],
        compiler_params=pltpu.CompilerParams(vmem_limit_bytes=53 * 1024 * 1024),
        cost_estimate=pl.CostEstimate(
            flops=6_000_000_000, bytes_accessed=12_000_000, transcendentals=400_000
        ),
        name="window_attention",
    )(
        place,
        *pieces,
        gain.reshape(1, width),
        jnp.asarray(maps, BF16),
        proj_in,
        proj_out,
    )


def band_map(tiles, cols):
    wide = tiles * cols
    chosen = np.zeros((WH * wide, WH * wide), np.float32)
    for r in range(WH):
        for c in range(wide):
            tile, at = divmod((c + HC) % wide, cols)
            chosen[r * wide + c, tile * WH * cols + r * cols + at] = 1
    return chosen


def order_band(tiles, cols, var, chosen, pieces, laid, wide, band, latent):
    size = WH * cols
    for s in range(tiles):
        tile = lax.rem(var + tiles - s, tiles)
        laid[pl.ds(pl.multiple_of(tile * size, 16), size), :] = pieces[s][...]
    wide[...] = jnp.dot(chosen[...], laid[...], preferred_element_type=F32)
    band[...] = wide[...].astype(BF16)
    for r in range(WH):
        start = pl.multiple_of(r * tiles * cols + var * cols, 8)
        latent[r] = wide[pl.ds(start, cols), :].astype(BF16)


def slot_errors(level, tile_counts, rows, weight, target):
    predicted = lax.dot_general(
        rows, weight, (((1,), (1,)), ((), ())), preferred_element_type=F32
    )
    live = jnp.where(level < tile_counts, 1.0, 0.0)
    diff = predicted - target.astype(F32).reshape(predicted.shape)
    return (diff * live).astype(BF16)


def head_halves(k, lats, lat, errors, rows, turned, keep, send):
    turned[k] = lax.dot_general(
        errors, rows, (((0,), (0,)), ((), ())), preferred_element_type=F32
    ).astype(BF16)
    piece = turned.shape[-1] // lats
    for q in range(lats):
        core, x, y = q & 1, (q >> 1) & 1, (q >> 2) & 1
        outer, inner = (x, y) if k == 0 else (y, x)
        start = pl.multiple_of(jnp.bitwise_xor(lat, q) * piece, piece)
        to = send if core else keep
        to[k, outer, inner, 0] = turned[k, :, pl.ds(start, piece)]


def add_back(lats, errs, gathered, scale, total):
    piece = gathered.shape[-1]
    for l in range(0, lats, 2):
        lanes = slice(l * piece, (l + 2) * piece)
        term = 0.0
        for k in range(2):
            weight = jnp.concatenate([gathered[l, k], gathered[l + 1, k]], axis=1)
            factor = scale[k][:, lanes]
            term = term + jnp.dot(errs[k], weight, preferred_element_type=F32) * factor
        total[:, lanes] += term


def slot_kernel(
    first_slot,
    lats,
    tiles,
    final,
    place,
    counts,
    datasets,
    levels,
    tile_of,
    scale,
    shift,
    gathered,
    target,
    *refs,
):
    if final:
        band, before, keep, send, out, total, rows0, rows1, errs, turned, tile_counts = refs
    else:
        chosen, pieces = refs[0], refs[1 : 1 + tiles]
        keep, send, total, band, latent, rows0, rows1, errs, turned, tile_counts = refs[1 + tiles :]
    rows = (rows0, rows1)
    step, steps = pl.program_id(0), pl.num_programs(0)
    slot = first_slot + 2 * step

    @pl.when(step == 0)
    def _():
        if final:
            total[...] = before[...]
        else:
            order_band(tiles, latent.shape[1], place[1], chosen, pieces, rows0, total, band, latent)
            total[...] = jnp.zeros_like(total)
        tile = tile_of[...]
        wanted = jnp.zeros_like(tile)
        for t in range(tiles):
            wanted = jnp.where(tile == t, counts[datasets[0, t]], wanted)
        tile_counts[...] = wanted

    for k in range(2):
        rows[k][...] = (band[...].astype(F32) * scale[k] + shift[k]).astype(BF16)
    for k in range(2):
        weight = jnp.concatenate([gathered[l, k] for l in range(lats)], axis=1)
        errs[k] = slot_errors(levels[slot + k], tile_counts[...], rows[k][...], weight, target[k])
    for k in range(2):
        head_halves(k, lats, place[0], errs[k], rows[k][...], turned, keep, send)
    add_back(lats, errs, gathered, scale, total)

    if final:

        @pl.when(step == steps - 1)
        def _():
            cols = out.shape[2]
            for s in range(tiles):
                for r in range(WH):
                    start = (r * tiles + s) * cols
                    out[s, r] = total[start : start + cols, :].astype(BF16)


def slot_group(pair, pairs, lats, place, small, tile_of, scale, shift, gathered, targets, pieces, before):
    places, width = tile_of.shape[0], scale.shape[-1]
    outs = targets.shape[-1]
    tiles = small[1].shape[1]
    piece = width // lats
    cols = places // (WH * tiles)
    smem = pl.BlockSpec(memory_space=pltpu.SMEM)
    fixed = lambda shape: pl.BlockSpec(shape, lambda i: (0,) * len(shape))
    halves = jax.ShapeDtypeStruct((2, 2, 2, pairs, outs, piece), BF16)
    half_spec = pl.BlockSpec((2, 2, 2, 1, outs, piece), lambda i: (0, 0, 0, i, 0, 0))
    level_spec = pl.BlockSpec((2, 1, width), lambda i: (i + pair, 0, 0))
    in_specs = [smem] * 4 + [
        fixed(tile_of.shape),
        level_spec,
        level_spec,
        pl.BlockSpec((lats, 2, outs, piece), lambda i: (0, i + pair, 0, 0)),
        pl.BlockSpec((2,) + targets.shape[1:], lambda i: (i + pair, 0, 0, 0)),
    ]
    args = [place, *small, tile_of, scale, shift, gathered, targets]
    final = before is not None
    scratch = [
        pltpu.VMEM((places, width), BF16),
        pltpu.VMEM((places, width), BF16),
        pltpu.VMEM((2, places, outs), BF16),
        pltpu.VMEM((2, outs, width), BF16),
        pltpu.VMEM((places, 1), jnp.int32),
    ]
    sums = jax.ShapeDtypeStruct((places, width), F32)
    if final:
        args.extend(before)
        scratch.insert(0, pltpu.VMEM(sums.shape, F32))
        results = [jax.ShapeDtypeStruct((tiles, WH, cols, width), BF16)]
    else:
        args.extend([jnp.asarray(band_map(tiles, cols), BF16), *pieces])
        results = [
            sums,
            jax.ShapeDtypeStruct((places, width), BF16),
            jax.ShapeDtypeStruct((WH, cols, width), BF16),
        ]
    in_specs.extend(fixed(arg.shape) for arg in args[len(in_specs) :])
    limit = (45 if final else 48) * 1024 * 1024
    return pl.pallas_call(
        functools.partial(slot_kernel, 2 * pair, lats, tiles, final),
        grid=(pairs,),
        out_shape=(halves, halves, *results),
        in_specs=in_specs,
        out_specs=(half_spec, half_spec, *(fixed(r.shape) for r in results)),
        scratch_shapes=scratch,
        compiler_params=pltpu.CompilerParams(vmem_limit_bytes=limit),
        cost_estimate=pl.CostEstimate(
            flops=pairs * 12 * places * width * outs, bytes_accessed=pairs * 5_000_000, transcendentals=0
        ),
        name="slot_group",
    )(*args)


def halve_kernel(keep, came, *refs):
    outs = refs[-4:]
    for k in range(2):
        for half in range(2):
            total = keep[k, half].astype(F32) + came[k, half].astype(F32)
            outs[2 * half + k][...] = total.astype(BF16)


def halve(keep, came, after):
    part = jax.ShapeDtypeStruct(keep.shape[2:], BF16)
    vmem = pl.BlockSpec(memory_space=pltpu.VMEM)
    out = pl.pallas_call(
        halve_kernel,
        out_shape=(part,) * 4,
        in_specs=[vmem, vmem] + [pl.BlockSpec(memory_space=pl.ANY)] * len(after),
        out_specs=(vmem,) * 4,
        compiler_params=pltpu.CompilerParams(vmem_limit_bytes=24 * 1024 * 1024),
        cost_estimate=pl.CostEstimate(flops=2_000_000, bytes_accessed=6_000_000, transcendentals=0),
        name="halve",
    )(keep, came, *after)
    return out[0:2], out[2:4]


def join_kernel(norm, *refs):
    out = refs[-1]
    pairs = refs[:-1]
    slot = 0
    for i in range(0, len(pairs), 4):
        for k in range(pairs[i].shape[0]):
            for kept, came in (pairs[i : i + 2], pairs[i + 2 : i + 4]):
                out[slot] = (kept[k].astype(F32) + came[k].astype(F32)) * norm
                slot += 1


def join_heads(pairs, norm):
    flat = [array for pair in pairs for array in pair]
    slots = sum(kept.shape[0] for kept, _ in pairs)
    _, outs, piece = flat[0].shape
    vmem = pl.BlockSpec(memory_space=pltpu.VMEM)
    return pl.pallas_call(
        functools.partial(join_kernel, norm),
        out_shape=jax.ShapeDtypeStruct((slots, outs, piece), F32),
        in_specs=[vmem] * len(flat),
        out_specs=vmem,
        compiler_params=pltpu.CompilerParams(vmem_limit_bytes=VMEM_LIMIT),
        cost_estimate=pl.CostEstimate(flops=1_000_000, bytes_accessed=4_000_000, transcendentals=0),
        name="join_heads",
    )(*flat)


def fast_local(
    patches, norm_gain, input_proj, output_proj, level_scale, level_shift, head_weight, targets,
    level_counts, tile_dataset, slot_level,
):
    rows, cols, width = patches.shape
    lats, tiles = lax.axis_size("lat"), lax.axis_size("var")
    slots = head_weight.shape[0]
    lat, var = lax.axis_index("lat"), lax.axis_index("var")
    place = jnp.stack([lat, var]).astype(jnp.int32)
    gathered = lax.all_gather(jnp.transpose(head_weight, (0, 2, 1)), "lat", axis=0, tiled=False)

    right = [(i, (i + 1) % tiles) for i in range(tiles)]
    up = [(i, i + 1) for i in range(lats - 1)]
    down = [(i + 1, i) for i in range(lats - 1)]
    left = lax.ppermute(patches[:, cols - HC :], "var", right)
    shifted = jnp.concatenate([left, patches[:, : cols - HC]], axis=1)
    above = lax.ppermute(shifted[HR:], "lat", up)
    below = lax.ppermute(shifted[:HR], "lat", down)
    mine = attention(place, (shifted, above, below), norm_gain, input_proj, output_proj, lats)
    pieces = [mine]
    for s in range(1, tiles):
        pieces.append(lax.ppermute(mine, "var", [(i, (i + s) % tiles) for i in range(tiles)]))

    tile_of = jnp.asarray(np.arange(rows * tiles * cols)[:, None] % (tiles * cols) // cols, jnp.int32)
    scale3, shift3 = level_scale.reshape(slots, 1, width), level_shift.reshape(slots, 1, width)
    small = (level_counts, tile_dataset, slot_level)
    flip = lambda array, bit: lax.ppermute(array, "lat", [(i, i ^ bit) for i in range(lats)])
    add = lambda a, b: (a.astype(F32) + b.astype(F32)).astype(BF16)
    common = (lats, place, small, tile_of, scale3, shift3, gathered, targets)
    most = slots // 2 - 1
    bits = (2, 4)
    keep_a, send_a, so_far, band, latent = slot_group(0, most, *common, pieces, None)
    keep_b, send_b, terms = slot_group(most, slots // 2 - most, *common, None, (band, so_far))
    grad_latent = lax.psum_scatter(terms, "var", scatter_dimension=0, tiled=False)
    pairs, came = [], [terms]
    for keep, send in ((keep_a, send_a), (keep_b, send_b)):
        kept, sent = halve(keep, flip(send, 1), came)
        came = [flip(sent[k], bits[k]) for k in range(2)]
        for k in range(2):
            last = flip(add(kept[k][1], came[k][1]), bits[1 - k])
            pairs.append((add(kept[k][0], came[k][0]), last))
    grad_head = join_heads(pairs, 1.0 / math.sqrt(lats * rows * tiles * cols))
    return (latent, grad_latent, jnp.transpose(grad_head, (0, 2, 1)))


def padded(array, sides, width, wrap):
    for axis, dim in sides:
        size, length = (lax.axis_size(axis), array.shape[dim])
        up = [(i, (i + 1) % size) for i in range(size if wrap else size - 1)]
        down = [(j, i) for i, j in up]
        last = lax.slice_in_dim(array, length - width, length, axis=dim)
        initial = lax.slice_in_dim(array, 0, width, axis=dim)
        before = lax.ppermute(last, axis, up)
        after = lax.ppermute(initial, axis, down)
        array = jnp.concatenate([before, array, after], axis=dim)
    return array


def layer_norm(values, gain):
    wide = values.astype(jnp.float32)
    average = jnp.mean(wide, axis=-1, keepdims=True)
    centred = wide - average
    variance = jnp.mean(centred * centred, axis=-1, keepdims=True)
    return (centred * lax.rsqrt(variance + EPS) * gain).astype(jnp.bfloat16)


def window_attention(query_ext, keyval, row_valid, heads):
    ext_rows, ext_cols, width = query_ext.shape
    head_size = width // heads
    win_rows = ext_rows // WH
    win_cols = ext_cols // WW

    def split(values, parts):
        shaped = values.reshape(win_rows, WH, win_cols, WW, parts, heads, head_size)
        return shaped.transpose(0, 2, 1, 3, 4, 5, 6).reshape(
            win_rows * win_cols, WH * WW, parts, heads, head_size
        )

    query_win = split(query_ext, 1)[:, :, 0]
    pairs = split(keyval, 2)
    key_win = pairs[:, :, 0]
    value_win = pairs[:, :, 1]
    key_mask = jnp.broadcast_to(
        row_valid.reshape(win_rows, 1, WH, 1), (win_rows, win_cols, WH, WW)
    ).reshape(win_rows * win_cols, WH * WW)
    scores = jnp.einsum(
        "wqhd,wkhd->whqk", query_win, key_win, preferred_element_type=jnp.float32
    ) / math.sqrt(head_size)
    scores = jnp.where(key_mask[:, None, None, :], scores, -jnp.inf)
    peak = jnp.max(scores, axis=-1, keepdims=True)
    weights = jnp.exp(scores - peak)
    probs = (weights / jnp.sum(weights, axis=-1, keepdims=True)).astype(jnp.bfloat16)
    mixed = jnp.einsum("whqk,wkhd->wqhd", probs, value_win, preferred_element_type=jnp.float32)
    return (
        mixed.reshape(win_rows, win_cols, WH, WW, width)
        .transpose(0, 2, 1, 3, 4)
        .reshape(ext_rows, ext_cols, width)
    )


def slot_terms(piece, target_rows, live_cols, level_scale, level_shift, heads_full):
    piece_wide = piece.astype(jnp.float32)
    rows = (
        piece_wide[None] * level_scale[:, None, None, :] + level_shift[:, None, None, :]
    ).astype(jnp.bfloat16)
    predicted = jnp.einsum("krnd,kdo->krno", rows, heads_full, preferred_element_type=jnp.float32)
    errors = ((predicted - target_rows.astype(jnp.float32)) * live_cols[:, None, :, None]).astype(
        jnp.bfloat16
    )
    back_grad = jnp.einsum("krno,kdo->krnd", errors, heads_full, preferred_element_type=jnp.float32)
    piece_grad = jnp.sum(back_grad * level_scale[:, None, None, :], axis=0)
    head_add = jnp.einsum("krnd,krno->dko", rows, errors, preferred_element_type=jnp.float32)
    return (piece_grad, head_add)


def local(
    patches,
    norm_gain,
    input_proj,
    output_proj,
    level_scale,
    level_shift,
    head_weight,
    targets,
    level_counts,
    tile_dataset,
    slot_level,
):
    band_rows, band_cols, width = patches.shape
    half_rows = WH // 2
    half_cols = WW // 2
    lat_count = lax.axis_size("lat")
    var_count = lax.axis_size("var")
    lat_place = lax.axis_index("lat")
    ext_rows = band_rows + WH
    ext_cols = band_cols + WW
    extended = padded(patches, (("lat", 0),), half_rows, False)
    extended = padded(extended, (("var", 1),), half_cols, True)
    normed_ext = layer_norm(extended, norm_gain)
    keyval = jnp.dot(
        normed_ext.reshape(-1, width), input_proj[:, width:], preferred_element_type=jnp.float32
    )
    keyval = keyval.astype(jnp.bfloat16).reshape(ext_rows, ext_cols, 2 * width)
    normed = normed_ext[half_rows : half_rows + band_rows, half_cols : half_cols + band_cols]
    queries = jnp.dot(
        normed.reshape(-1, width), input_proj[:, :width], preferred_element_type=jnp.float32
    )
    queries = queries.astype(jnp.bfloat16).reshape(band_rows, band_cols, width)
    query_ext = jnp.pad(queries, ((half_rows, WH - half_rows), (half_cols, WW - half_cols), (0, 0)))
    global_row = lat_place * band_rows - half_rows + jnp.arange(ext_rows, dtype=jnp.int32)
    row_valid = (global_row >= 0) & (global_row < lat_count * band_rows)
    mixed = window_attention(query_ext, keyval, row_valid, HEADS)
    attn = mixed[half_rows : half_rows + band_rows, half_cols : half_cols + band_cols].astype(
        jnp.bfloat16
    )
    update = jnp.dot(
        attn.reshape(-1, width), output_proj, preferred_element_type=jnp.float32
    ).reshape(band_rows, band_cols, width)
    latent = (patches.astype(jnp.float32) + update).astype(jnp.bfloat16)
    dataset_row = tile_dataset[0]
    dataset_ids = jnp.arange(level_counts.shape[0], dtype=jnp.int32)
    tile_levels = jnp.sum(
        jnp.where(dataset_row[:, None] == dataset_ids[None, :], level_counts[None, :], 0), axis=1
    )
    live_tiles = (slot_level[None, :] < tile_levels[:, None]).astype(jnp.float32)
    heads_full = lax.all_gather(head_weight, "lat", axis=1, tiled=True)
    tile_ids = jnp.arange(var_count, dtype=jnp.int32)
    piece = lax.all_gather(latent, "var", axis=1, tiled=True)
    piece_cols = piece.shape[1]
    column_tile = jnp.arange(piece_cols, dtype=jnp.int32) // band_cols
    onehot = (column_tile[:, None] == tile_ids[None, :]).astype(jnp.float32)
    column_live = jnp.dot(onehot, live_tiles)
    piece_grad, head_add = slot_terms(
        piece, targets, column_live.T, level_scale, level_shift, heads_full
    )
    latent_terms = piece_grad
    latent_terms, head_terms = (latent_terms, head_add)
    grad_latent = lax.psum_scatter(
        latent_terms.astype(jnp.bfloat16), "var", scatter_dimension=1, tiled=True
    )
    head_terms = head_terms * (1.0 / math.sqrt(lat_count * band_rows * var_count * band_cols))
    mine = lax.psum_scatter(
        head_terms.astype(jnp.bfloat16), "lat", scatter_dimension=0, tiled=True
    ).astype(jnp.float32)
    grad_head = jnp.transpose(mine, (1, 0, 2))
    return (latent, grad_latent, grad_head)


def solution(mesh):
    in_specs = (
        P("lat", "var", None),
        P(),
        P(),
        P(),
        P("var", None),
        P("var", None),
        P("var", "lat", None),
        P("var", "lat", None, None),
        P(),
        P("lat", None),
        P("var"),
    )
    fast = mesh.shape["lat"] == 8 and mesh.shape["var"] == 4
    body = fast_local if fast else local
    out_specs = (P("lat", "var", None), P("lat", "var", None), P("var", "lat", None))
    return jax.shard_map(body, mesh=mesh, in_specs=in_specs, out_specs=out_specs, check_vma=False)
```

```python
import functools
import math

import jax
import jax.numpy as jnp
import numpy as np
from jax import lax
from jax.experimental import pallas as pl
from jax.experimental.pallas import tpu as pltpu
from jax.sharding import PartitionSpec as P

HEADS = 16
WH = 6
WW = 12
EPS = 1e-05
HR = WH // 2
HC = WW // 2
QP = 48
VMEM_LIMIT = 48 * 1024 * 1024
F32 = jnp.float32
BF16 = jnp.bfloat16


def gather_maps(cols):
    win_cols = cols // WW
    windows = 2 * win_cols
    into = np.zeros((windows * 2 * QP, 2 * WH * cols), np.float32)
    back = np.zeros((WH * cols, windows * QP), np.float32)
    for win in range(windows):
        win_row, win_col = divmod(win, win_cols)
        for row in range(HR):
            for c in range(WW):
                own = (win_row * HR + row) * cols + win_col * WW + c
                slot = row * WW + c
                into[win * 2 * QP + slot, own] = 1
                into[win * 2 * QP + QP + slot, WH * cols + own] = 1
                back[own, win * QP + slot] = 1
    return into, back


def attention_kernel(
    bands,
    place,
    own,
    above,
    below,
    gain_hbm,
    maps_hbm,
    in_hbm,
    out_hbm,
    out,
    raw,
    qkv,
    attn,
    gain,
    maps,
    proj_in,
    proj_out,
    sems,
):
    moves = [
        pltpu.make_async_copy(src, dst, sems.at[i])
        for i, (src, dst) in enumerate(
            ((gain_hbm, gain), (maps_hbm, maps), (in_hbm, proj_in), (out_hbm, proj_out))
        )
    ]
    for move in moves:
        move.start()
    cols, width = own.shape[1], own.shape[2]
    win_cols = cols // WW
    windows = 2 * win_cols
    slots = windows * 2 * QP
    head_size = width // HEADS
    quad = 256 // head_size
    size = WH * cols
    start = 0
    for ref in (own, above, below):
        count = ref.shape[0] * cols
        raw[start : start + count, :] = ref[...].astype(F32).reshape(count, width)
        start += count
    moves[0].wait()
    wide = raw[...]
    average = jnp.mean(wide, axis=-1, keepdims=True)
    centred = wide - average
    variance = jnp.mean(centred * centred, axis=-1, keepdims=True)
    normed = (centred * lax.rsqrt(variance + EPS) * gain[...]).astype(BF16)
    moves[1].wait()
    win_x = jnp.dot(maps[0:slots, :], normed, preferred_element_type=F32).astype(BF16)
    moves[2].wait()
    step = 512
    for j in range(3 * width // step):
        part = slice(j * step, (j + 1) * step)
        qkv[:, part] = jnp.dot(win_x, proj_in[:, part], preferred_element_type=F32).astype(BF16)
    lane = lax.broadcasted_iota(jnp.int32, (1, 256), 1) // head_size
    heads = [jnp.where(lane == h, 1.0, 0.0) for h in range(quad)]
    key_id = lax.broadcasted_iota(jnp.int32, (1, 2 * QP), 1)
    scale = 1.0 / math.sqrt(head_size)
    for win in range(windows):
        win_row = win // win_cols
        edge = 0 if win_row == 0 else bands - 1
        has_halo = place[0] != edge
        halo_keys = jnp.logical_and(key_id >= QP, key_id < QP + HR * WW)
        valid = jnp.logical_or(key_id < HR * WW, jnp.logical_and(halo_keys, has_halo))
        bias = jnp.where(valid, 0.0, -1e30)
        row0 = win * 2 * QP
        for g in range(width // 256):
            lanes = slice(g * 256, (g + 1) * 256)
            query = qkv[row0 : row0 + QP, lanes].astype(F32) * scale
            stacked = jnp.concatenate([query * h for h in heads], axis=0).astype(BF16)
            key = qkv[row0 : row0 + 2 * QP, width + g * 256 : width + (g + 1) * 256]
            value = qkv[row0 : row0 + 2 * QP, 2 * width + g * 256 : 2 * width + (g + 1) * 256]
            scores = (
                lax.dot_general(
                    stacked, key, (((1,), (1,)), ((), ())), preferred_element_type=F32
                )
                + bias
            )
            weights = jnp.exp(scores - jnp.max(scores, axis=-1, keepdims=True))
            probs = (weights / jnp.sum(weights, axis=-1, keepdims=True)).astype(BF16)
            mixed = jnp.dot(probs, value, preferred_element_type=F32)
            chosen = mixed[0:QP] * heads[0]
            for h in range(1, quad):
                chosen = chosen + mixed[h * QP : (h + 1) * QP] * heads[h]
            attn[win * QP : (win + 1) * QP, lanes] = chosen.astype(BF16)
    back = maps[slots : slots + size, 0 : windows * QP]
    ordered = jnp.dot(back, attn[...], preferred_element_type=F32).astype(BF16)
    moves[3].wait()
    update = jnp.dot(ordered, proj_out[...], preferred_element_type=F32)
    out[...] = (raw[0:size, :] + update).astype(BF16)


def attention(place, pieces, gain, proj_in, proj_out, bands):
    rows, cols, width = pieces[0].shape
    into, back = gather_maps(cols)
    total = into.shape[1]
    windows = 2 * (cols // WW)
    back = np.pad(back, ((0, 0), (0, total - back.shape[1])))
    maps = np.concatenate([into, back])
    vmem = pl.BlockSpec(memory_space=pltpu.VMEM)
    hbm = pl.BlockSpec(memory_space=pltpu.HBM)
    return pl.pallas_call(
        functools.partial(attention_kernel, bands),
        out_shape=jax.ShapeDtypeStruct((rows * cols, width), BF16),
        in_specs=[pl.BlockSpec(memory_space=pltpu.SMEM)] + [vmem] * 3 + [hbm] * 4,
        out_specs=vmem,
        scratch_shapes=[
            pltpu.VMEM((total, width), F32),
            pltpu.VMEM((windows * 2 * QP, 3 * width), BF16),
            pltpu.VMEM((windows * QP, width), BF16),
            pltpu.VMEM((1, width), F32),
            pltpu.VMEM(maps.shape, BF16),
            pltpu.VMEM(proj_in.shape, BF16),
            pltpu.VMEM(proj_out.shape, BF16),
            pltpu.SemaphoreType.DMA((4,)),
        ],
        compiler_params=pltpu.CompilerParams(vmem_limit_bytes=53 * 1024 * 1024),
        cost_estimate=pl.CostEstimate(
            flops=6_000_000_000, bytes_accessed=12_000_000, transcendentals=400_000
        ),
        name="window_attention",
    )(
        place,
        *pieces,
        gain.reshape(1, width),
        jnp.asarray(maps, BF16),
        proj_in,
        proj_out,
    )


def band_map(tiles, cols):
    wide = tiles * cols
    chosen = np.zeros((WH * wide, WH * wide), np.float32)
    for r in range(WH):
        for c in range(wide):
            tile, at = divmod((c + HC) % wide, cols)
            chosen[r * wide + c, tile * WH * cols + r * cols + at] = 1
    return chosen


def band_kernel(tiles, cols, place, chosen, *refs):
    pieces, (band, latent, laid, wide) = refs[:tiles], refs[tiles:]
    size = WH * cols
    var = place[1]
    for s in range(tiles):
        tile = lax.rem(var + tiles - s, tiles)
        laid[pl.ds(pl.multiple_of(tile * size, 16), size), :] = pieces[s][...]
    wide[...] = jnp.dot(chosen[...], laid[...], preferred_element_type=F32)
    band[...] = wide[...].astype(BF16)
    for r in range(WH):
        start = pl.multiple_of(r * tiles * cols + var * cols, 8)
        latent[r] = wide[pl.ds(start, cols), :].astype(BF16)


def band_latents(place, pieces, cols):
    tiles = len(pieces)
    width = pieces[0].shape[1]
    total = WH * tiles * cols
    vmem = pl.BlockSpec(memory_space=pltpu.VMEM)
    return pl.pallas_call(
        functools.partial(band_kernel, tiles, cols),
        out_shape=(
            jax.ShapeDtypeStruct((total, width), BF16),
            jax.ShapeDtypeStruct((WH, cols, width), BF16),
        ),
        in_specs=[pl.BlockSpec(memory_space=pltpu.SMEM)] + [vmem] * (tiles + 1),
        out_specs=(vmem, vmem),
        scratch_shapes=[pltpu.VMEM((total, width), BF16), pltpu.VMEM((total, width), F32)],
        compiler_params=pltpu.CompilerParams(vmem_limit_bytes=VMEM_LIMIT),
        cost_estimate=pl.CostEstimate(
            flops=2 * total * total * width, bytes_accessed=4_000_000, transcendentals=0
        ),
        name="band_latents",
    )(place, jnp.asarray(band_map(tiles, cols), BF16), *pieces)


def slot_errors(level, tile_counts, rows, weight, target):
    predicted = lax.dot_general(
        rows, weight, (((1,), (1,)), ((), ())), preferred_element_type=F32
    )
    live = jnp.where(level < tile_counts, 1.0, 0.0)
    diff = predicted - target.astype(F32).reshape(predicted.shape)
    return (diff * live).astype(BF16)


def head_halves(k, lats, lat, errors, rows, turned, keep, send):
    turned[k] = lax.dot_general(
        errors, rows, (((0,), (0,)), ((), ())), preferred_element_type=F32
    ).astype(BF16)
    piece = turned.shape[-1] // lats
    for q in range(lats):
        core, x, y = q & 1, (q >> 1) & 1, (q >> 2) & 1
        outer, inner = (x, y) if k == 0 else (y, x)
        start = pl.multiple_of(jnp.bitwise_xor(lat, q) * piece, piece)
        to = send if core else keep
        to[k, outer, inner, 0] = turned[k, :, pl.ds(start, piece)]


def add_back(lats, errs, gathered, scale, total):
    piece = gathered.shape[-1]
    for l in range(0, lats, 2):
        lanes = slice(l * piece, (l + 2) * piece)
        term = 0.0
        for k in range(2):
            weight = jnp.concatenate([gathered[l, k], gathered[l + 1, k]], axis=1)
            factor = scale[k][:, lanes]
            term = term + jnp.dot(errs[k], weight, preferred_element_type=F32) * factor
        total[:, lanes] += term


def slot_kernel(
    first_slot,
    lats,
    tiles,
    final,
    place,
    counts,
    datasets,
    levels,
    tile_of,
    scale,
    shift,
    gathered,
    target,
    *refs,
):
    if final:
        band, before, keep, send, out, total, rows0, rows1, errs, turned, tile_counts = refs
    else:
        band, keep, send, total, rows0, rows1, errs, turned, tile_counts = refs
    rows = (rows0, rows1)
    step, steps = pl.program_id(0), pl.num_programs(0)
    slot = first_slot + 2 * step

    @pl.when(step == 0)
    def _():
        total[...] = before[...] if final else jnp.zeros_like(total)
        tile = tile_of[...]
        wanted = jnp.zeros_like(tile)
        for t in range(tiles):
            wanted = jnp.where(tile == t, counts[datasets[0, t]], wanted)
        tile_counts[...] = wanted

    for k in range(2):
        rows[k][...] = (band[...].astype(F32) * scale[k] + shift[k]).astype(BF16)
    for k in range(2):
        weight = jnp.concatenate([gathered[l, k] for l in range(lats)], axis=1)
        errs[k] = slot_errors(levels[slot + k], tile_counts[...], rows[k][...], weight, target[k])
    for k in range(2):
        head_halves(k, lats, place[0], errs[k], rows[k][...], turned, keep, send)
    add_back(lats, errs, gathered, scale, total)

    if final:

        @pl.when(step == steps - 1)
        def _():
            cols = out.shape[2]
            for s in range(tiles):
                for r in range(WH):
                    start = (r * tiles + s) * cols
                    out[s, r] = total[start : start + cols, :].astype(BF16)


def slot_group(pair, pairs, lats, place, small, tile_of, scale, shift, gathered, targets, band, before):
    places, width = tile_of.shape[0], scale.shape[-1]
    outs = targets.shape[-1]
    tiles = small[1].shape[1]
    piece = width // lats
    cols = places // (WH * tiles)
    smem = pl.BlockSpec(memory_space=pltpu.SMEM)
    fixed = lambda shape: pl.BlockSpec(shape, lambda i: (0,) * len(shape))
    halves = jax.ShapeDtypeStruct((2, 2, 2, pairs, outs, piece), BF16)
    half_spec = pl.BlockSpec((2, 2, 2, 1, outs, piece), lambda i: (0, 0, 0, i, 0, 0))
    level_spec = pl.BlockSpec((2, 1, width), lambda i: (i + pair, 0, 0))
    in_specs = [smem] * 4 + [
        fixed(tile_of.shape),
        level_spec,
        level_spec,
        pl.BlockSpec((lats, 2, outs, piece), lambda i: (0, i + pair, 0, 0)),
        pl.BlockSpec((2,) + targets.shape[1:], lambda i: (i + pair, 0, 0, 0)),
    ]
    args = [place, *small, tile_of, scale, shift, gathered, targets, band]
    final = before is not None
    scratch = [
        pltpu.VMEM((places, width), BF16),
        pltpu.VMEM((places, width), BF16),
        pltpu.VMEM((2, places, outs), BF16),
        pltpu.VMEM((2, outs, width), BF16),
        pltpu.VMEM((places, 1), jnp.int32),
    ]
    sums = jax.ShapeDtypeStruct((places, width), F32)
    if final:
        args.append(before)
        scratch.insert(0, pltpu.VMEM(sums.shape, F32))
        results = [jax.ShapeDtypeStruct((tiles, WH, cols, width), BF16)]
    else:
        results = [sums]
    in_specs.extend(fixed(arg.shape) for arg in args[len(in_specs) :])
    limit = (45 if final else 46) * 1024 * 1024
    return pl.pallas_call(
        functools.partial(slot_kernel, 2 * pair, lats, tiles, final),
        grid=(pairs,),
        out_shape=(halves, halves, *results),
        in_specs=in_specs,
        out_specs=(half_spec, half_spec, *(fixed(r.shape) for r in results)),
        scratch_shapes=scratch,
        compiler_params=pltpu.CompilerParams(
            vmem_limit_bytes=limit, fuse_transposed_lhs_in_matmul=True
        ),
        cost_estimate=pl.CostEstimate(
            flops=pairs * 12 * places * width * outs, bytes_accessed=pairs * 5_000_000, transcendentals=0
        ),
        name="slot_group",
    )(*args)


def halve_kernel(keep, came, *refs):
    outs = refs[-4:]
    for k in range(2):
        for half in range(2):
            total = keep[k, half].astype(F32) + came[k, half].astype(F32)
            outs[2 * half + k][...] = total.astype(BF16)


def halve(keep, came, after):
    part = jax.ShapeDtypeStruct(keep.shape[2:], BF16)
    vmem = pl.BlockSpec(memory_space=pltpu.VMEM)
    out = pl.pallas_call(
        halve_kernel,
        out_shape=(part,) * 4,
        in_specs=[vmem, vmem] + [pl.BlockSpec(memory_space=pl.ANY)] * len(after),
        out_specs=(vmem,) * 4,
        compiler_params=pltpu.CompilerParams(vmem_limit_bytes=24 * 1024 * 1024),
        cost_estimate=pl.CostEstimate(flops=2_000_000, bytes_accessed=6_000_000, transcendentals=0),
        name="halve",
    )(keep, came, *after)
    return out[0:2], out[2:4]


def join_kernel(norm, *refs):
    out = refs[-1]
    pairs = refs[:-1]
    slot = 0
    for i in range(0, len(pairs), 4):
        for k in range(pairs[i].shape[0]):
            for kept, came in (pairs[i : i + 2], pairs[i + 2 : i + 4]):
                out[slot] = (kept[k].astype(F32) + came[k].astype(F32)) * norm
                slot += 1


def join_heads(pairs, norm):
    flat = [array for pair in pairs for array in pair]
    slots = sum(kept.shape[0] for kept, _ in pairs)
    _, outs, piece = flat[0].shape
    vmem = pl.BlockSpec(memory_space=pltpu.VMEM)
    return pl.pallas_call(
        functools.partial(join_kernel, norm),
        out_shape=jax.ShapeDtypeStruct((slots, outs, piece), F32),
        in_specs=[vmem] * len(flat),
        out_specs=vmem,
        compiler_params=pltpu.CompilerParams(vmem_limit_bytes=VMEM_LIMIT),
        cost_estimate=pl.CostEstimate(flops=1_000_000, bytes_accessed=4_000_000, transcendentals=0),
        name="join_heads",
    )(*flat)


def fast_local(
    patches, norm_gain, input_proj, output_proj, level_scale, level_shift, head_weight, targets,
    level_counts, tile_dataset, slot_level,
):
    rows, cols, width = patches.shape
    lats, tiles = lax.axis_size("lat"), lax.axis_size("var")
    slots = head_weight.shape[0]
    lat, var = lax.axis_index("lat"), lax.axis_index("var")
    place = jnp.stack([lat, var]).astype(jnp.int32)
    gathered = lax.all_gather(jnp.transpose(head_weight, (0, 2, 1)), "lat", axis=0, tiled=False)

    right = [(i, (i + 1) % tiles) for i in range(tiles)]
    up = [(i, i + 1) for i in range(lats - 1)]
    down = [(i + 1, i) for i in range(lats - 1)]
    left = lax.ppermute(patches[:, cols - HC :], "var", right)
    shifted = jnp.concatenate([left, patches[:, : cols - HC]], axis=1)
    above = lax.ppermute(shifted[HR:], "lat", up)
    below = lax.ppermute(shifted[:HR], "lat", down)
    mine = attention(place, (shifted, above, below), norm_gain, input_proj, output_proj, lats)
    pieces = [mine]
    for s in range(1, tiles):
        pieces.append(lax.ppermute(mine, "var", [(i, (i + s) % tiles) for i in range(tiles)]))

    band, latent = band_latents(place, pieces, cols)
    tile_of = jnp.asarray(np.arange(rows * tiles * cols)[:, None] % (tiles * cols) // cols, jnp.int32)
    scale3, shift3 = level_scale.reshape(slots, 1, width), level_shift.reshape(slots, 1, width)
    small = (level_counts, tile_dataset, slot_level)
    flip = lambda array, bit: lax.ppermute(array, "lat", [(i, i ^ bit) for i in range(lats)])
    add = lambda a, b: (a.astype(F32) + b.astype(F32)).astype(BF16)
    common = (lats, place, small, tile_of, scale3, shift3, gathered, targets, band)
    most = slots // 2 - 1
    bits = (2, 4)
    keep_a, send_a, so_far = slot_group(0, most, *common, None)
    keep_b, send_b, terms = slot_group(most, slots // 2 - most, *common, so_far)
    grad_latent = lax.psum_scatter(terms, "var", scatter_dimension=0, tiled=False)
    pairs, came = [], [terms]
    for keep, send in ((keep_a, send_a), (keep_b, send_b)):
        kept, sent = halve(keep, flip(send, 1), came)
        came = [flip(sent[k], bits[k]) for k in range(2)]
        for k in range(2):
            last = flip(add(kept[k][1], came[k][1]), bits[1 - k])
            pairs.append((add(kept[k][0], came[k][0]), last))
    grad_head = join_heads(pairs, 1.0 / math.sqrt(lats * rows * tiles * cols))
    return (latent, grad_latent, jnp.transpose(grad_head, (0, 2, 1)))


def padded(array, sides, width, wrap):
    for axis, dim in sides:
        size, length = (lax.axis_size(axis), array.shape[dim])
        up = [(i, (i + 1) % size) for i in range(size if wrap else size - 1)]
        down = [(j, i) for i, j in up]
        last = lax.slice_in_dim(array, length - width, length, axis=dim)
        initial = lax.slice_in_dim(array, 0, width, axis=dim)
        before = lax.ppermute(last, axis, up)
        after = lax.ppermute(initial, axis, down)
        array = jnp.concatenate([before, array, after], axis=dim)
    return array


def layer_norm(values, gain):
    wide = values.astype(jnp.float32)
    average = jnp.mean(wide, axis=-1, keepdims=True)
    centred = wide - average
    variance = jnp.mean(centred * centred, axis=-1, keepdims=True)
    return (centred * lax.rsqrt(variance + EPS) * gain).astype(jnp.bfloat16)


def window_attention(query_ext, keyval, row_valid, heads):
    ext_rows, ext_cols, width = query_ext.shape
    head_size = width // heads
    win_rows = ext_rows // WH
    win_cols = ext_cols // WW

    def split(values, parts):
        shaped = values.reshape(win_rows, WH, win_cols, WW, parts, heads, head_size)
        return shaped.transpose(0, 2, 1, 3, 4, 5, 6).reshape(
            win_rows * win_cols, WH * WW, parts, heads, head_size
        )

    query_win = split(query_ext, 1)[:, :, 0]
    pairs = split(keyval, 2)
    key_win = pairs[:, :, 0]
    value_win = pairs[:, :, 1]
    key_mask = jnp.broadcast_to(
        row_valid.reshape(win_rows, 1, WH, 1), (win_rows, win_cols, WH, WW)
    ).reshape(win_rows * win_cols, WH * WW)
    scores = jnp.einsum(
        "wqhd,wkhd->whqk", query_win, key_win, preferred_element_type=jnp.float32
    ) / math.sqrt(head_size)
    scores = jnp.where(key_mask[:, None, None, :], scores, -jnp.inf)
    peak = jnp.max(scores, axis=-1, keepdims=True)
    weights = jnp.exp(scores - peak)
    probs = (weights / jnp.sum(weights, axis=-1, keepdims=True)).astype(jnp.bfloat16)
    mixed = jnp.einsum("whqk,wkhd->wqhd", probs, value_win, preferred_element_type=jnp.float32)
    return (
        mixed.reshape(win_rows, win_cols, WH, WW, width)
        .transpose(0, 2, 1, 3, 4)
        .reshape(ext_rows, ext_cols, width)
    )


def slot_terms(piece, target_rows, live_cols, level_scale, level_shift, heads_full):
    piece_wide = piece.astype(jnp.float32)
    rows = (
        piece_wide[None] * level_scale[:, None, None, :] + level_shift[:, None, None, :]
    ).astype(jnp.bfloat16)
    predicted = jnp.einsum("krnd,kdo->krno", rows, heads_full, preferred_element_type=jnp.float32)
    errors = ((predicted - target_rows.astype(jnp.float32)) * live_cols[:, None, :, None]).astype(
        jnp.bfloat16
    )
    back_grad = jnp.einsum("krno,kdo->krnd", errors, heads_full, preferred_element_type=jnp.float32)
    piece_grad = jnp.sum(back_grad * level_scale[:, None, None, :], axis=0)
    head_add = jnp.einsum("krnd,krno->dko", rows, errors, preferred_element_type=jnp.float32)
    return (piece_grad, head_add)


def local(
    patches,
    norm_gain,
    input_proj,
    output_proj,
    level_scale,
    level_shift,
    head_weight,
    targets,
    level_counts,
    tile_dataset,
    slot_level,
):
    band_rows, band_cols, width = patches.shape
    half_rows = WH // 2
    half_cols = WW // 2
    lat_count = lax.axis_size("lat")
    var_count = lax.axis_size("var")
    lat_place = lax.axis_index("lat")
    ext_rows = band_rows + WH
    ext_cols = band_cols + WW
    extended = padded(patches, (("lat", 0),), half_rows, False)
    extended = padded(extended, (("var", 1),), half_cols, True)
    normed_ext = layer_norm(extended, norm_gain)
    keyval = jnp.dot(
        normed_ext.reshape(-1, width), input_proj[:, width:], preferred_element_type=jnp.float32
    )
    keyval = keyval.astype(jnp.bfloat16).reshape(ext_rows, ext_cols, 2 * width)
    normed = normed_ext[half_rows : half_rows + band_rows, half_cols : half_cols + band_cols]
    queries = jnp.dot(
        normed.reshape(-1, width), input_proj[:, :width], preferred_element_type=jnp.float32
    )
    queries = queries.astype(jnp.bfloat16).reshape(band_rows, band_cols, width)
    query_ext = jnp.pad(queries, ((half_rows, WH - half_rows), (half_cols, WW - half_cols), (0, 0)))
    global_row = lat_place * band_rows - half_rows + jnp.arange(ext_rows, dtype=jnp.int32)
    row_valid = (global_row >= 0) & (global_row < lat_count * band_rows)
    mixed = window_attention(query_ext, keyval, row_valid, HEADS)
    attn = mixed[half_rows : half_rows + band_rows, half_cols : half_cols + band_cols].astype(
        jnp.bfloat16
    )
    update = jnp.dot(
        attn.reshape(-1, width), output_proj, preferred_element_type=jnp.float32
    ).reshape(band_rows, band_cols, width)
    latent = (patches.astype(jnp.float32) + update).astype(jnp.bfloat16)
    dataset_row = tile_dataset[0]
    dataset_ids = jnp.arange(level_counts.shape[0], dtype=jnp.int32)
    tile_levels = jnp.sum(
        jnp.where(dataset_row[:, None] == dataset_ids[None, :], level_counts[None, :], 0), axis=1
    )
    live_tiles = (slot_level[None, :] < tile_levels[:, None]).astype(jnp.float32)
    heads_full = lax.all_gather(head_weight, "lat", axis=1, tiled=True)
    tile_ids = jnp.arange(var_count, dtype=jnp.int32)
    piece = lax.all_gather(latent, "var", axis=1, tiled=True)
    piece_cols = piece.shape[1]
    column_tile = jnp.arange(piece_cols, dtype=jnp.int32) // band_cols
    onehot = (column_tile[:, None] == tile_ids[None, :]).astype(jnp.float32)
    column_live = jnp.dot(onehot, live_tiles)
    piece_grad, head_add = slot_terms(
        piece, targets, column_live.T, level_scale, level_shift, heads_full
    )
    latent_terms = piece_grad
    latent_terms, head_terms = (latent_terms, head_add)
    grad_latent = lax.psum_scatter(
        latent_terms.astype(jnp.bfloat16), "var", scatter_dimension=1, tiled=True
    )
    head_terms = head_terms * (1.0 / math.sqrt(lat_count * band_rows * var_count * band_cols))
    mine = lax.psum_scatter(
        head_terms.astype(jnp.bfloat16), "lat", scatter_dimension=0, tiled=True
    ).astype(jnp.float32)
    grad_head = jnp.transpose(mine, (1, 0, 2))
    return (latent, grad_latent, grad_head)


def solution(mesh):
    in_specs = (
        P("lat", "var", None),
        P(),
        P(),
        P(),
        P("var", None),
        P("var", None),
        P("var", "lat", None),
        P("var", "lat", None, None),
        P(),
        P("lat", None),
        P("var"),
    )
    fast = mesh.shape["lat"] == 8 and mesh.shape["var"] == 4
    body = fast_local if fast else local
    out_specs = (P("lat", "var", None), P("lat", "var", None), P("var", "lat", None))
    return jax.shard_map(body, mesh=mesh, in_specs=in_specs, out_specs=out_specs, check_vma=False)
```

```python
import functools
import math

import jax
import jax.numpy as jnp
import numpy as np
from jax import lax
from jax.experimental import pallas as pl
from jax.experimental.pallas import tpu as pltpu
from jax.sharding import PartitionSpec as P

HEADS = 16
WH = 6
WW = 12
EPS = 1e-05
HR = WH // 2
HC = WW // 2
QP = 48
VMEM_LIMIT = 48 * 1024 * 1024
F32 = jnp.float32
BF16 = jnp.bfloat16


def gather_maps(cols):
    win_cols = cols // WW
    windows = 2 * win_cols
    into = np.zeros((windows * 2 * QP, 2 * WH * cols), np.float32)
    back = np.zeros((WH * cols, windows * QP), np.float32)
    for win in range(windows):
        win_row, win_col = divmod(win, win_cols)
        for row in range(HR):
            for c in range(WW):
                own = (win_row * HR + row) * cols + win_col * WW + c
                slot = row * WW + c
                into[win * 2 * QP + slot, own] = 1
                into[win * 2 * QP + QP + slot, WH * cols + own] = 1
                back[own, win * QP + slot] = 1
    return into, back


def attention_kernel(
    bands,
    place,
    own,
    above,
    below,
    gain_hbm,
    maps_hbm,
    in_hbm,
    out_hbm,
    out,
    raw,
    qkv,
    attn,
    gain,
    maps,
    proj_in,
    proj_out,
    sems,
):
    moves = [
        pltpu.make_async_copy(src, dst, sems.at[i])
        for i, (src, dst) in enumerate(
            ((gain_hbm, gain), (maps_hbm, maps), (in_hbm, proj_in), (out_hbm, proj_out))
        )
    ]
    for move in moves:
        move.start()
    cols, width = own.shape[1], own.shape[2]
    win_cols = cols // WW
    windows = 2 * win_cols
    slots = windows * 2 * QP
    head_size = width // HEADS
    quad = 256 // head_size
    size = WH * cols
    start = 0
    for ref in (own, above, below):
        count = ref.shape[0] * cols
        raw[start : start + count, :] = ref[...].astype(F32).reshape(count, width)
        start += count
    moves[0].wait()
    wide = raw[...]
    average = jnp.mean(wide, axis=-1, keepdims=True)
    centred = wide - average
    variance = jnp.mean(centred * centred, axis=-1, keepdims=True)
    normed = (centred * lax.rsqrt(variance + EPS) * gain[...]).astype(BF16)
    moves[1].wait()
    win_x = jnp.dot(maps[0:slots, :], normed, preferred_element_type=F32).astype(BF16)
    moves[2].wait()
    step = 512
    for j in range(3 * width // step):
        part = slice(j * step, (j + 1) * step)
        qkv[:, part] = jnp.dot(win_x, proj_in[:, part], preferred_element_type=F32).astype(BF16)
    lane = lax.broadcasted_iota(jnp.int32, (1, 256), 1) // head_size
    heads = [jnp.where(lane == h, 1.0, 0.0) for h in range(quad)]
    key_id = lax.broadcasted_iota(jnp.int32, (1, 2 * QP), 1)
    scale = 1.0 / math.sqrt(head_size)
    for win in range(windows):
        win_row = win // win_cols
        edge = 0 if win_row == 0 else bands - 1
        has_halo = place[0] != edge
        halo_keys = jnp.logical_and(key_id >= QP, key_id < QP + HR * WW)
        valid = jnp.logical_or(key_id < HR * WW, jnp.logical_and(halo_keys, has_halo))
        bias = jnp.where(valid, 0.0, -1e30)
        row0 = win * 2 * QP
        for g in range(width // 256):
            lanes = slice(g * 256, (g + 1) * 256)
            query = qkv[row0 : row0 + QP, lanes].astype(F32) * scale
            stacked = jnp.concatenate([query * h for h in heads], axis=0).astype(BF16)
            key = qkv[row0 : row0 + 2 * QP, width + g * 256 : width + (g + 1) * 256]
            value = qkv[row0 : row0 + 2 * QP, 2 * width + g * 256 : 2 * width + (g + 1) * 256]
            scores = (
                lax.dot_general(
                    stacked, key, (((1,), (1,)), ((), ())), preferred_element_type=F32
                )
                + bias
            )
            weights = jnp.exp(scores - jnp.max(scores, axis=-1, keepdims=True))
            probs = (weights / jnp.sum(weights, axis=-1, keepdims=True)).astype(BF16)
            mixed = jnp.dot(probs, value, preferred_element_type=F32)
            chosen = mixed[0:QP] * heads[0]
            for h in range(1, quad):
                chosen = chosen + mixed[h * QP : (h + 1) * QP] * heads[h]
            attn[win * QP : (win + 1) * QP, lanes] = chosen.astype(BF16)
    back = maps[slots : slots + size, 0 : windows * QP]
    ordered = jnp.dot(back, attn[...], preferred_element_type=F32).astype(BF16)
    moves[3].wait()
    update = jnp.dot(ordered, proj_out[...], preferred_element_type=F32)
    out[...] = (raw[0:size, :] + update).astype(BF16)


def attention(place, pieces, gain, proj_in, proj_out, bands):
    rows, cols, width = pieces[0].shape
    into, back = gather_maps(cols)
    total = into.shape[1]
    windows = 2 * (cols // WW)
    back = np.pad(back, ((0, 0), (0, total - back.shape[1])))
    maps = np.concatenate([into, back])
    vmem = pl.BlockSpec(memory_space=pltpu.VMEM)
    hbm = pl.BlockSpec(memory_space=pltpu.HBM)
    return pl.pallas_call(
        functools.partial(attention_kernel, bands),
        out_shape=jax.ShapeDtypeStruct((rows * cols, width), BF16),
        in_specs=[pl.BlockSpec(memory_space=pltpu.SMEM)] + [vmem] * 3 + [hbm] * 4,
        out_specs=vmem,
        scratch_shapes=[
            pltpu.VMEM((total, width), F32),
            pltpu.VMEM((windows * 2 * QP, 3 * width), BF16),
            pltpu.VMEM((windows * QP, width), BF16),
            pltpu.VMEM((1, width), F32),
            pltpu.VMEM(maps.shape, BF16),
            pltpu.VMEM(proj_in.shape, BF16),
            pltpu.VMEM(proj_out.shape, BF16),
            pltpu.SemaphoreType.DMA((4,)),
        ],
        compiler_params=pltpu.CompilerParams(vmem_limit_bytes=53 * 1024 * 1024),
        cost_estimate=pl.CostEstimate(
            flops=6_000_000_000, bytes_accessed=12_000_000, transcendentals=400_000
        ),
        name="window_attention",
    )(
        place,
        *pieces,
        gain.reshape(1, width),
        jnp.asarray(maps, BF16),
        proj_in,
        proj_out,
    )


def band_map(tiles, cols):
    wide = tiles * cols
    chosen = np.zeros((WH * wide, WH * wide), np.float32)
    for r in range(WH):
        for c in range(wide):
            tile, at = divmod((c + HC) % wide, cols)
            chosen[r * wide + c, tile * WH * cols + r * cols + at] = 1
    return chosen


def order_band(tiles, cols, var, chosen, pieces, laid, wide, band, latent):
    size = WH * cols
    for s in range(tiles):
        tile = lax.rem(var + tiles - s, tiles)
        laid[pl.ds(pl.multiple_of(tile * size, 16), size), :] = pieces[s][...]
    wide[...] = jnp.dot(chosen[...], laid[...], preferred_element_type=F32)
    band[...] = wide[...].astype(BF16)
    for r in range(WH):
        start = pl.multiple_of(r * tiles * cols + var * cols, 8)
        latent[r] = wide[pl.ds(start, cols), :].astype(BF16)


def slot_errors(level, tile_counts, rows, weight, target):
    predicted = lax.dot_general(
        rows, weight, (((1,), (1,)), ((), ())), preferred_element_type=F32
    )
    live = jnp.where(level < tile_counts, 1.0, 0.0)
    diff = predicted - target.astype(F32).reshape(predicted.shape)
    return (diff * live).astype(BF16)


def head_halves(k, lats, lat, errors, rows, turned, keep, send):
    turned[k] = lax.dot_general(
        errors, rows, (((0,), (0,)), ((), ())), preferred_element_type=F32
    ).astype(BF16)
    piece = turned.shape[-1] // lats
    for q in range(lats):
        core, x, y = q & 1, (q >> 1) & 1, (q >> 2) & 1
        outer, inner = (x, y) if k == 0 else (y, x)
        start = pl.multiple_of(jnp.bitwise_xor(lat, q) * piece, piece)
        to = send if core else keep
        to[k, outer, inner, 0] = turned[k, :, pl.ds(start, piece)]


def add_back(lats, at, errs, gathered, scale, total):
    piece = gathered.shape[-1]
    for l in range(0, lats, 2):
        lanes = slice(l * piece, (l + 2) * piece)
        term = 0.0
        for k in range(2):
            weight = jnp.concatenate([gathered[at[l], k], gathered[at[l + 1], k]], axis=1)
            factor = scale[k][:, lanes]
            term = term + jnp.dot(errs[k], weight, preferred_element_type=F32) * factor
        total[:, lanes] += term


def slot_kernel(
    first_slot,
    lats,
    tiles,
    final,
    place,
    counts,
    datasets,
    levels,
    tile_of,
    scale,
    shift,
    gathered,
    target,
    *refs,
):
    if final:
        band, before, keep, send, out, total, rows0, rows1, errs, turned, tile_counts = refs
    else:
        chosen, pieces = refs[0], refs[1 : 1 + tiles]
        refs = refs[1:]
        keep, send, total, band, latent, rows0, rows1, errs, turned, tile_counts = refs[1 + tiles :]
    rows = (rows0, rows1)
    step, steps = pl.program_id(0), pl.num_programs(0)
    slot = first_slot + 2 * step
    at = range(lats)
    if final:
        flips = [jnp.bitwise_xor(place[0], l) for l in range(lats)]
        at = [(q % 2) * 4 + q // 2 % 2 * 2 + q // 4 for q in flips]

    @pl.when(step == 0)
    def _():
        if final:
            total[...] = before[...]
        else:
            order_band(tiles, latent.shape[1], place[1], chosen, pieces, rows0, total, band, latent)
            total[...] = jnp.zeros_like(total)
        tile = tile_of[...]
        wanted = jnp.zeros_like(tile)
        for t in range(tiles):
            wanted = jnp.where(tile == t, counts[datasets[0, t]], wanted)
        tile_counts[...] = wanted

    for k in range(2):
        rows[k][...] = (band[...].astype(F32) * scale[k] + shift[k]).astype(BF16)
    for k in range(2):
        weight = jnp.concatenate([gathered[at[l], k] for l in range(lats)], axis=1)
        errs[k] = slot_errors(levels[slot + k], tile_counts[...], rows[k][...], weight, target[k])
    for k in range(2):
        head_halves(k, lats, place[0], errs[k], rows[k][...], turned, keep, send)
    add_back(lats, at, errs, gathered, scale, total)

    if final:

        @pl.when(step == steps - 1)
        def _():
            cols = out.shape[2]
            for s in range(tiles):
                for r in range(WH):
                    start = (r * tiles + s) * cols
                    out[s, r] = total[start : start + cols, :].astype(BF16)


def slot_group(pair, pairs, lats, place, small, tile_of, scale, shift, gathered, targets, pieces, before, after=None):
    places, width = tile_of.shape[0], scale.shape[-1]
    outs = targets.shape[-1]
    tiles = small[1].shape[1]
    piece = width // lats
    cols = places // (WH * tiles)
    smem = pl.BlockSpec(memory_space=pltpu.SMEM)
    fixed = lambda shape: pl.BlockSpec(shape, lambda i: (0,) * len(shape))
    halves = jax.ShapeDtypeStruct((2, 2, 2, pairs, outs, piece), BF16)
    half_spec = pl.BlockSpec((2, 2, 2, 1, outs, piece), lambda i: (0, 0, 0, i, 0, 0))
    level_spec = pl.BlockSpec((2, 1, width), lambda i: (i + pair, 0, 0))
    in_specs = [smem] * 4 + [
        fixed(tile_of.shape),
        level_spec,
        level_spec,
        pl.BlockSpec((lats, 2, outs, piece), lambda i: (0, i, 0, 0)),
        pl.BlockSpec((2,) + targets.shape[1:], lambda i: (i + pair, 0, 0, 0)),
    ]
    args = [place, *small, tile_of, scale, shift, gathered, targets]
    final = before is not None
    scratch = [
        pltpu.VMEM((places, width), BF16),
        pltpu.VMEM((places, width), BF16),
        pltpu.VMEM((2, places, outs), BF16),
        pltpu.VMEM((2, outs, width), BF16),
        pltpu.VMEM((places, 1), jnp.int32),
    ]
    sums = jax.ShapeDtypeStruct((places, width), F32)
    if final:
        args.extend(before)
        scratch.insert(0, pltpu.VMEM(sums.shape, F32))
        results = [jax.ShapeDtypeStruct((tiles, WH, cols, width), BF16)]
    else:
        args.extend([jnp.asarray(band_map(tiles, cols), BF16), *pieces])
        results = [
            sums,
            jax.ShapeDtypeStruct((places, width), BF16),
            jax.ShapeDtypeStruct((WH, cols, width), BF16),
        ]
    in_specs.extend(fixed(arg.shape) for arg in args[len(in_specs) :])
    if after is not None:
        args.append(after)
        in_specs.append(pl.BlockSpec(memory_space=pl.ANY))
    limit = (45 if final else 48) * 1024 * 1024
    return pl.pallas_call(
        functools.partial(slot_kernel, 2 * pair, lats, tiles, final),
        grid=(pairs,),
        out_shape=(halves, halves, *results),
        in_specs=in_specs,
        out_specs=(half_spec, half_spec, *(fixed(r.shape) for r in results)),
        scratch_shapes=scratch,
        compiler_params=pltpu.CompilerParams(vmem_limit_bytes=limit),
        cost_estimate=pl.CostEstimate(
            flops=pairs * 12 * places * width * outs, bytes_accessed=pairs * 5_000_000, transcendentals=0
        ),
        name="slot_group",
    )(*args)


def halve_kernel(keep, came, *refs):
    outs = refs[-4:]
    for k in range(2):
        for half in range(2):
            total = keep[k, half].astype(F32) + came[k, half].astype(F32)
            outs[2 * half + k][...] = total.astype(BF16)


def halve(keep, came, after):
    part = jax.ShapeDtypeStruct(keep.shape[2:], BF16)
    vmem = pl.BlockSpec(memory_space=pltpu.VMEM)
    out = pl.pallas_call(
        halve_kernel,
        out_shape=(part,) * 4,
        in_specs=[vmem, vmem] + [pl.BlockSpec(memory_space=pl.ANY)] * len(after),
        out_specs=(vmem,) * 4,
        compiler_params=pltpu.CompilerParams(vmem_limit_bytes=24 * 1024 * 1024),
        cost_estimate=pl.CostEstimate(flops=2_000_000, bytes_accessed=6_000_000, transcendentals=0),
        name="halve",
    )(keep, came, *after)
    return out[0:2], out[2:4]


def join_kernel(norm, *refs):
    out = refs[-1]
    pairs = refs[:-1]
    slot = 0
    for i in range(0, len(pairs), 4):
        for k in range(pairs[i].shape[0]):
            for kept, came in (pairs[i : i + 2], pairs[i + 2 : i + 4]):
                out[slot] = (kept[k].astype(F32) + came[k].astype(F32)) * norm
                slot += 1


def join_heads(pairs, norm):
    flat = [array for pair in pairs for array in pair]
    slots = sum(kept.shape[0] for kept, _ in pairs)
    _, outs, piece = flat[0].shape
    vmem = pl.BlockSpec(memory_space=pltpu.VMEM)
    return pl.pallas_call(
        functools.partial(join_kernel, norm),
        out_shape=jax.ShapeDtypeStruct((slots, outs, piece), F32),
        in_specs=[vmem] * len(flat),
        out_specs=vmem,
        compiler_params=pltpu.CompilerParams(vmem_limit_bytes=VMEM_LIMIT),
        cost_estimate=pl.CostEstimate(flops=1_000_000, bytes_accessed=4_000_000, transcendentals=0),
        name="join_heads",
    )(*flat)


def fast_local(
    patches, norm_gain, input_proj, output_proj, level_scale, level_shift, head_weight, targets,
    level_counts, tile_dataset, slot_level,
):
    rows, cols, width = patches.shape
    lats, tiles = lax.axis_size("lat"), lax.axis_size("var")
    slots = head_weight.shape[0]
    lat, var = lax.axis_index("lat"), lax.axis_index("var")
    place = jnp.stack([lat, var]).astype(jnp.int32)
    most = slots // 2 - 1
    flip = lambda array, bit: lax.ppermute(array, "lat", [(i, i ^ bit) for i in range(lats)])
    turned = jnp.transpose(head_weight, (0, 2, 1))
    gathered_a = lax.all_gather(turned[: 2 * most], "lat", axis=0, tiled=False)
    gathered_b = turned[None, 2 * most :]
    for bit in (4, 2, 1):
        gathered_b = jnp.concatenate([gathered_b, flip(gathered_b, bit)], axis=0)

    right = [(i, (i + 1) % tiles) for i in range(tiles)]
    up = [(i, i + 1) for i in range(lats - 1)]
    down = [(i + 1, i) for i in range(lats - 1)]
    left = lax.ppermute(patches[:, cols - HC :], "var", right)
    shifted = jnp.concatenate([left, patches[:, : cols - HC]], axis=1)
    above = lax.ppermute(shifted[HR:], "lat", up)
    below = lax.ppermute(shifted[:HR], "lat", down)
    mine = attention(place, (shifted, above, below), norm_gain, input_proj, output_proj, lats)
    pieces = [mine]
    for s in range(1, tiles):
        pieces.append(lax.ppermute(mine, "var", [(i, (i + s) % tiles) for i in range(tiles)]))

    tile_of = jnp.asarray(np.arange(rows * tiles * cols)[:, None] % (tiles * cols) // cols, jnp.int32)
    scale3, shift3 = level_scale.reshape(slots, 1, width), level_shift.reshape(slots, 1, width)
    small = (level_counts, tile_dataset, slot_level)
    add = lambda a, b: (a.astype(F32) + b.astype(F32)).astype(BF16)
    common = (lats, place, small, tile_of, scale3, shift3)
    bits = (2, 4)
    keep_a, send_a, so_far, band, latent = slot_group(
        0, most, *common, gathered_a, targets, pieces, None, gathered_b
    )
    keep_b, send_b, terms = slot_group(
        most, slots // 2 - most, *common, gathered_b, targets, None, (band, so_far)
    )
    grad_latent = lax.psum_scatter(terms, "var", scatter_dimension=0, tiled=False)
    pairs, came = [], [terms]
    for keep, send in ((keep_a, send_a), (keep_b, send_b)):
        kept, sent = halve(keep, flip(send, 1), came)
        came = [flip(sent[k], bits[k]) for k in range(2)]
        for k in range(2):
            last = flip(add(kept[k][1], came[k][1]), bits[1 - k])
            pairs.append((add(kept[k][0], came[k][0]), last))
    grad_head = join_heads(pairs, 1.0 / math.sqrt(lats * rows * tiles * cols))
    return (latent, grad_latent, jnp.transpose(grad_head, (0, 2, 1)))


def padded(array, sides, width, wrap):
    for axis, dim in sides:
        size, length = (lax.axis_size(axis), array.shape[dim])
        up = [(i, (i + 1) % size) for i in range(size if wrap else size - 1)]
        down = [(j, i) for i, j in up]
        last = lax.slice_in_dim(array, length - width, length, axis=dim)
        initial = lax.slice_in_dim(array, 0, width, axis=dim)
        before = lax.ppermute(last, axis, up)
        after = lax.ppermute(initial, axis, down)
        array = jnp.concatenate([before, array, after], axis=dim)
    return array


def layer_norm(values, gain):
    wide = values.astype(jnp.float32)
    average = jnp.mean(wide, axis=-1, keepdims=True)
    centred = wide - average
    variance = jnp.mean(centred * centred, axis=-1, keepdims=True)
    return (centred * lax.rsqrt(variance + EPS) * gain).astype(jnp.bfloat16)


def window_attention(query_ext, keyval, row_valid, heads):
    ext_rows, ext_cols, width = query_ext.shape
    head_size = width // heads
    win_rows = ext_rows // WH
    win_cols = ext_cols // WW

    def split(values, parts):
        shaped = values.reshape(win_rows, WH, win_cols, WW, parts, heads, head_size)
        return shaped.transpose(0, 2, 1, 3, 4, 5, 6).reshape(
            win_rows * win_cols, WH * WW, parts, heads, head_size
        )

    query_win = split(query_ext, 1)[:, :, 0]
    pairs = split(keyval, 2)
    key_win = pairs[:, :, 0]
    value_win = pairs[:, :, 1]
    key_mask = jnp.broadcast_to(
        row_valid.reshape(win_rows, 1, WH, 1), (win_rows, win_cols, WH, WW)
    ).reshape(win_rows * win_cols, WH * WW)
    scores = jnp.einsum(
        "wqhd,wkhd->whqk", query_win, key_win, preferred_element_type=jnp.float32
    ) / math.sqrt(head_size)
    scores = jnp.where(key_mask[:, None, None, :], scores, -jnp.inf)
    peak = jnp.max(scores, axis=-1, keepdims=True)
    weights = jnp.exp(scores - peak)
    probs = (weights / jnp.sum(weights, axis=-1, keepdims=True)).astype(jnp.bfloat16)
    mixed = jnp.einsum("whqk,wkhd->wqhd", probs, value_win, preferred_element_type=jnp.float32)
    return (
        mixed.reshape(win_rows, win_cols, WH, WW, width)
        .transpose(0, 2, 1, 3, 4)
        .reshape(ext_rows, ext_cols, width)
    )


def slot_terms(piece, target_rows, live_cols, level_scale, level_shift, heads_full):
    piece_wide = piece.astype(jnp.float32)
    rows = (
        piece_wide[None] * level_scale[:, None, None, :] + level_shift[:, None, None, :]
    ).astype(jnp.bfloat16)
    predicted = jnp.einsum("krnd,kdo->krno", rows, heads_full, preferred_element_type=jnp.float32)
    errors = ((predicted - target_rows.astype(jnp.float32)) * live_cols[:, None, :, None]).astype(
        jnp.bfloat16
    )
    back_grad = jnp.einsum("krno,kdo->krnd", errors, heads_full, preferred_element_type=jnp.float32)
    piece_grad = jnp.sum(back_grad * level_scale[:, None, None, :], axis=0)
    head_add = jnp.einsum("krnd,krno->dko", rows, errors, preferred_element_type=jnp.float32)
    return (piece_grad, head_add)


def local(
    patches,
    norm_gain,
    input_proj,
    output_proj,
    level_scale,
    level_shift,
    head_weight,
    targets,
    level_counts,
    tile_dataset,
    slot_level,
):
    band_rows, band_cols, width = patches.shape
    half_rows = WH // 2
    half_cols = WW // 2
    lat_count = lax.axis_size("lat")
    var_count = lax.axis_size("var")
    lat_place = lax.axis_index("lat")
    ext_rows = band_rows + WH
    ext_cols = band_cols + WW
    extended = padded(patches, (("lat", 0),), half_rows, False)
    extended = padded(extended, (("var", 1),), half_cols, True)
    normed_ext = layer_norm(extended, norm_gain)
    keyval = jnp.dot(
        normed_ext.reshape(-1, width), input_proj[:, width:], preferred_element_type=jnp.float32
    )
    keyval = keyval.astype(jnp.bfloat16).reshape(ext_rows, ext_cols, 2 * width)
    normed = normed_ext[half_rows : half_rows + band_rows, half_cols : half_cols + band_cols]
    queries = jnp.dot(
        normed.reshape(-1, width), input_proj[:, :width], preferred_element_type=jnp.float32
    )
    queries = queries.astype(jnp.bfloat16).reshape(band_rows, band_cols, width)
    query_ext = jnp.pad(queries, ((half_rows, WH - half_rows), (half_cols, WW - half_cols), (0, 0)))
    global_row = lat_place * band_rows - half_rows + jnp.arange(ext_rows, dtype=jnp.int32)
    row_valid = (global_row >= 0) & (global_row < lat_count * band_rows)
    mixed = window_attention(query_ext, keyval, row_valid, HEADS)
    attn = mixed[half_rows : half_rows + band_rows, half_cols : half_cols + band_cols].astype(
        jnp.bfloat16
    )
    update = jnp.dot(
        attn.reshape(-1, width), output_proj, preferred_element_type=jnp.float32
    ).reshape(band_rows, band_cols, width)
    latent = (patches.astype(jnp.float32) + update).astype(jnp.bfloat16)
    dataset_row = tile_dataset[0]
    dataset_ids = jnp.arange(level_counts.shape[0], dtype=jnp.int32)
    tile_levels = jnp.sum(
        jnp.where(dataset_row[:, None] == dataset_ids[None, :], level_counts[None, :], 0), axis=1
    )
    live_tiles = (slot_level[None, :] < tile_levels[:, None]).astype(jnp.float32)
    heads_full = lax.all_gather(head_weight, "lat", axis=1, tiled=True)
    tile_ids = jnp.arange(var_count, dtype=jnp.int32)
    piece = lax.all_gather(latent, "var", axis=1, tiled=True)
    piece_cols = piece.shape[1]
    column_tile = jnp.arange(piece_cols, dtype=jnp.int32) // band_cols
    onehot = (column_tile[:, None] == tile_ids[None, :]).astype(jnp.float32)
    column_live = jnp.dot(onehot, live_tiles)
    piece_grad, head_add = slot_terms(
        piece, targets, column_live.T, level_scale, level_shift, heads_full
    )
    latent_terms = piece_grad
    latent_terms, head_terms = (latent_terms, head_add)
    grad_latent = lax.psum_scatter(
        latent_terms.astype(jnp.bfloat16), "var", scatter_dimension=1, tiled=True
    )
    head_terms = head_terms * (1.0 / math.sqrt(lat_count * band_rows * var_count * band_cols))
    mine = lax.psum_scatter(
        head_terms.astype(jnp.bfloat16), "lat", scatter_dimension=0, tiled=True
    ).astype(jnp.float32)
    grad_head = jnp.transpose(mine, (1, 0, 2))
    return (latent, grad_latent, grad_head)


def solution(mesh):
    in_specs = (
        P("lat", "var", None),
        P(),
        P(),
        P(),
        P("var", None),
        P("var", None),
        P("var", "lat", None),
        P("var", "lat", None, None),
        P(),
        P("lat", None),
        P("var"),
    )
    fast = mesh.shape["lat"] == 8 and mesh.shape["var"] == 4
    body = fast_local if fast else local
    out_specs = (P("lat", "var", None), P("lat", "var", None), P("var", "lat", None))
    return jax.shard_map(body, mesh=mesh, in_specs=in_specs, out_specs=out_specs, check_vma=False)
```

```python
import functools
import math

import jax
import jax.numpy as jnp
import numpy as np
from jax import lax
from jax.experimental import pallas as pl
from jax.experimental.pallas import tpu as pltpu
from jax.sharding import PartitionSpec as P

HEADS = 16
WH = 6
WW = 12
EPS = 1e-05
HR = WH // 2
HC = WW // 2
QP = 48
VMEM_LIMIT = 48 * 1024 * 1024
F32 = jnp.float32
BF16 = jnp.bfloat16


def gather_maps(cols):
    win_cols = cols // WW
    windows = 2 * win_cols
    into = np.zeros((windows * 2 * QP, 2 * WH * cols), np.float32)
    back = np.zeros((WH * cols, windows * QP), np.float32)
    for win in range(windows):
        win_row, win_col = divmod(win, win_cols)
        for row in range(HR):
            for c in range(WW):
                own = (win_row * HR + row) * cols + win_col * WW + c
                slot = row * WW + c
                into[win * 2 * QP + slot, own] = 1
                into[win * 2 * QP + QP + slot, WH * cols + own] = 1
                back[own, win * QP + slot] = 1
    return into, back


def attention_kernel(
    bands,
    place,
    own,
    above,
    below,
    gain_hbm,
    maps_hbm,
    in_hbm,
    out_hbm,
    out,
    raw,
    qkv,
    attn,
    gain,
    maps,
    proj_in,
    proj_out,
    sems,
):
    moves = [
        pltpu.make_async_copy(src, dst, sems.at[i])
        for i, (src, dst) in enumerate(
            ((gain_hbm, gain), (maps_hbm, maps), (in_hbm, proj_in), (out_hbm, proj_out))
        )
    ]
    for move in moves:
        move.start()
    cols, width = own.shape[1], own.shape[2]
    win_cols = cols // WW
    windows = 2 * win_cols
    slots = windows * 2 * QP
    head_size = width // HEADS
    quad = 256 // head_size
    size = WH * cols
    start = 0
    for ref in (own, above, below):
        count = ref.shape[0] * cols
        raw[start : start + count, :] = ref[...].astype(F32).reshape(count, width)
        start += count
    moves[0].wait()
    wide = raw[...]
    average = jnp.mean(wide, axis=-1, keepdims=True)
    centred = wide - average
    variance = jnp.mean(centred * centred, axis=-1, keepdims=True)
    normed = (centred * lax.rsqrt(variance + EPS) * gain[...]).astype(BF16)
    moves[1].wait()
    win_x = jnp.dot(maps[0:slots, :], normed, preferred_element_type=F32).astype(BF16)
    moves[2].wait()
    step = 512
    for j in range(3 * width // step):
        part = slice(j * step, (j + 1) * step)
        qkv[:, part] = jnp.dot(win_x, proj_in[:, part], preferred_element_type=F32).astype(BF16)
    lane = lax.broadcasted_iota(jnp.int32, (1, 256), 1) // head_size
    heads = [jnp.where(lane == h, 1.0, 0.0) for h in range(quad)]
    key_id = lax.broadcasted_iota(jnp.int32, (1, 2 * QP), 1)
    scale = 1.0 / math.sqrt(head_size)
    for win in range(windows):
        win_row = win // win_cols
        edge = 0 if win_row == 0 else bands - 1
        has_halo = place[0] != edge
        halo_keys = jnp.logical_and(key_id >= QP, key_id < QP + HR * WW)
        valid = jnp.logical_or(key_id < HR * WW, jnp.logical_and(halo_keys, has_halo))
        bias = jnp.where(valid, 0.0, -1e30)
        row0 = win * 2 * QP
        for g in range(width // 256):
            lanes = slice(g * 256, (g + 1) * 256)
            query = qkv[row0 : row0 + QP, lanes].astype(F32) * scale
            stacked = jnp.concatenate([query * h for h in heads], axis=0).astype(BF16)
            key = qkv[row0 : row0 + 2 * QP, width + g * 256 : width + (g + 1) * 256]
            value = qkv[row0 : row0 + 2 * QP, 2 * width + g * 256 : 2 * width + (g + 1) * 256]
            scores = (
                lax.dot_general(
                    stacked, key, (((1,), (1,)), ((), ())), preferred_element_type=F32
                )
                + bias
            )
            weights = jnp.exp(scores - jnp.max(scores, axis=-1, keepdims=True))
            probs = (weights / jnp.sum(weights, axis=-1, keepdims=True)).astype(BF16)
            mixed = jnp.dot(probs, value, preferred_element_type=F32)
            chosen = mixed[0:QP] * heads[0]
            for h in range(1, quad):
                chosen = chosen + mixed[h * QP : (h + 1) * QP] * heads[h]
            attn[win * QP : (win + 1) * QP, lanes] = chosen.astype(BF16)
    back = maps[slots : slots + size, 0 : windows * QP]
    ordered = jnp.dot(back, attn[...], preferred_element_type=F32).astype(BF16)
    moves[3].wait()
    update = jnp.dot(ordered, proj_out[...], preferred_element_type=F32)
    out[...] = (raw[0:size, :] + update).astype(BF16)


def attention(place, pieces, gain, proj_in, proj_out, bands):
    rows, cols, width = pieces[0].shape
    into, back = gather_maps(cols)
    total = into.shape[1]
    windows = 2 * (cols // WW)
    back = np.pad(back, ((0, 0), (0, total - back.shape[1])))
    maps = np.concatenate([into, back])
    vmem = pl.BlockSpec(memory_space=pltpu.VMEM)
    hbm = pl.BlockSpec(memory_space=pltpu.HBM)
    return pl.pallas_call(
        functools.partial(attention_kernel, bands),
        out_shape=jax.ShapeDtypeStruct((rows * cols, width), BF16),
        in_specs=[pl.BlockSpec(memory_space=pltpu.SMEM)] + [vmem] * 3 + [hbm] * 4,
        out_specs=vmem,
        scratch_shapes=[
            pltpu.VMEM((total, width), F32),
            pltpu.VMEM((windows * 2 * QP, 3 * width), BF16),
            pltpu.VMEM((windows * QP, width), BF16),
            pltpu.VMEM((1, width), F32),
            pltpu.VMEM(maps.shape, BF16),
            pltpu.VMEM(proj_in.shape, BF16),
            pltpu.VMEM(proj_out.shape, BF16),
            pltpu.SemaphoreType.DMA((4,)),
        ],
        compiler_params=pltpu.CompilerParams(vmem_limit_bytes=53 * 1024 * 1024),
        cost_estimate=pl.CostEstimate(
            flops=6_000_000_000, bytes_accessed=12_000_000, transcendentals=400_000
        ),
        name="window_attention",
    )(
        place,
        *pieces,
        gain.reshape(1, width),
        jnp.asarray(maps, BF16),
        proj_in,
        proj_out,
    )


def band_map(tiles, cols):
    wide = tiles * cols
    chosen = np.zeros((WH * wide, WH * wide), np.float32)
    for r in range(WH):
        for c in range(wide):
            tile, at = divmod((c + HC) % wide, cols)
            chosen[r * wide + c, tile * WH * cols + r * cols + at] = 1
    return chosen


def band_kernel(tiles, cols, place, chosen, *refs):
    pieces, (band, latent, laid, wide) = refs[:tiles], refs[tiles:]
    size = WH * cols
    var = place[1]
    for s in range(tiles):
        tile = lax.rem(var + tiles - s, tiles)
        laid[pl.ds(pl.multiple_of(tile * size, 16), size), :] = pieces[s][...]
    wide[...] = jnp.dot(chosen[...], laid[...], preferred_element_type=F32)
    band[...] = wide[...].astype(BF16)
    for r in range(WH):
        start = pl.multiple_of(r * tiles * cols + var * cols, 8)
        latent[r] = wide[pl.ds(start, cols), :].astype(BF16)


def band_latents(place, pieces, cols):
    tiles = len(pieces)
    width = pieces[0].shape[1]
    total = WH * tiles * cols
    vmem = pl.BlockSpec(memory_space=pltpu.VMEM)
    return pl.pallas_call(
        functools.partial(band_kernel, tiles, cols),
        out_shape=(
            jax.ShapeDtypeStruct((total, width), BF16),
            jax.ShapeDtypeStruct((WH, cols, width), BF16),
        ),
        in_specs=[pl.BlockSpec(memory_space=pltpu.SMEM)] + [vmem] * (tiles + 1),
        out_specs=(vmem, vmem),
        scratch_shapes=[pltpu.VMEM((total, width), BF16), pltpu.VMEM((total, width), F32)],
        compiler_params=pltpu.CompilerParams(vmem_limit_bytes=VMEM_LIMIT),
        cost_estimate=pl.CostEstimate(
            flops=2 * total * total * width, bytes_accessed=4_000_000, transcendentals=0
        ),
        name="band_latents",
    )(place, jnp.asarray(band_map(tiles, cols), BF16), *pieces)


def slot_errors(level, tile_counts, rows, weight, target):
    predicted = lax.dot_general(
        rows, weight, (((1,), (1,)), ((), ())), preferred_element_type=F32
    )
    live = jnp.where(level < tile_counts, 1.0, 0.0)
    diff = predicted - target.astype(F32).reshape(predicted.shape)
    return (diff * live).astype(BF16)


def head_halves(k, lats, lat, errors, rows, turned, keep, send):
    turned[k] = lax.dot_general(
        errors, rows, (((0,), (0,)), ((), ())), preferred_element_type=F32
    ).astype(BF16)
    piece = turned.shape[-1] // lats
    for q in range(lats):
        core, x, y = q & 1, (q >> 1) & 1, (q >> 2) & 1
        outer, inner = (x, y) if k == 0 else (y, x)
        start = pl.multiple_of(jnp.bitwise_xor(lat, q) * piece, piece)
        to = send if core else keep
        to[k, outer, inner, 0] = turned[k, :, pl.ds(start, piece)]


def add_back(lats, errs, gathered, scale, total):
    piece = gathered.shape[-1]
    for l in range(0, lats, 2):
        lanes = slice(l * piece, (l + 2) * piece)
        term = 0.0
        for k in range(2):
            weight = jnp.concatenate([gathered[l, k], gathered[l + 1, k]], axis=1)
            factor = scale[k][:, lanes]
            term = term + jnp.dot(errs[k], weight, preferred_element_type=F32) * factor
        total[:, lanes] += term


def slot_kernel(
    first_slot,
    lats,
    tiles,
    final,
    place,
    counts,
    datasets,
    levels,
    tile_of,
    scale,
    shift,
    gathered,
    target,
    *refs,
):
    if final:
        band, before, keep, send, out, total, rows0, rows1, errs, turned, tile_counts = refs
    else:
        band, keep, send, total, rows0, rows1, errs, turned, tile_counts = refs
    rows = (rows0, rows1)
    step, steps = pl.program_id(0), pl.num_programs(0)
    slot = first_slot + 2 * step

    @pl.when(step == 0)
    def _():
        total[...] = before[...] if final else jnp.zeros_like(total)
        tile = tile_of[...]
        wanted = jnp.zeros_like(tile)
        for t in range(tiles):
            wanted = jnp.where(tile == t, counts[datasets[0, t]], wanted)
        tile_counts[...] = wanted

    for k in range(2):
        rows[k][...] = (band[...].astype(F32) * scale[k] + shift[k]).astype(BF16)
    for k in range(2):
        weight = jnp.concatenate([gathered[l, k] for l in range(lats)], axis=1)
        errs[k] = slot_errors(levels[slot + k], tile_counts[...], rows[k][...], weight, target[k])
    for k in range(2):
        head_halves(k, lats, place[0], errs[k], rows[k][...], turned, keep, send)
    add_back(lats, errs, gathered, scale, total)

    if final:

        @pl.when(step == steps - 1)
        def _():
            cols = out.shape[2]
            for s in range(tiles):
                for r in range(WH):
                    start = (r * tiles + s) * cols
                    out[s, r] = total[start : start + cols, :].astype(BF16)


def slot_group(pair, pairs, lats, place, small, tile_of, scale, shift, gathered, targets, band, before):
    places, width = tile_of.shape[0], scale.shape[-1]
    outs = targets.shape[-1]
    tiles = small[1].shape[1]
    piece = width // lats
    cols = places // (WH * tiles)
    smem = pl.BlockSpec(memory_space=pltpu.SMEM)
    fixed = lambda shape: pl.BlockSpec(shape, lambda i: (0,) * len(shape))
    halves = jax.ShapeDtypeStruct((2, 2, 2, pairs, outs, piece), BF16)
    half_spec = pl.BlockSpec((2, 2, 2, 1, outs, piece), lambda i: (0, 0, 0, i, 0, 0))
    level_spec = pl.BlockSpec((2, 1, width), lambda i: (i + pair, 0, 0))
    in_specs = [smem] * 4 + [
        fixed(tile_of.shape),
        level_spec,
        level_spec,
        pl.BlockSpec((lats, 2, outs, piece), lambda i: (0, i + pair, 0, 0)),
        pl.BlockSpec((2,) + targets.shape[1:], lambda i: (i + pair, 0, 0, 0)),
    ]
    args = [place, *small, tile_of, scale, shift, gathered, targets, band]
    final = before is not None
    scratch = [
        pltpu.VMEM((places, width), BF16),
        pltpu.VMEM((places, width), BF16),
        pltpu.VMEM((2, places, outs), BF16),
        pltpu.VMEM((2, outs, width), BF16),
        pltpu.VMEM((places, 1), jnp.int32),
    ]
    sums = jax.ShapeDtypeStruct((places, width), F32)
    if final:
        args.append(before)
        scratch.insert(0, pltpu.VMEM(sums.shape, F32))
        results = [jax.ShapeDtypeStruct((tiles, WH, cols, width), BF16)]
    else:
        results = [sums]
    in_specs.extend(fixed(arg.shape) for arg in args[len(in_specs) :])
    limit = (45 if final else 48) * 1024 * 1024
    return pl.pallas_call(
        functools.partial(slot_kernel, 2 * pair, lats, tiles, final),
        grid=(pairs,),
        out_shape=(halves, halves, *results),
        in_specs=in_specs,
        out_specs=(half_spec, half_spec, *(fixed(r.shape) for r in results)),
        scratch_shapes=scratch,
        compiler_params=pltpu.CompilerParams(vmem_limit_bytes=limit),
        cost_estimate=pl.CostEstimate(
            flops=pairs * 12 * places * width * outs, bytes_accessed=pairs * 5_000_000, transcendentals=0
        ),
        name="slot_group",
    )(*args)


def halve_kernel(*refs):
    groups, outs = refs[:-4], refs[-4:]
    start = 0
    for keep, came in zip(groups[0::2], groups[1::2]):
        pairs = keep.shape[3]
        for k in range(2):
            for half in range(2):
                total = keep[k, half].astype(F32) + came[k, half].astype(F32)
                outs[2 * half + k][:, start : start + pairs] = total.astype(BF16)
        start += pairs


def halve(groups):
    flat = [array for group in groups for array in group]
    pairs = sum(keep.shape[3] for keep, _ in groups)
    shape = flat[0].shape
    part = jax.ShapeDtypeStruct((2, pairs) + shape[4:], BF16)
    vmem = pl.BlockSpec(memory_space=pltpu.VMEM)
    out = pl.pallas_call(
        halve_kernel,
        out_shape=(part,) * 4,
        in_specs=[vmem] * len(flat),
        out_specs=(vmem,) * 4,
        compiler_params=pltpu.CompilerParams(vmem_limit_bytes=24 * 1024 * 1024),
        cost_estimate=pl.CostEstimate(flops=2_000_000, bytes_accessed=6_000_000, transcendentals=0),
        name="halve",
    )(*flat)
    return out[0:2], out[2:4]


def join_kernel(norm, *refs):
    out = refs[-1]
    pairs = refs[:-1]
    slot = 0
    for i in range(0, len(pairs), 4):
        for k in range(pairs[i].shape[0]):
            for kept, came in (pairs[i : i + 2], pairs[i + 2 : i + 4]):
                out[slot] = (kept[k].astype(F32) + came[k].astype(F32)) * norm
                slot += 1


def join_heads(pairs, norm):
    flat = [array for pair in pairs for array in pair]
    slots = sum(kept.shape[0] for kept, _ in pairs)
    _, outs, piece = flat[0].shape
    vmem = pl.BlockSpec(memory_space=pltpu.VMEM)
    return pl.pallas_call(
        functools.partial(join_kernel, norm),
        out_shape=jax.ShapeDtypeStruct((slots, outs, piece), F32),
        in_specs=[vmem] * len(flat),
        out_specs=vmem,
        compiler_params=pltpu.CompilerParams(vmem_limit_bytes=VMEM_LIMIT),
        cost_estimate=pl.CostEstimate(flops=1_000_000, bytes_accessed=4_000_000, transcendentals=0),
        name="join_heads",
    )(*flat)


def fast_local(
    patches, norm_gain, input_proj, output_proj, level_scale, level_shift, head_weight, targets,
    level_counts, tile_dataset, slot_level,
):
    rows, cols, width = patches.shape
    lats, tiles = lax.axis_size("lat"), lax.axis_size("var")
    slots = head_weight.shape[0]
    lat, var = lax.axis_index("lat"), lax.axis_index("var")
    place = jnp.stack([lat, var]).astype(jnp.int32)
    gathered = lax.all_gather(jnp.transpose(head_weight, (0, 2, 1)), "lat", axis=0, tiled=False)

    right = [(i, (i + 1) % tiles) for i in range(tiles)]
    up = [(i, i + 1) for i in range(lats - 1)]
    down = [(i + 1, i) for i in range(lats - 1)]
    left = lax.ppermute(patches[:, cols - HC :], "var", right)
    shifted = jnp.concatenate([left, patches[:, : cols - HC]], axis=1)
    above = lax.ppermute(shifted[HR:], "lat", up)
    below = lax.ppermute(shifted[:HR], "lat", down)
    mine = attention(place, (shifted, above, below), norm_gain, input_proj, output_proj, lats)
    pieces = [mine]
    for s in range(1, tiles):
        pieces.append(lax.ppermute(mine, "var", [(i, (i + s) % tiles) for i in range(tiles)]))

    band, latent = band_latents(place, pieces, cols)
    tile_of = jnp.asarray(np.arange(rows * tiles * cols)[:, None] % (tiles * cols) // cols, jnp.int32)
    scale3, shift3 = level_scale.reshape(slots, 1, width), level_shift.reshape(slots, 1, width)
    small = (level_counts, tile_dataset, slot_level)
    flip = lambda array, bit: lax.ppermute(array, "lat", [(i, i ^ bit) for i in range(lats)])
    add = lambda a, b: (a.astype(F32) + b.astype(F32)).astype(BF16)
    common = (lats, place, small, tile_of, scale3, shift3, gathered, targets, band)
    most = slots // 2 - 1
    bits = (2, 4)
    keep_a, send_a, so_far = slot_group(0, most, *common, None)
    keep_b, send_b, terms = slot_group(most, slots // 2 - most, *common, so_far)
    grad_latent = lax.psum_scatter(terms, "var", scatter_dimension=0, tiled=False)
    kept, sent = halve([(keep_a, flip(send_a, 1)), (keep_b, flip(send_b, 1))])
    came = [flip(sent[k], bits[k]) for k in range(2)]
    pairs = []
    for k in range(2):
        last = flip(add(kept[k][1], came[k][1]), bits[1 - k])
        pairs.append((add(kept[k][0], came[k][0]), last))
    grad_head = join_heads(pairs, 1.0 / math.sqrt(lats * rows * tiles * cols))
    return (latent, grad_latent, jnp.transpose(grad_head, (0, 2, 1)))


def padded(array, sides, width, wrap):
    for axis, dim in sides:
        size, length = (lax.axis_size(axis), array.shape[dim])
        up = [(i, (i + 1) % size) for i in range(size if wrap else size - 1)]
        down = [(j, i) for i, j in up]
        last = lax.slice_in_dim(array, length - width, length, axis=dim)
        initial = lax.slice_in_dim(array, 0, width, axis=dim)
        before = lax.ppermute(last, axis, up)
        after = lax.ppermute(initial, axis, down)
        array = jnp.concatenate([before, array, after], axis=dim)
    return array


def layer_norm(values, gain):
    wide = values.astype(jnp.float32)
    average = jnp.mean(wide, axis=-1, keepdims=True)
    centred = wide - average
    variance = jnp.mean(centred * centred, axis=-1, keepdims=True)
    return (centred * lax.rsqrt(variance + EPS) * gain).astype(jnp.bfloat16)


def window_attention(query_ext, keyval, row_valid, heads):
    ext_rows, ext_cols, width = query_ext.shape
    head_size = width // heads
    win_rows = ext_rows // WH
    win_cols = ext_cols // WW

    def split(values, parts):
        shaped = values.reshape(win_rows, WH, win_cols, WW, parts, heads, head_size)
        return shaped.transpose(0, 2, 1, 3, 4, 5, 6).reshape(
            win_rows * win_cols, WH * WW, parts, heads, head_size
        )

    query_win = split(query_ext, 1)[:, :, 0]
    pairs = split(keyval, 2)
    key_win = pairs[:, :, 0]
    value_win = pairs[:, :, 1]
    key_mask = jnp.broadcast_to(
        row_valid.reshape(win_rows, 1, WH, 1), (win_rows, win_cols, WH, WW)
    ).reshape(win_rows * win_cols, WH * WW)
    scores = jnp.einsum(
        "wqhd,wkhd->whqk", query_win, key_win, preferred_element_type=jnp.float32
    ) / math.sqrt(head_size)
    scores = jnp.where(key_mask[:, None, None, :], scores, -jnp.inf)
    peak = jnp.max(scores, axis=-1, keepdims=True)
    weights = jnp.exp(scores - peak)
    probs = (weights / jnp.sum(weights, axis=-1, keepdims=True)).astype(jnp.bfloat16)
    mixed = jnp.einsum("whqk,wkhd->wqhd", probs, value_win, preferred_element_type=jnp.float32)
    return (
        mixed.reshape(win_rows, win_cols, WH, WW, width)
        .transpose(0, 2, 1, 3, 4)
        .reshape(ext_rows, ext_cols, width)
    )


def slot_terms(piece, target_rows, live_cols, level_scale, level_shift, heads_full):
    piece_wide = piece.astype(jnp.float32)
    rows = (
        piece_wide[None] * level_scale[:, None, None, :] + level_shift[:, None, None, :]
    ).astype(jnp.bfloat16)
    predicted = jnp.einsum("krnd,kdo->krno", rows, heads_full, preferred_element_type=jnp.float32)
    errors = ((predicted - target_rows.astype(jnp.float32)) * live_cols[:, None, :, None]).astype(
        jnp.bfloat16
    )
    back_grad = jnp.einsum("krno,kdo->krnd", errors, heads_full, preferred_element_type=jnp.float32)
    piece_grad = jnp.sum(back_grad * level_scale[:, None, None, :], axis=0)
    head_add = jnp.einsum("krnd,krno->dko", rows, errors, preferred_element_type=jnp.float32)
    return (piece_grad, head_add)


def local(
    patches,
    norm_gain,
    input_proj,
    output_proj,
    level_scale,
    level_shift,
    head_weight,
    targets,
    level_counts,
    tile_dataset,
    slot_level,
):
    band_rows, band_cols, width = patches.shape
    half_rows = WH // 2
    half_cols = WW // 2
    lat_count = lax.axis_size("lat")
    var_count = lax.axis_size("var")
    lat_place = lax.axis_index("lat")
    ext_rows = band_rows + WH
    ext_cols = band_cols + WW
    extended = padded(patches, (("lat", 0),), half_rows, False)
    extended = padded(extended, (("var", 1),), half_cols, True)
    normed_ext = layer_norm(extended, norm_gain)
    keyval = jnp.dot(
        normed_ext.reshape(-1, width), input_proj[:, width:], preferred_element_type=jnp.float32
    )
    keyval = keyval.astype(jnp.bfloat16).reshape(ext_rows, ext_cols, 2 * width)
    normed = normed_ext[half_rows : half_rows + band_rows, half_cols : half_cols + band_cols]
    queries = jnp.dot(
        normed.reshape(-1, width), input_proj[:, :width], preferred_element_type=jnp.float32
    )
    queries = queries.astype(jnp.bfloat16).reshape(band_rows, band_cols, width)
    query_ext = jnp.pad(queries, ((half_rows, WH - half_rows), (half_cols, WW - half_cols), (0, 0)))
    global_row = lat_place * band_rows - half_rows + jnp.arange(ext_rows, dtype=jnp.int32)
    row_valid = (global_row >= 0) & (global_row < lat_count * band_rows)
    mixed = window_attention(query_ext, keyval, row_valid, HEADS)
    attn = mixed[half_rows : half_rows + band_rows, half_cols : half_cols + band_cols].astype(
        jnp.bfloat16
    )
    update = jnp.dot(
        attn.reshape(-1, width), output_proj, preferred_element_type=jnp.float32
    ).reshape(band_rows, band_cols, width)
    latent = (patches.astype(jnp.float32) + update).astype(jnp.bfloat16)
    dataset_row = tile_dataset[0]
    dataset_ids = jnp.arange(level_counts.shape[0], dtype=jnp.int32)
    tile_levels = jnp.sum(
        jnp.where(dataset_row[:, None] == dataset_ids[None, :], level_counts[None, :], 0), axis=1
    )
    live_tiles = (slot_level[None, :] < tile_levels[:, None]).astype(jnp.float32)
    heads_full = lax.all_gather(head_weight, "lat", axis=1, tiled=True)
    tile_ids = jnp.arange(var_count, dtype=jnp.int32)
    piece = lax.all_gather(latent, "var", axis=1, tiled=True)
    piece_cols = piece.shape[1]
    column_tile = jnp.arange(piece_cols, dtype=jnp.int32) // band_cols
    onehot = (column_tile[:, None] == tile_ids[None, :]).astype(jnp.float32)
    column_live = jnp.dot(onehot, live_tiles)
    piece_grad, head_add = slot_terms(
        piece, targets, column_live.T, level_scale, level_shift, heads_full
    )
    latent_terms = piece_grad
    latent_terms, head_terms = (latent_terms, head_add)
    grad_latent = lax.psum_scatter(
        latent_terms.astype(jnp.bfloat16), "var", scatter_dimension=1, tiled=True
    )
    head_terms = head_terms * (1.0 / math.sqrt(lat_count * band_rows * var_count * band_cols))
    mine = lax.psum_scatter(
        head_terms.astype(jnp.bfloat16), "lat", scatter_dimension=0, tiled=True
    ).astype(jnp.float32)
    grad_head = jnp.transpose(mine, (1, 0, 2))
    return (latent, grad_latent, grad_head)


def solution(mesh):
    in_specs = (
        P("lat", "var", None),
        P(),
        P(),
        P(),
        P("var", None),
        P("var", None),
        P("var", "lat", None),
        P("var", "lat", None, None),
        P(),
        P("lat", None),
        P("var"),
    )
    fast = mesh.shape["lat"] == 8 and mesh.shape["var"] == 4
    body = fast_local if fast else local
    out_specs = (P("lat", "var", None), P("lat", "var", None), P("var", "lat", None))
    return jax.shard_map(body, mesh=mesh, in_specs=in_specs, out_specs=out_specs, check_vma=False)
```

```python
import functools
import math

import jax
import jax.numpy as jnp
import numpy as np
from jax import lax
from jax.experimental import pallas as pl
from jax.experimental.pallas import tpu as pltpu
from jax.sharding import PartitionSpec as P

HEADS = 16
WH = 6
WW = 12
EPS = 1e-05
HR = WH // 2
HC = WW // 2
QP = 48
VMEM_LIMIT = 48 * 1024 * 1024
F32 = jnp.float32
BF16 = jnp.bfloat16


def gather_maps(cols):
    win_cols = cols // WW
    windows = 2 * win_cols
    into = np.zeros((windows * 2 * QP, 2 * WH * cols), np.float32)
    back = np.zeros((WH * cols, windows * QP), np.float32)
    for win in range(windows):
        win_row, win_col = divmod(win, win_cols)
        for row in range(HR):
            for c in range(WW):
                own = (win_row * HR + row) * cols + win_col * WW + c
                slot = row * WW + c
                into[win * 2 * QP + slot, own] = 1
                into[win * 2 * QP + QP + slot, WH * cols + own] = 1
                back[own, win * QP + slot] = 1
    return into, back


def attention_kernel(
    bands,
    place,
    own,
    above,
    below,
    gain_hbm,
    maps_hbm,
    in_hbm,
    out_hbm,
    out,
    raw,
    qkv,
    attn,
    gain,
    maps,
    proj_in,
    proj_out,
    sems,
):
    moves = [
        pltpu.make_async_copy(src, dst, sems.at[i])
        for i, (src, dst) in enumerate(
            ((gain_hbm, gain), (maps_hbm, maps), (in_hbm, proj_in), (out_hbm, proj_out))
        )
    ]
    for move in moves:
        move.start()
    cols, width = own.shape[1], own.shape[2]
    win_cols = cols // WW
    windows = 2 * win_cols
    slots = windows * 2 * QP
    head_size = width // HEADS
    quad = 256 // head_size
    size = WH * cols
    start = 0
    for ref in (own, above, below):
        count = ref.shape[0] * cols
        raw[start : start + count, :] = ref[...].astype(F32).reshape(count, width)
        start += count
    moves[0].wait()
    wide = raw[...]
    average = jnp.mean(wide, axis=-1, keepdims=True)
    centred = wide - average
    variance = jnp.mean(centred * centred, axis=-1, keepdims=True)
    normed = (centred * lax.rsqrt(variance + EPS) * gain[...]).astype(BF16)
    moves[1].wait()
    win_x = jnp.dot(maps[0:slots, :], normed, preferred_element_type=F32).astype(BF16)
    moves[2].wait()
    step = 512
    for j in range(3 * width // step):
        part = slice(j * step, (j + 1) * step)
        qkv[:, part] = jnp.dot(win_x, proj_in[:, part], preferred_element_type=F32).astype(BF16)
    lane = lax.broadcasted_iota(jnp.int32, (1, 256), 1) // head_size
    heads = [jnp.where(lane == h, 1.0, 0.0) for h in range(quad)]
    key_id = lax.broadcasted_iota(jnp.int32, (1, 2 * QP), 1)
    scale = 1.0 / math.sqrt(head_size)
    for win in range(windows):
        win_row = win // win_cols
        edge = 0 if win_row == 0 else bands - 1
        has_halo = place[0] != edge
        halo_keys = jnp.logical_and(key_id >= QP, key_id < QP + HR * WW)
        valid = jnp.logical_or(key_id < HR * WW, jnp.logical_and(halo_keys, has_halo))
        bias = jnp.where(valid, 0.0, -1e30)
        row0 = win * 2 * QP
        for g in range(width // 256):
            lanes = slice(g * 256, (g + 1) * 256)
            query = qkv[row0 : row0 + QP, lanes].astype(F32) * scale
            stacked = jnp.concatenate([query * h for h in heads], axis=0).astype(BF16)
            key = qkv[row0 : row0 + 2 * QP, width + g * 256 : width + (g + 1) * 256]
            value = qkv[row0 : row0 + 2 * QP, 2 * width + g * 256 : 2 * width + (g + 1) * 256]
            scores = (
                lax.dot_general(
                    stacked, key, (((1,), (1,)), ((), ())), preferred_element_type=F32
                )
                + bias
            )
            weights = jnp.exp(scores - jnp.max(scores, axis=-1, keepdims=True))
            probs = (weights / jnp.sum(weights, axis=-1, keepdims=True)).astype(BF16)
            mixed = jnp.dot(probs, value, preferred_element_type=F32)
            chosen = mixed[0:QP] * heads[0]
            for h in range(1, quad):
                chosen = chosen + mixed[h * QP : (h + 1) * QP] * heads[h]
            attn[win * QP : (win + 1) * QP, lanes] = chosen.astype(BF16)
    back = maps[slots : slots + size, 0 : windows * QP]
    ordered = jnp.dot(back, attn[...], preferred_element_type=F32).astype(BF16)
    moves[3].wait()
    update = jnp.dot(ordered, proj_out[...], preferred_element_type=F32)
    out[...] = (raw[0:size, :] + update).astype(BF16)


def attention(place, pieces, gain, proj_in, proj_out, bands):
    rows, cols, width = pieces[0].shape
    into, back = gather_maps(cols)
    total = into.shape[1]
    windows = 2 * (cols // WW)
    back = np.pad(back, ((0, 0), (0, total - back.shape[1])))
    maps = np.concatenate([into, back])
    vmem = pl.BlockSpec(memory_space=pltpu.VMEM)
    hbm = pl.BlockSpec(memory_space=pltpu.HBM)
    return pl.pallas_call(
        functools.partial(attention_kernel, bands),
        out_shape=jax.ShapeDtypeStruct((rows * cols, width), BF16),
        in_specs=[pl.BlockSpec(memory_space=pltpu.SMEM)] + [vmem] * 3 + [hbm] * 4,
        out_specs=vmem,
        scratch_shapes=[
            pltpu.VMEM((total, width), F32),
            pltpu.VMEM((windows * 2 * QP, 3 * width), BF16),
            pltpu.VMEM((windows * QP, width), BF16),
            pltpu.VMEM((1, width), F32),
            pltpu.VMEM(maps.shape, BF16),
            pltpu.VMEM(proj_in.shape, BF16),
            pltpu.VMEM(proj_out.shape, BF16),
            pltpu.SemaphoreType.DMA((4,)),
        ],
        compiler_params=pltpu.CompilerParams(vmem_limit_bytes=53 * 1024 * 1024),
        cost_estimate=pl.CostEstimate(
            flops=6_000_000_000, bytes_accessed=12_000_000, transcendentals=400_000
        ),
        name="window_attention",
    )(
        place,
        *pieces,
        gain.reshape(1, width),
        jnp.asarray(maps, BF16),
        proj_in,
        proj_out,
    )


def band_map(tiles, cols):
    wide = tiles * cols
    chosen = np.zeros((WH * wide, WH * wide), np.float32)
    for r in range(WH):
        for c in range(wide):
            tile, at = divmod((c + HC) % wide, cols)
            chosen[r * wide + c, tile * WH * cols + r * cols + at] = 1
    return chosen


def band_kernel(tiles, cols, place, chosen, *refs):
    pieces, (band, latent, laid, wide) = refs[:tiles], refs[tiles:]
    size = WH * cols
    var = place[1]
    for s in range(tiles):
        tile = lax.rem(var + tiles - s, tiles)
        laid[pl.ds(pl.multiple_of(tile * size, 16), size), :] = pieces[s][...]
    wide[...] = jnp.dot(chosen[...], laid[...], preferred_element_type=F32)
    band[...] = wide[...].astype(BF16)
    for r in range(WH):
        start = pl.multiple_of(r * tiles * cols + var * cols, 8)
        latent[r] = wide[pl.ds(start, cols), :].astype(BF16)


def band_latents(place, pieces, cols):
    tiles = len(pieces)
    width = pieces[0].shape[1]
    total = WH * tiles * cols
    vmem = pl.BlockSpec(memory_space=pltpu.VMEM)
    return pl.pallas_call(
        functools.partial(band_kernel, tiles, cols),
        out_shape=(
            jax.ShapeDtypeStruct((total, width), BF16),
            jax.ShapeDtypeStruct((WH, cols, width), BF16),
        ),
        in_specs=[pl.BlockSpec(memory_space=pltpu.SMEM)] + [vmem] * (tiles + 1),
        out_specs=(vmem, vmem),
        scratch_shapes=[pltpu.VMEM((total, width), BF16), pltpu.VMEM((total, width), F32)],
        compiler_params=pltpu.CompilerParams(vmem_limit_bytes=VMEM_LIMIT),
        cost_estimate=pl.CostEstimate(
            flops=2 * total * total * width, bytes_accessed=4_000_000, transcendentals=0
        ),
        name="band_latents",
    )(place, jnp.asarray(band_map(tiles, cols), BF16), *pieces)


def slot_errors(level, tile_counts, rows, weight, target):
    predicted = lax.dot_general(
        rows, weight, (((1,), (1,)), ((), ())), preferred_element_type=F32
    )
    live = jnp.where(level < tile_counts, 1.0, 0.0)
    diff = predicted - target.astype(F32).reshape(predicted.shape)
    return (diff * live).astype(BF16)


def head_halves(k, lats, lat, errors, rows, turned, keep, send):
    turned[k] = lax.dot_general(
        errors, rows, (((0,), (0,)), ((), ())), preferred_element_type=F32
    ).astype(BF16)
    piece = turned.shape[-1] // lats
    for q in range(lats):
        core, x, y = q & 1, (q >> 1) & 1, (q >> 2) & 1
        outer, inner = (x, y) if k == 0 else (y, x)
        start = pl.multiple_of(jnp.bitwise_xor(lat, q) * piece, piece)
        to = send if core else keep
        to[k, outer, inner, 0] = turned[k, :, pl.ds(start, piece)]


def add_back(lats, errs, gathered, scale, total):
    piece = gathered.shape[-1]
    for l in range(0, lats, 2):
        lanes = slice(l * piece, (l + 2) * piece)
        term = 0.0
        for k in range(2):
            weight = jnp.concatenate([gathered[l, k], gathered[l + 1, k]], axis=1)
            factor = scale[k][:, lanes]
            term = term + jnp.dot(errs[k], weight, preferred_element_type=F32) * factor
        total[:, lanes] += term


def slot_kernel(
    first_slot,
    lats,
    tiles,
    final,
    place,
    counts,
    datasets,
    levels,
    tile_of,
    scale,
    shift,
    gathered,
    target,
    *refs,
):
    if final:
        band, before, keep, send, out, total, rows0, rows1, errs, turned, tile_counts = refs
    else:
        band, keep, send, total, rows0, rows1, errs, turned, tile_counts = refs
    rows = (rows0, rows1)
    step, steps = pl.program_id(0), pl.num_programs(0)
    slot = first_slot + 2 * step

    @pl.when(step == 0)
    def _():
        total[...] = before[...] if final else jnp.zeros_like(total)
        tile = tile_of[...]
        wanted = jnp.zeros_like(tile)
        for t in range(tiles):
            wanted = jnp.where(tile == t, counts[datasets[0, t]], wanted)
        tile_counts[...] = wanted

    for k in range(2):
        rows[k][...] = (band[...].astype(F32) * scale[k] + shift[k]).astype(BF16)
    for k in range(2):
        weight = jnp.concatenate([gathered[l, k] for l in range(lats)], axis=1)
        errs[k] = slot_errors(levels[slot + k], tile_counts[...], rows[k][...], weight, target[k])
    for k in range(2):
        head_halves(k, lats, place[0], errs[k], rows[k][...], turned, keep, send)
    add_back(lats, errs, gathered, scale, total)

    if final:

        @pl.when(step == steps - 1)
        def _():
            cols = out.shape[2]
            for s in range(tiles):
                for r in range(WH):
                    start = (r * tiles + s) * cols
                    out[s, r] = total[start : start + cols, :].astype(BF16)


def slot_group(pair, pairs, lats, place, small, tile_of, scale, shift, gathered, targets, band, before):
    places, width = tile_of.shape[0], scale.shape[-1]
    outs = targets.shape[-1]
    tiles = small[1].shape[1]
    piece = width // lats
    cols = places // (WH * tiles)
    smem = pl.BlockSpec(memory_space=pltpu.SMEM)
    fixed = lambda shape: pl.BlockSpec(shape, lambda i: (0,) * len(shape))
    halves = jax.ShapeDtypeStruct((2, 2, 2, pairs, outs, piece), BF16)
    half_spec = pl.BlockSpec((2, 2, 2, 1, outs, piece), lambda i: (0, 0, 0, i, 0, 0))
    level_spec = pl.BlockSpec((2, 1, width), lambda i: (i + pair, 0, 0))
    in_specs = [smem] * 4 + [
        fixed(tile_of.shape),
        level_spec,
        level_spec,
        pl.BlockSpec((lats, 2, outs, piece), lambda i: (0, i + pair, 0, 0)),
        pl.BlockSpec((2,) + targets.shape[1:], lambda i: (i + pair, 0, 0, 0)),
    ]
    args = [place, *small, tile_of, scale, shift, gathered, targets, band]
    final = before is not None
    scratch = [
        pltpu.VMEM((places, width), BF16),
        pltpu.VMEM((places, width), BF16),
        pltpu.VMEM((2, places, outs), BF16),
        pltpu.VMEM((2, outs, width), BF16),
        pltpu.VMEM((places, 1), jnp.int32),
    ]
    sums = jax.ShapeDtypeStruct((places, width), F32)
    if final:
        args.append(before)
        scratch.insert(0, pltpu.VMEM(sums.shape, F32))
        results = [jax.ShapeDtypeStruct((tiles, WH, cols, width), BF16)]
    else:
        results = [sums]
    in_specs.extend(fixed(arg.shape) for arg in args[len(in_specs) :])
    limit = (45 if final else 48) * 1024 * 1024
    return pl.pallas_call(
        functools.partial(slot_kernel, 2 * pair, lats, tiles, final),
        grid=(pairs,),
        out_shape=(halves, halves, *results),
        in_specs=in_specs,
        out_specs=(half_spec, half_spec, *(fixed(r.shape) for r in results)),
        scratch_shapes=scratch,
        compiler_params=pltpu.CompilerParams(vmem_limit_bytes=limit),
        cost_estimate=pl.CostEstimate(
            flops=pairs * 12 * places * width * outs, bytes_accessed=pairs * 5_000_000, transcendentals=0
        ),
        name="slot_group",
    )(*args)


def halve_kernel(keep, came, *refs):
    outs = refs[-4:]
    for k in range(2):
        for half in range(2):
            total = keep[k, half].astype(F32) + came[k, half].astype(F32)
            outs[2 * half + k][...] = total.astype(BF16)


def halve(keep, came, after):
    part = jax.ShapeDtypeStruct(keep.shape[2:], BF16)
    vmem = pl.BlockSpec(memory_space=pltpu.VMEM)
    out = pl.pallas_call(
        halve_kernel,
        out_shape=(part,) * 4,
        in_specs=[vmem, vmem] + [pl.BlockSpec(memory_space=pl.ANY)] * len(after),
        out_specs=(vmem,) * 4,
        compiler_params=pltpu.CompilerParams(vmem_limit_bytes=24 * 1024 * 1024),
        cost_estimate=pl.CostEstimate(flops=2_000_000, bytes_accessed=6_000_000, transcendentals=0),
        name="halve",
    )(keep, came, *after)
    return out[0:2], out[2:4]


def join_kernel(norm, *refs):
    out = refs[-1]
    pairs = refs[:-1]
    slot = 0
    for i in range(0, len(pairs), 4):
        for k in range(pairs[i].shape[0]):
            for kept, came in (pairs[i : i + 2], pairs[i + 2 : i + 4]):
                out[slot] = (kept[k].astype(F32) + came[k].astype(F32)) * norm
                slot += 1


def join_heads(pairs, norm):
    flat = [array for pair in pairs for array in pair]
    slots = sum(kept.shape[0] for kept, _ in pairs)
    _, outs, piece = flat[0].shape
    vmem = pl.BlockSpec(memory_space=pltpu.VMEM)
    return pl.pallas_call(
        functools.partial(join_kernel, norm),
        out_shape=jax.ShapeDtypeStruct((slots, outs, piece), F32),
        in_specs=[vmem] * len(flat),
        out_specs=vmem,
        compiler_params=pltpu.CompilerParams(vmem_limit_bytes=VMEM_LIMIT),
        cost_estimate=pl.CostEstimate(flops=1_000_000, bytes_accessed=4_000_000, transcendentals=0),
        name="join_heads",
    )(*flat)


def fast_local(
    patches, norm_gain, input_proj, output_proj, level_scale, level_shift, head_weight, targets,
    level_counts, tile_dataset, slot_level,
):
    rows, cols, width = patches.shape
    lats, tiles = lax.axis_size("lat"), lax.axis_size("var")
    slots = head_weight.shape[0]
    lat, var = lax.axis_index("lat"), lax.axis_index("var")
    place = jnp.stack([lat, var]).astype(jnp.int32)
    gathered = lax.all_gather(jnp.transpose(head_weight, (0, 2, 1)), "lat", axis=0, tiled=False)

    right = [(i, (i + 1) % tiles) for i in range(tiles)]
    up = [(i, i + 1) for i in range(lats - 1)]
    down = [(i + 1, i) for i in range(lats - 1)]
    left = lax.ppermute(patches[:, cols - HC :], "var", right)
    shifted = jnp.concatenate([left, patches[:, : cols - HC]], axis=1)
    above = lax.ppermute(shifted[HR:], "lat", up)
    below = lax.ppermute(shifted[:HR], "lat", down)
    mine = attention(place, (shifted, above, below), norm_gain, input_proj, output_proj, lats)
    pieces = [mine]
    for s in range(1, tiles):
        pieces.append(lax.ppermute(mine, "var", [(i, (i + s) % tiles) for i in range(tiles)]))

    band, latent = band_latents(place, pieces, cols)
    tile_of = jnp.asarray(np.arange(rows * tiles * cols)[:, None] % (tiles * cols) // cols, jnp.int32)
    scale3, shift3 = level_scale.reshape(slots, 1, width), level_shift.reshape(slots, 1, width)
    small = (level_counts, tile_dataset, slot_level)
    flip = lambda array, bit: lax.ppermute(array, "lat", [(i, i ^ bit) for i in range(lats)])
    add = lambda a, b: (a.astype(F32) + b.astype(F32)).astype(BF16)
    common = (lats, place, small, tile_of, scale3, shift3, gathered, targets, band)
    most = slots // 2 - 1
    bits = (2, 4)
    keep_a, send_a, so_far = slot_group(0, most, *common, None)
    keep_b, send_b, terms = slot_group(most, slots // 2 - most, *common, so_far)
    grad_latent = lax.psum_scatter(terms, "var", scatter_dimension=0, tiled=False)
    pairs, came = [], [terms]
    for keep, send in ((keep_a, send_a), (keep_b, send_b)):
        kept, sent = halve(keep, flip(send, 1), came)
        came = [flip(sent[k], bits[k]) for k in range(2)]
        for k in range(2):
            last = flip(add(kept[k][1], came[k][1]), bits[1 - k])
            pairs.append((add(kept[k][0], came[k][0]), last))
    grad_head = join_heads(pairs, 1.0 / math.sqrt(lats * rows * tiles * cols))
    return (latent, grad_latent, jnp.transpose(grad_head, (0, 2, 1)))


def padded(array, sides, width, wrap):
    for axis, dim in sides:
        size, length = (lax.axis_size(axis), array.shape[dim])
        up = [(i, (i + 1) % size) for i in range(size if wrap else size - 1)]
        down = [(j, i) for i, j in up]
        last = lax.slice_in_dim(array, length - width, length, axis=dim)
        initial = lax.slice_in_dim(array, 0, width, axis=dim)
        before = lax.ppermute(last, axis, up)
        after = lax.ppermute(initial, axis, down)
        array = jnp.concatenate([before, array, after], axis=dim)
    return array


def layer_norm(values, gain):
    wide = values.astype(jnp.float32)
    average = jnp.mean(wide, axis=-1, keepdims=True)
    centred = wide - average
    variance = jnp.mean(centred * centred, axis=-1, keepdims=True)
    return (centred * lax.rsqrt(variance + EPS) * gain).astype(jnp.bfloat16)


def window_attention(query_ext, keyval, row_valid, heads):
    ext_rows, ext_cols, width = query_ext.shape
    head_size = width // heads
    win_rows = ext_rows // WH
    win_cols = ext_cols // WW

    def split(values, parts):
        shaped = values.reshape(win_rows, WH, win_cols, WW, parts, heads, head_size)
        return shaped.transpose(0, 2, 1, 3, 4, 5, 6).reshape(
            win_rows * win_cols, WH * WW, parts, heads, head_size
        )

    query_win = split(query_ext, 1)[:, :, 0]
    pairs = split(keyval, 2)
    key_win = pairs[:, :, 0]
    value_win = pairs[:, :, 1]
    key_mask = jnp.broadcast_to(
        row_valid.reshape(win_rows, 1, WH, 1), (win_rows, win_cols, WH, WW)
    ).reshape(win_rows * win_cols, WH * WW)
    scores = jnp.einsum(
        "wqhd,wkhd->whqk", query_win, key_win, preferred_element_type=jnp.float32
    ) / math.sqrt(head_size)
    scores = jnp.where(key_mask[:, None, None, :], scores, -jnp.inf)
    peak = jnp.max(scores, axis=-1, keepdims=True)
    weights = jnp.exp(scores - peak)
    probs = (weights / jnp.sum(weights, axis=-1, keepdims=True)).astype(jnp.bfloat16)
    mixed = jnp.einsum("whqk,wkhd->wqhd", probs, value_win, preferred_element_type=jnp.float32)
    return (
        mixed.reshape(win_rows, win_cols, WH, WW, width)
        .transpose(0, 2, 1, 3, 4)
        .reshape(ext_rows, ext_cols, width)
    )


def slot_terms(piece, target_rows, live_cols, level_scale, level_shift, heads_full):
    piece_wide = piece.astype(jnp.float32)
    rows = (
        piece_wide[None] * level_scale[:, None, None, :] + level_shift[:, None, None, :]
    ).astype(jnp.bfloat16)
    predicted = jnp.einsum("krnd,kdo->krno", rows, heads_full, preferred_element_type=jnp.float32)
    errors = ((predicted - target_rows.astype(jnp.float32)) * live_cols[:, None, :, None]).astype(
        jnp.bfloat16
    )
    back_grad = jnp.einsum("krno,kdo->krnd", errors, heads_full, preferred_element_type=jnp.float32)
    piece_grad = jnp.sum(back_grad * level_scale[:, None, None, :], axis=0)
    head_add = jnp.einsum("krnd,krno->dko", rows, errors, preferred_element_type=jnp.float32)
    return (piece_grad, head_add)


def local(
    patches,
    norm_gain,
    input_proj,
    output_proj,
    level_scale,
    level_shift,
    head_weight,
    targets,
    level_counts,
    tile_dataset,
    slot_level,
):
    band_rows, band_cols, width = patches.shape
    half_rows = WH // 2
    half_cols = WW // 2
    lat_count = lax.axis_size("lat")
    var_count = lax.axis_size("var")
    lat_place = lax.axis_index("lat")
    ext_rows = band_rows + WH
    ext_cols = band_cols + WW
    extended = padded(patches, (("lat", 0),), half_rows, False)
    extended = padded(extended, (("var", 1),), half_cols, True)
    normed_ext = layer_norm(extended, norm_gain)
    keyval = jnp.dot(
        normed_ext.reshape(-1, width), input_proj[:, width:], preferred_element_type=jnp.float32
    )
    keyval = keyval.astype(jnp.bfloat16).reshape(ext_rows, ext_cols, 2 * width)
    normed = normed_ext[half_rows : half_rows + band_rows, half_cols : half_cols + band_cols]
    queries = jnp.dot(
        normed.reshape(-1, width), input_proj[:, :width], preferred_element_type=jnp.float32
    )
    queries = queries.astype(jnp.bfloat16).reshape(band_rows, band_cols, width)
    query_ext = jnp.pad(queries, ((half_rows, WH - half_rows), (half_cols, WW - half_cols), (0, 0)))
    global_row = lat_place * band_rows - half_rows + jnp.arange(ext_rows, dtype=jnp.int32)
    row_valid = (global_row >= 0) & (global_row < lat_count * band_rows)
    mixed = window_attention(query_ext, keyval, row_valid, HEADS)
    attn = mixed[half_rows : half_rows + band_rows, half_cols : half_cols + band_cols].astype(
        jnp.bfloat16
    )
    update = jnp.dot(
        attn.reshape(-1, width), output_proj, preferred_element_type=jnp.float32
    ).reshape(band_rows, band_cols, width)
    latent = (patches.astype(jnp.float32) + update).astype(jnp.bfloat16)
    dataset_row = tile_dataset[0]
    dataset_ids = jnp.arange(level_counts.shape[0], dtype=jnp.int32)
    tile_levels = jnp.sum(
        jnp.where(dataset_row[:, None] == dataset_ids[None, :], level_counts[None, :], 0), axis=1
    )
    live_tiles = (slot_level[None, :] < tile_levels[:, None]).astype(jnp.float32)
    heads_full = lax.all_gather(head_weight, "lat", axis=1, tiled=True)
    tile_ids = jnp.arange(var_count, dtype=jnp.int32)
    piece = lax.all_gather(latent, "var", axis=1, tiled=True)
    piece_cols = piece.shape[1]
    column_tile = jnp.arange(piece_cols, dtype=jnp.int32) // band_cols
    onehot = (column_tile[:, None] == tile_ids[None, :]).astype(jnp.float32)
    column_live = jnp.dot(onehot, live_tiles)
    piece_grad, head_add = slot_terms(
        piece, targets, column_live.T, level_scale, level_shift, heads_full
    )
    latent_terms = piece_grad
    latent_terms, head_terms = (latent_terms, head_add)
    grad_latent = lax.psum_scatter(
        latent_terms.astype(jnp.bfloat16), "var", scatter_dimension=1, tiled=True
    )
    head_terms = head_terms * (1.0 / math.sqrt(lat_count * band_rows * var_count * band_cols))
    mine = lax.psum_scatter(
        head_terms.astype(jnp.bfloat16), "lat", scatter_dimension=0, tiled=True
    ).astype(jnp.float32)
    grad_head = jnp.transpose(mine, (1, 0, 2))
    return (latent, grad_latent, grad_head)


def solution(mesh):
    in_specs = (
        P("lat", "var", None),
        P(),
        P(),
        P(),
        P("var", None),
        P("var", None),
        P("var", "lat", None),
        P("var", "lat", None, None),
        P(),
        P("lat", None),
        P("var"),
    )
    fast = mesh.shape["lat"] == 8 and mesh.shape["var"] == 4
    body = fast_local if fast else local
    out_specs = (P("lat", "var", None), P("lat", "var", None), P("var", "lat", None))
    return jax.shard_map(body, mesh=mesh, in_specs=in_specs, out_specs=out_specs, check_vma=False)
```

```python
import functools
import math

import jax
import jax.numpy as jnp
import numpy as np
from jax import lax
from jax.experimental import pallas as pl
from jax.experimental.pallas import tpu as pltpu
from jax.sharding import PartitionSpec as P

HEADS = 16
WH = 6
WW = 12
EPS = 1e-05
HR = WH // 2
HC = WW // 2
QP = 48
VMEM_LIMIT = 48 * 1024 * 1024
F32 = jnp.float32
BF16 = jnp.bfloat16


def gather_maps(cols):
    win_cols = cols // WW
    windows = 2 * win_cols
    into = np.zeros((windows * 2 * QP, 2 * WH * cols), np.float32)
    back = np.zeros((WH * cols, windows * QP), np.float32)
    for win in range(windows):
        win_row, win_col = divmod(win, win_cols)
        for row in range(HR):
            for c in range(WW):
                own = (win_row * HR + row) * cols + win_col * WW + c
                slot = row * WW + c
                into[win * 2 * QP + slot, own] = 1
                into[win * 2 * QP + QP + slot, WH * cols + own] = 1
                back[own, win * QP + slot] = 1
    return into, back


def attention_kernel(
    bands,
    place,
    own,
    above,
    below,
    gain,
    maps_hbm,
    in_hbm,
    out_hbm,
    out,
    raw,
    qkv,
    attn,
    maps,
    proj_in,
    proj_out,
    sems,
):
    moves = [
        pltpu.make_async_copy(src, dst, sems.at[i])
        for i, (src, dst) in enumerate(((maps_hbm, maps), (in_hbm, proj_in), (out_hbm, proj_out)))
    ]
    for move in moves:
        move.start()
    cols, width = own.shape[1], own.shape[2]
    win_cols = cols // WW
    windows = 2 * win_cols
    slots = windows * 2 * QP
    head_size = width // HEADS
    quad = 256 // head_size
    size = WH * cols
    start = 0
    for ref in (own, above, below):
        count = ref.shape[0] * cols
        raw[start : start + count, :] = ref[...].astype(F32).reshape(count, width)
        start += count
    wide = raw[...]
    average = jnp.mean(wide, axis=-1, keepdims=True)
    centred = wide - average
    variance = jnp.mean(centred * centred, axis=-1, keepdims=True)
    normed = (centred * lax.rsqrt(variance + EPS) * gain[...]).astype(BF16)
    moves[0].wait()
    win_x = jnp.dot(maps[0:slots, :], normed, preferred_element_type=F32).astype(BF16)
    moves[1].wait()
    step = 512
    for j in range(3 * width // step):
        part = slice(j * step, (j + 1) * step)
        qkv[:, part] = jnp.dot(win_x, proj_in[:, part], preferred_element_type=F32).astype(BF16)
    lane = lax.broadcasted_iota(jnp.int32, (1, 256), 1) // head_size
    heads = [jnp.where(lane == h, 1.0, 0.0) for h in range(quad)]
    key_id = lax.broadcasted_iota(jnp.int32, (1, 2 * QP), 1)
    scale = 1.0 / math.sqrt(head_size)
    for win in range(windows):
        win_row = win // win_cols
        edge = 0 if win_row == 0 else bands - 1
        has_halo = place[0] != edge
        halo_keys = jnp.logical_and(key_id >= QP, key_id < QP + HR * WW)
        valid = jnp.logical_or(key_id < HR * WW, jnp.logical_and(halo_keys, has_halo))
        bias = jnp.where(valid, 0.0, -1e30)
        row0 = win * 2 * QP
        for g in range(width // 256):
            lanes = slice(g * 256, (g + 1) * 256)
            query = qkv[row0 : row0 + QP, lanes].astype(F32) * scale
            stacked = jnp.concatenate([query * h for h in heads], axis=0).astype(BF16)
            key = qkv[row0 : row0 + 2 * QP, width + g * 256 : width + (g + 1) * 256]
            value = qkv[row0 : row0 + 2 * QP, 2 * width + g * 256 : 2 * width + (g + 1) * 256]
            scores = (
                lax.dot_general(
                    stacked, key, (((1,), (1,)), ((), ())), preferred_element_type=F32
                )
                + bias
            )
            weights = jnp.exp(scores - jnp.max(scores, axis=-1, keepdims=True))
            probs = (weights / jnp.sum(weights, axis=-1, keepdims=True)).astype(BF16)
            mixed = jnp.dot(probs, value, preferred_element_type=F32)
            chosen = mixed[0:QP] * heads[0]
            for h in range(1, quad):
                chosen = chosen + mixed[h * QP : (h + 1) * QP] * heads[h]
            attn[win * QP : (win + 1) * QP, lanes] = chosen.astype(BF16)
    back = maps[slots : slots + size, 0 : windows * QP]
    ordered = jnp.dot(back, attn[...], preferred_element_type=F32).astype(BF16)
    moves[2].wait()
    update = jnp.dot(ordered, proj_out[...], preferred_element_type=F32)
    out[...] = (raw[0:size, :] + update).astype(BF16)


def attention(place, pieces, gain, proj_in, proj_out, bands):
    rows, cols, width = pieces[0].shape
    into, back = gather_maps(cols)
    total = into.shape[1]
    windows = 2 * (cols // WW)
    back = np.pad(back, ((0, 0), (0, total - back.shape[1])))
    maps = np.concatenate([into, back])
    vmem = pl.BlockSpec(memory_space=pltpu.VMEM)
    hbm = pl.BlockSpec(memory_space=pltpu.HBM)
    return pl.pallas_call(
        functools.partial(attention_kernel, bands),
        out_shape=jax.ShapeDtypeStruct((rows * cols, width), BF16),
        in_specs=[pl.BlockSpec(memory_space=pltpu.SMEM)] + [vmem] * 4 + [hbm] * 3,
        out_specs=vmem,
        scratch_shapes=[
            pltpu.VMEM((total, width), F32),
            pltpu.VMEM((windows * 2 * QP, 3 * width), BF16),
            pltpu.VMEM((windows * QP, width), BF16),
            pltpu.VMEM(maps.shape, BF16),
            pltpu.VMEM(proj_in.shape, BF16),
            pltpu.VMEM(proj_out.shape, BF16),
            pltpu.SemaphoreType.DMA((3,)),
        ],
        compiler_params=pltpu.CompilerParams(vmem_limit_bytes=53 * 1024 * 1024),
        cost_estimate=pl.CostEstimate(
            flops=6_000_000_000, bytes_accessed=12_000_000, transcendentals=400_000
        ),
        name="window_attention",
    )(
        place,
        *pieces,
        gain.reshape(1, width),
        jnp.asarray(maps, BF16),
        proj_in,
        proj_out,
    )


def band_map(tiles, cols):
    wide = tiles * cols
    chosen = np.zeros((WH * wide, WH * wide), np.float32)
    for r in range(WH):
        for c in range(wide):
            tile, at = divmod((c + HC) % wide, cols)
            chosen[r * wide + c, tile * WH * cols + r * cols + at] = 1
    return chosen


def order_band(tiles, cols, var, chosen, pieces, laid, wide, band, latent):
    size = WH * cols
    for s in range(tiles):
        tile = lax.rem(var + tiles - s, tiles)
        laid[pl.ds(pl.multiple_of(tile * size, 16), size), :] = pieces[s][...]
    wide[...] = jnp.dot(chosen[...], laid[...], preferred_element_type=F32)
    band[...] = wide[...].astype(BF16)
    for r in range(WH):
        start = pl.multiple_of(r * tiles * cols + var * cols, 8)
        latent[r] = wide[pl.ds(start, cols), :].astype(BF16)


def slot_errors(level, tile_counts, rows, weight, target):
    predicted = lax.dot_general(
        rows, weight, (((1,), (1,)), ((), ())), preferred_element_type=F32
    )
    live = jnp.where(level < tile_counts, 1.0, 0.0)
    diff = predicted - target.astype(F32).reshape(predicted.shape)
    return (diff * live).astype(BF16)


def head_halves(k, lats, lat, errors, rows, turned, keep, send):
    turned[k] = lax.dot_general(
        errors, rows, (((0,), (0,)), ((), ())), preferred_element_type=F32
    ).astype(BF16)
    piece = turned.shape[-1] // lats
    for q in range(lats):
        core, x, y = q & 1, (q >> 1) & 1, (q >> 2) & 1
        outer, inner = (x, y) if k == 0 else (y, x)
        start = pl.multiple_of(jnp.bitwise_xor(lat, q) * piece, piece)
        to = send if core else keep
        to[k, outer, inner, 0] = turned[k, :, pl.ds(start, piece)]


def add_back(lats, errs, gathered, scale, total):
    piece = gathered.shape[-1]
    for l in range(0, lats, 2):
        lanes = slice(l * piece, (l + 2) * piece)
        term = 0.0
        for k in range(2):
            weight = jnp.concatenate([gathered[l, k], gathered[l + 1, k]], axis=1)
            factor = scale[k][:, lanes]
            term = term + jnp.dot(errs[k], weight, preferred_element_type=F32) * factor
        total[:, lanes] += term


def slot_kernel(
    first_slot,
    lats,
    tiles,
    final,
    place,
    counts,
    datasets,
    levels,
    tile_of,
    scale,
    shift,
    gathered,
    target,
    *refs,
):
    if final:
        band, before, keep, send, out, total, rows0, rows1, errs, turned, tile_counts = refs
    else:
        chosen, pieces = refs[0], refs[1 : 1 + tiles]
        keep, send, total, band, latent, rows0, rows1, errs, turned, tile_counts = refs[1 + tiles :]
    rows = (rows0, rows1)
    step, steps = pl.program_id(0), pl.num_programs(0)
    slot = first_slot + 2 * step

    @pl.when(step == 0)
    def _():
        if final:
            total[...] = before[...]
        else:
            order_band(tiles, latent.shape[1], place[1], chosen, pieces, rows0, total, band, latent)
            total[...] = jnp.zeros_like(total)
        tile = tile_of[...]
        wanted = jnp.zeros_like(tile)
        for t in range(tiles):
            wanted = jnp.where(tile == t, counts[datasets[0, t]], wanted)
        tile_counts[...] = wanted

    for k in range(2):
        rows[k][...] = (band[...].astype(F32) * scale[k] + shift[k]).astype(BF16)
    for k in range(2):
        weight = jnp.concatenate([gathered[l, k] for l in range(lats)], axis=1)
        errs[k] = slot_errors(levels[slot + k], tile_counts[...], rows[k][...], weight, target[k])
    for k in range(2):
        head_halves(k, lats, place[0], errs[k], rows[k][...], turned, keep, send)
    add_back(lats, errs, gathered, scale, total)

    if final:

        @pl.when(step == steps - 1)
        def _():
            cols = out.shape[2]
            for s in range(tiles):
                for r in range(WH):
                    start = (r * tiles + s) * cols
                    out[s, r] = total[start : start + cols, :].astype(BF16)


def slot_group(pair, pairs, lats, place, small, tile_of, scale, shift, gathered, targets, pieces, before):
    places, width = tile_of.shape[0], scale.shape[-1]
    outs = targets.shape[-1]
    tiles = small[1].shape[1]
    piece = width // lats
    cols = places // (WH * tiles)
    smem = pl.BlockSpec(memory_space=pltpu.SMEM)
    fixed = lambda shape: pl.BlockSpec(shape, lambda i: (0,) * len(shape))
    halves = jax.ShapeDtypeStruct((2, 2, 2, pairs, outs, piece), BF16)
    half_spec = pl.BlockSpec((2, 2, 2, 1, outs, piece), lambda i: (0, 0, 0, i, 0, 0))
    level_spec = pl.BlockSpec((2, 1, width), lambda i: (i + pair, 0, 0))
    in_specs = [smem] * 4 + [
        fixed(tile_of.shape),
        level_spec,
        level_spec,
        pl.BlockSpec((lats, 2, outs, piece), lambda i: (0, i + pair, 0, 0)),
        pl.BlockSpec((2,) + targets.shape[1:], lambda i: (i + pair, 0, 0, 0)),
    ]
    args = [place, *small, tile_of, scale, shift, gathered, targets]
    final = before is not None
    scratch = [
        pltpu.VMEM((places, width), BF16),
        pltpu.VMEM((places, width), BF16),
        pltpu.VMEM((2, places, outs), BF16),
        pltpu.VMEM((2, outs, width), BF16),
        pltpu.VMEM((places, 1), jnp.int32),
    ]
    sums = jax.ShapeDtypeStruct((places, width), F32)
    if final:
        args.extend(before)
        scratch.insert(0, pltpu.VMEM(sums.shape, F32))
        results = [jax.ShapeDtypeStruct((tiles, WH, cols, width), BF16)]
    else:
        args.extend([jnp.asarray(band_map(tiles, cols), BF16), *pieces])
        results = [
            sums,
            jax.ShapeDtypeStruct((places, width), BF16),
            jax.ShapeDtypeStruct((WH, cols, width), BF16),
        ]
    in_specs.extend(fixed(arg.shape) for arg in args[len(in_specs) :])
    limit = (45 if final else 48) * 1024 * 1024
    return pl.pallas_call(
        functools.partial(slot_kernel, 2 * pair, lats, tiles, final),
        grid=(pairs,),
        out_shape=(halves, halves, *results),
        in_specs=in_specs,
        out_specs=(half_spec, half_spec, *(fixed(r.shape) for r in results)),
        scratch_shapes=scratch,
        compiler_params=pltpu.CompilerParams(vmem_limit_bytes=limit),
        cost_estimate=pl.CostEstimate(
            flops=pairs * 12 * places * width * outs, bytes_accessed=pairs * 5_000_000, transcendentals=0
        ),
        name="slot_group",
    )(*args)


def halve_kernel(keep, came, *refs):
    outs = refs[-4:]
    for k in range(2):
        for half in range(2):
            total = keep[k, half].astype(F32) + came[k, half].astype(F32)
            outs[2 * half + k][...] = total.astype(BF16)


def halve(keep, came, after):
    part = jax.ShapeDtypeStruct(keep.shape[2:], BF16)
    vmem = pl.BlockSpec(memory_space=pltpu.VMEM)
    out = pl.pallas_call(
        halve_kernel,
        out_shape=(part,) * 4,
        in_specs=[vmem, vmem] + [pl.BlockSpec(memory_space=pl.ANY)] * len(after),
        out_specs=(vmem,) * 4,
        compiler_params=pltpu.CompilerParams(vmem_limit_bytes=24 * 1024 * 1024),
        cost_estimate=pl.CostEstimate(flops=2_000_000, bytes_accessed=6_000_000, transcendentals=0),
        name="halve",
    )(keep, came, *after)
    return out[0:2], out[2:4]


def join_kernel(norm, *refs):
    out = refs[-1]
    pairs = refs[:-1]
    slot = 0
    for i in range(0, len(pairs), 4):
        for k in range(pairs[i].shape[0]):
            for kept, came in (pairs[i : i + 2], pairs[i + 2 : i + 4]):
                out[slot] = (kept[k].astype(F32) + came[k].astype(F32)) * norm
                slot += 1


def join_heads(pairs, norm):
    flat = [array for pair in pairs for array in pair]
    slots = sum(kept.shape[0] for kept, _ in pairs)
    _, outs, piece = flat[0].shape
    vmem = pl.BlockSpec(memory_space=pltpu.VMEM)
    return pl.pallas_call(
        functools.partial(join_kernel, norm),
        out_shape=jax.ShapeDtypeStruct((slots, outs, piece), F32),
        in_specs=[vmem] * len(flat),
        out_specs=vmem,
        compiler_params=pltpu.CompilerParams(vmem_limit_bytes=VMEM_LIMIT),
        cost_estimate=pl.CostEstimate(flops=1_000_000, bytes_accessed=4_000_000, transcendentals=0),
        name="join_heads",
    )(*flat)


def fast_local(
    patches, norm_gain, input_proj, output_proj, level_scale, level_shift, head_weight, targets,
    level_counts, tile_dataset, slot_level,
):
    rows, cols, width = patches.shape
    lats, tiles = lax.axis_size("lat"), lax.axis_size("var")
    slots = head_weight.shape[0]
    lat, var = lax.axis_index("lat"), lax.axis_index("var")
    place = jnp.stack([lat, var]).astype(jnp.int32)
    gathered = lax.all_gather(jnp.transpose(head_weight, (0, 2, 1)), "lat", axis=0, tiled=False)

    right = [(i, (i + 1) % tiles) for i in range(tiles)]
    up = [(i, i + 1) for i in range(lats - 1)]
    down = [(i + 1, i) for i in range(lats - 1)]
    left = lax.ppermute(patches[:, cols - HC :], "var", right)
    shifted = jnp.concatenate([left, patches[:, : cols - HC]], axis=1)
    above = lax.ppermute(shifted[HR:], "lat", up)
    below = lax.ppermute(shifted[:HR], "lat", down)
    mine = attention(place, (shifted, above, below), norm_gain, input_proj, output_proj, lats)
    pieces = [mine]
    for s in range(1, tiles):
        pieces.append(lax.ppermute(mine, "var", [(i, (i + s) % tiles) for i in range(tiles)]))

    tile_of = jnp.asarray(np.arange(rows * tiles * cols)[:, None] % (tiles * cols) // cols, jnp.int32)
    scale3, shift3 = level_scale.reshape(slots, 1, width), level_shift.reshape(slots, 1, width)
    small = (level_counts, tile_dataset, slot_level)
    flip = lambda array, bit: lax.ppermute(array, "lat", [(i, i ^ bit) for i in range(lats)])
    add = lambda a, b: (a.astype(F32) + b.astype(F32)).astype(BF16)
    common = (lats, place, small, tile_of, scale3, shift3, gathered, targets)
    most = slots // 2 - 1
    bits = (2, 4)
    keep_a, send_a, so_far, band, latent = slot_group(0, most, *common, pieces, None)
    keep_b, send_b, terms = slot_group(most, slots // 2 - most, *common, None, (band, so_far))
    grad_latent = lax.psum_scatter(terms, "var", scatter_dimension=0, tiled=False)
    pairs, after = [], [terms]
    for keep, send in ((keep_a, send_a), (keep_b, send_b)):
        kept, sent = halve(keep, flip(send, 1), after)
        after = list(sent)
        came = [flip(sent[k], bits[k]) for k in range(2)]
        for k in range(2):
            last = flip(add(kept[k][1], came[k][1]), bits[1 - k])
            pairs.append((add(kept[k][0], came[k][0]), last))
    grad_head = join_heads(pairs, 1.0 / math.sqrt(lats * rows * tiles * cols))
    return (latent, grad_latent, jnp.transpose(grad_head, (0, 2, 1)))


def padded(array, sides, width, wrap):
    for axis, dim in sides:
        size, length = (lax.axis_size(axis), array.shape[dim])
        up = [(i, (i + 1) % size) for i in range(size if wrap else size - 1)]
        down = [(j, i) for i, j in up]
        last = lax.slice_in_dim(array, length - width, length, axis=dim)
        initial = lax.slice_in_dim(array, 0, width, axis=dim)
        before = lax.ppermute(last, axis, up)
        after = lax.ppermute(initial, axis, down)
        array = jnp.concatenate([before, array, after], axis=dim)
    return array


def layer_norm(values, gain):
    wide = values.astype(jnp.float32)
    average = jnp.mean(wide, axis=-1, keepdims=True)
    centred = wide - average
    variance = jnp.mean(centred * centred, axis=-1, keepdims=True)
    return (centred * lax.rsqrt(variance + EPS) * gain).astype(jnp.bfloat16)


def window_attention(query_ext, keyval, row_valid, heads):
    ext_rows, ext_cols, width = query_ext.shape
    head_size = width // heads
    win_rows = ext_rows // WH
    win_cols = ext_cols // WW

    def split(values, parts):
        shaped = values.reshape(win_rows, WH, win_cols, WW, parts, heads, head_size)
        return shaped.transpose(0, 2, 1, 3, 4, 5, 6).reshape(
            win_rows * win_cols, WH * WW, parts, heads, head_size
        )

    query_win = split(query_ext, 1)[:, :, 0]
    pairs = split(keyval, 2)
    key_win = pairs[:, :, 0]
    value_win = pairs[:, :, 1]
    key_mask = jnp.broadcast_to(
        row_valid.reshape(win_rows, 1, WH, 1), (win_rows, win_cols, WH, WW)
    ).reshape(win_rows * win_cols, WH * WW)
    scores = jnp.einsum(
        "wqhd,wkhd->whqk", query_win, key_win, preferred_element_type=jnp.float32
    ) / math.sqrt(head_size)
    scores = jnp.where(key_mask[:, None, None, :], scores, -jnp.inf)
    peak = jnp.max(scores, axis=-1, keepdims=True)
    weights = jnp.exp(scores - peak)
    probs = (weights / jnp.sum(weights, axis=-1, keepdims=True)).astype(jnp.bfloat16)
    mixed = jnp.einsum("whqk,wkhd->wqhd", probs, value_win, preferred_element_type=jnp.float32)
    return (
        mixed.reshape(win_rows, win_cols, WH, WW, width)
        .transpose(0, 2, 1, 3, 4)
        .reshape(ext_rows, ext_cols, width)
    )


def slot_terms(piece, target_rows, live_cols, level_scale, level_shift, heads_full):
    piece_wide = piece.astype(jnp.float32)
    rows = (
        piece_wide[None] * level_scale[:, None, None, :] + level_shift[:, None, None, :]
    ).astype(jnp.bfloat16)
    predicted = jnp.einsum("krnd,kdo->krno", rows, heads_full, preferred_element_type=jnp.float32)
    errors = ((predicted - target_rows.astype(jnp.float32)) * live_cols[:, None, :, None]).astype(
        jnp.bfloat16
    )
    back_grad = jnp.einsum("krno,kdo->krnd", errors, heads_full, preferred_element_type=jnp.float32)
    piece_grad = jnp.sum(back_grad * level_scale[:, None, None, :], axis=0)
    head_add = jnp.einsum("krnd,krno->dko", rows, errors, preferred_element_type=jnp.float32)
    return (piece_grad, head_add)


def local(
    patches,
    norm_gain,
    input_proj,
    output_proj,
    level_scale,
    level_shift,
    head_weight,
    targets,
    level_counts,
    tile_dataset,
    slot_level,
):
    band_rows, band_cols, width = patches.shape
    half_rows = WH // 2
    half_cols = WW // 2
    lat_count = lax.axis_size("lat")
    var_count = lax.axis_size("var")
    lat_place = lax.axis_index("lat")
    ext_rows = band_rows + WH
    ext_cols = band_cols + WW
    extended = padded(patches, (("lat", 0),), half_rows, False)
    extended = padded(extended, (("var", 1),), half_cols, True)
    normed_ext = layer_norm(extended, norm_gain)
    keyval = jnp.dot(
        normed_ext.reshape(-1, width), input_proj[:, width:], preferred_element_type=jnp.float32
    )
    keyval = keyval.astype(jnp.bfloat16).reshape(ext_rows, ext_cols, 2 * width)
    normed = normed_ext[half_rows : half_rows + band_rows, half_cols : half_cols + band_cols]
    queries = jnp.dot(
        normed.reshape(-1, width), input_proj[:, :width], preferred_element_type=jnp.float32
    )
    queries = queries.astype(jnp.bfloat16).reshape(band_rows, band_cols, width)
    query_ext = jnp.pad(queries, ((half_rows, WH - half_rows), (half_cols, WW - half_cols), (0, 0)))
    global_row = lat_place * band_rows - half_rows + jnp.arange(ext_rows, dtype=jnp.int32)
    row_valid = (global_row >= 0) & (global_row < lat_count * band_rows)
    mixed = window_attention(query_ext, keyval, row_valid, HEADS)
    attn = mixed[half_rows : half_rows + band_rows, half_cols : half_cols + band_cols].astype(
        jnp.bfloat16
    )
    update = jnp.dot(
        attn.reshape(-1, width), output_proj, preferred_element_type=jnp.float32
    ).reshape(band_rows, band_cols, width)
    latent = (patches.astype(jnp.float32) + update).astype(jnp.bfloat16)
    dataset_row = tile_dataset[0]
    dataset_ids = jnp.arange(level_counts.shape[0], dtype=jnp.int32)
    tile_levels = jnp.sum(
        jnp.where(dataset_row[:, None] == dataset_ids[None, :], level_counts[None, :], 0), axis=1
    )
    live_tiles = (slot_level[None, :] < tile_levels[:, None]).astype(jnp.float32)
    heads_full = lax.all_gather(head_weight, "lat", axis=1, tiled=True)
    tile_ids = jnp.arange(var_count, dtype=jnp.int32)
    piece = lax.all_gather(latent, "var", axis=1, tiled=True)
    piece_cols = piece.shape[1]
    column_tile = jnp.arange(piece_cols, dtype=jnp.int32) // band_cols
    onehot = (column_tile[:, None] == tile_ids[None, :]).astype(jnp.float32)
    column_live = jnp.dot(onehot, live_tiles)
    piece_grad, head_add = slot_terms(
        piece, targets, column_live.T, level_scale, level_shift, heads_full
    )
    latent_terms = piece_grad
    latent_terms, head_terms = (latent_terms, head_add)
    grad_latent = lax.psum_scatter(
        latent_terms.astype(jnp.bfloat16), "var", scatter_dimension=1, tiled=True
    )
    head_terms = head_terms * (1.0 / math.sqrt(lat_count * band_rows * var_count * band_cols))
    mine = lax.psum_scatter(
        head_terms.astype(jnp.bfloat16), "lat", scatter_dimension=0, tiled=True
    ).astype(jnp.float32)
    grad_head = jnp.transpose(mine, (1, 0, 2))
    return (latent, grad_latent, grad_head)


def solution(mesh):
    in_specs = (
        P("lat", "var", None),
        P(),
        P(),
        P(),
        P("var", None),
        P("var", None),
        P("var", "lat", None),
        P("var", "lat", None, None),
        P(),
        P("lat", None),
        P("var"),
    )
    fast = mesh.shape["lat"] == 8 and mesh.shape["var"] == 4
    body = fast_local if fast else local
    out_specs = (P("lat", "var", None), P("lat", "var", None), P("var", "lat", None))
    return jax.shard_map(body, mesh=mesh, in_specs=in_specs, out_specs=out_specs, check_vma=False)
```

```python
import functools
import math

import jax
import jax.numpy as jnp
import numpy as np
from jax import lax
from jax.experimental import pallas as pl
from jax.experimental.pallas import tpu as pltpu
from jax.sharding import PartitionSpec as P

HEADS = 16
WH = 6
WW = 12
EPS = 1e-05
HR = WH // 2
HC = WW // 2
QP = 48
VMEM_LIMIT = 48 * 1024 * 1024
F32 = jnp.float32
BF16 = jnp.bfloat16


def gather_maps(cols):
    win_cols = cols // WW
    windows = 2 * win_cols
    into = np.zeros((windows * 2 * QP, 2 * WH * cols), np.float32)
    back = np.zeros((WH * cols, windows * QP), np.float32)
    for win in range(windows):
        win_row, win_col = divmod(win, win_cols)
        for row in range(HR):
            for c in range(WW):
                own = (win_row * HR + row) * cols + win_col * WW + c
                slot = row * WW + c
                into[win * 2 * QP + slot, own] = 1
                into[win * 2 * QP + QP + slot, WH * cols + own] = 1
                back[own, win * QP + slot] = 1
    return into, back


def attention_kernel(
    bands,
    place,
    own,
    above,
    below,
    gain,
    maps_hbm,
    in_hbm,
    out_hbm,
    out,
    raw,
    qkv,
    attn,
    maps,
    proj_in,
    proj_out,
    sems,
):
    moves = [
        pltpu.make_async_copy(src, dst, sems.at[i])
        for i, (src, dst) in enumerate(((maps_hbm, maps), (in_hbm, proj_in), (out_hbm, proj_out)))
    ]
    for move in moves:
        move.start()
    cols, width = own.shape[1], own.shape[2]
    win_cols = cols // WW
    windows = 2 * win_cols
    slots = windows * 2 * QP
    head_size = width // HEADS
    quad = 256 // head_size
    size = WH * cols
    start = 0
    for ref in (own, above, below):
        count = ref.shape[0] * cols
        raw[start : start + count, :] = ref[...].astype(F32).reshape(count, width)
        start += count
    wide = raw[...]
    average = jnp.mean(wide, axis=-1, keepdims=True)
    centred = wide - average
    variance = jnp.mean(centred * centred, axis=-1, keepdims=True)
    normed = (centred * lax.rsqrt(variance + EPS) * gain[...]).astype(BF16)
    moves[0].wait()
    win_x = jnp.dot(maps[0:slots, :], normed, preferred_element_type=F32).astype(BF16)
    moves[1].wait()
    step = 512
    for j in range(3 * width // step):
        part = slice(j * step, (j + 1) * step)
        qkv[:, part] = jnp.dot(win_x, proj_in[:, part], preferred_element_type=F32).astype(BF16)
    lane = lax.broadcasted_iota(jnp.int32, (1, 256), 1) // head_size
    heads = [jnp.where(lane == h, 1.0, 0.0) for h in range(quad)]
    key_id = lax.broadcasted_iota(jnp.int32, (1, 2 * QP), 1)
    scale = 1.0 / math.sqrt(head_size)
    for win in range(windows):
        win_row = win // win_cols
        edge = 0 if win_row == 0 else bands - 1
        has_halo = place[0] != edge
        halo_keys = jnp.logical_and(key_id >= QP, key_id < QP + HR * WW)
        valid = jnp.logical_or(key_id < HR * WW, jnp.logical_and(halo_keys, has_halo))
        bias = jnp.where(valid, 0.0, -1e30)
        row0 = win * 2 * QP
        for g in range(width // 256):
            lanes = slice(g * 256, (g + 1) * 256)
            query = qkv[row0 : row0 + QP, lanes].astype(F32) * scale
            stacked = jnp.concatenate([query * h for h in heads], axis=0).astype(BF16)
            key = qkv[row0 : row0 + 2 * QP, width + g * 256 : width + (g + 1) * 256]
            value = qkv[row0 : row0 + 2 * QP, 2 * width + g * 256 : 2 * width + (g + 1) * 256]
            scores = (
                lax.dot_general(
                    stacked, key, (((1,), (1,)), ((), ())), preferred_element_type=F32
                )
                + bias
            )
            weights = jnp.exp(scores - jnp.max(scores, axis=-1, keepdims=True))
            probs = (weights / jnp.sum(weights, axis=-1, keepdims=True)).astype(BF16)
            mixed = jnp.dot(probs, value, preferred_element_type=F32)
            chosen = mixed[0:QP] * heads[0]
            for h in range(1, quad):
                chosen = chosen + mixed[h * QP : (h + 1) * QP] * heads[h]
            attn[win * QP : (win + 1) * QP, lanes] = chosen.astype(BF16)
    back = maps[slots : slots + size, 0 : windows * QP]
    ordered = jnp.dot(back, attn[...], preferred_element_type=F32).astype(BF16)
    moves[2].wait()
    update = jnp.dot(ordered, proj_out[...], preferred_element_type=F32)
    out[...] = (raw[0:size, :] + update).astype(BF16)


def attention(place, pieces, gain, proj_in, proj_out, bands):
    rows, cols, width = pieces[0].shape
    into, back = gather_maps(cols)
    total = into.shape[1]
    windows = 2 * (cols // WW)
    back = np.pad(back, ((0, 0), (0, total - back.shape[1])))
    maps = np.concatenate([into, back])
    vmem = pl.BlockSpec(memory_space=pltpu.VMEM)
    hbm = pl.BlockSpec(memory_space=pltpu.HBM)
    return pl.pallas_call(
        functools.partial(attention_kernel, bands),
        out_shape=jax.ShapeDtypeStruct((rows * cols, width), BF16),
        in_specs=[pl.BlockSpec(memory_space=pltpu.SMEM)] + [vmem] * 4 + [hbm] * 3,
        out_specs=vmem,
        scratch_shapes=[
            pltpu.VMEM((total, width), F32),
            pltpu.VMEM((windows * 2 * QP, 3 * width), BF16),
            pltpu.VMEM((windows * QP, width), BF16),
            pltpu.VMEM(maps.shape, BF16),
            pltpu.VMEM(proj_in.shape, BF16),
            pltpu.VMEM(proj_out.shape, BF16),
            pltpu.SemaphoreType.DMA((3,)),
        ],
        compiler_params=pltpu.CompilerParams(vmem_limit_bytes=53 * 1024 * 1024),
        cost_estimate=pl.CostEstimate(
            flops=6_000_000_000, bytes_accessed=12_000_000, transcendentals=400_000
        ),
        name="window_attention",
    )(
        place,
        *pieces,
        gain.reshape(1, width),
        jnp.asarray(maps, BF16),
        proj_in,
        proj_out,
    )


def band_map(tiles, cols):
    wide = tiles * cols
    chosen = np.zeros((WH * wide, WH * wide), np.float32)
    for r in range(WH):
        for c in range(wide):
            tile, at = divmod((c + HC) % wide, cols)
            chosen[r * wide + c, tile * WH * cols + r * cols + at] = 1
    return chosen


def order_band(tiles, cols, var, chosen, pieces, laid, wide, band, latent):
    size = WH * cols
    for s in range(tiles):
        tile = lax.rem(var + tiles - s, tiles)
        laid[pl.ds(pl.multiple_of(tile * size, 16), size), :] = pieces[s][...]
    wide[...] = jnp.dot(chosen[...], laid[...], preferred_element_type=F32)
    band[...] = wide[...].astype(BF16)
    for r in range(WH):
        start = pl.multiple_of(r * tiles * cols + var * cols, 8)
        latent[r] = wide[pl.ds(start, cols), :].astype(BF16)


def slot_errors(level, tile_counts, rows, weight, target):
    predicted = lax.dot_general(
        rows, weight, (((1,), (1,)), ((), ())), preferred_element_type=F32
    )
    live = jnp.where(level < tile_counts, 1.0, 0.0)
    diff = predicted - target.astype(F32).reshape(predicted.shape)
    return (diff * live).astype(BF16)


def head_halves(k, lats, lat, errors, rows, turned, keep, send):
    turned[k] = lax.dot_general(
        errors, rows, (((0,), (0,)), ((), ())), preferred_element_type=F32
    ).astype(BF16)
    piece = turned.shape[-1] // lats
    for q in range(lats):
        core, x, y = q & 1, (q >> 1) & 1, (q >> 2) & 1
        outer, inner = (x, y) if k == 0 else (y, x)
        start = pl.multiple_of(jnp.bitwise_xor(lat, q) * piece, piece)
        to = send if core else keep
        to[k, outer, inner, 0] = turned[k, :, pl.ds(start, piece)]


def add_back(lats, errs, gathered, scale, total):
    piece = gathered.shape[-1]
    for l in range(0, lats, 2):
        lanes = slice(l * piece, (l + 2) * piece)
        term = 0.0
        for k in range(2):
            weight = jnp.concatenate([gathered[l, k], gathered[l + 1, k]], axis=1)
            factor = scale[k][:, lanes]
            term = term + jnp.dot(errs[k], weight, preferred_element_type=F32) * factor
        total[:, lanes] += term


def slot_kernel(
    first_slot,
    lats,
    tiles,
    final,
    place,
    counts,
    datasets,
    levels,
    tile_of,
    scale,
    shift,
    gathered,
    target,
    *refs,
):
    if final:
        band, before, keep, send, out, total, rows0, rows1, errs, turned, tile_counts = refs
    else:
        chosen, pieces = refs[0], refs[1 : 1 + tiles]
        keep, send, total, band, latent, rows0, rows1, errs, turned, tile_counts = refs[1 + tiles :]
    rows = (rows0, rows1)
    step, steps = pl.program_id(0), pl.num_programs(0)
    slot = first_slot + 2 * step

    @pl.when(step == 0)
    def _():
        if final:
            total[...] = before[...]
        else:
            order_band(tiles, latent.shape[1], place[1], chosen, pieces, rows0, total, band, latent)
            total[...] = jnp.zeros_like(total)
        tile = tile_of[...]
        wanted = jnp.zeros_like(tile)
        for t in range(tiles):
            wanted = jnp.where(tile == t, counts[datasets[0, t]], wanted)
        tile_counts[...] = wanted

    for k in range(2):
        rows[k][...] = band[...] * scale[k].astype(BF16) + shift[k].astype(BF16)
    for k in range(2):
        weight = jnp.concatenate([gathered[l, k] for l in range(lats)], axis=1)
        errs[k] = slot_errors(levels[slot + k], tile_counts[...], rows[k][...], weight, target[k])
    for k in range(2):
        head_halves(k, lats, place[0], errs[k], rows[k][...], turned, keep, send)
    add_back(lats, errs, gathered, scale, total)

    if final:

        @pl.when(step == steps - 1)
        def _():
            cols = out.shape[2]
            for s in range(tiles):
                for r in range(WH):
                    start = (r * tiles + s) * cols
                    out[s, r] = total[start : start + cols, :].astype(BF16)


def slot_group(pair, pairs, lats, place, small, tile_of, scale, shift, gathered, targets, pieces, before):
    places, width = tile_of.shape[0], scale.shape[-1]
    outs = targets.shape[-1]
    tiles = small[1].shape[1]
    piece = width // lats
    cols = places // (WH * tiles)
    smem = pl.BlockSpec(memory_space=pltpu.SMEM)
    fixed = lambda shape: pl.BlockSpec(shape, lambda i: (0,) * len(shape))
    halves = jax.ShapeDtypeStruct((2, 2, 2, pairs, outs, piece), BF16)
    half_spec = pl.BlockSpec((2, 2, 2, 1, outs, piece), lambda i: (0, 0, 0, i, 0, 0))
    level_spec = pl.BlockSpec((2, 1, width), lambda i: (i + pair, 0, 0))
    in_specs = [smem] * 4 + [
        fixed(tile_of.shape),
        level_spec,
        level_spec,
        pl.BlockSpec((lats, 2, outs, piece), lambda i: (0, i + pair, 0, 0)),
        pl.BlockSpec((2,) + targets.shape[1:], lambda i: (i + pair, 0, 0, 0)),
    ]
    args = [place, *small, tile_of, scale, shift, gathered, targets]
    final = before is not None
    scratch = [
        pltpu.VMEM((places, width), BF16),
        pltpu.VMEM((places, width), BF16),
        pltpu.VMEM((2, places, outs), BF16),
        pltpu.VMEM((2, outs, width), BF16),
        pltpu.VMEM((places, 1), jnp.int32),
    ]
    sums = jax.ShapeDtypeStruct((places, width), F32)
    if final:
        args.extend(before)
        scratch.insert(0, pltpu.VMEM(sums.shape, F32))
        results = [jax.ShapeDtypeStruct((tiles, WH, cols, width), BF16)]
    else:
        args.extend([jnp.asarray(band_map(tiles, cols), BF16), *pieces])
        results = [
            sums,
            jax.ShapeDtypeStruct((places, width), BF16),
            jax.ShapeDtypeStruct((WH, cols, width), BF16),
        ]
    in_specs.extend(fixed(arg.shape) for arg in args[len(in_specs) :])
    limit = (45 if final else 48) * 1024 * 1024
    return pl.pallas_call(
        functools.partial(slot_kernel, 2 * pair, lats, tiles, final),
        grid=(pairs,),
        out_shape=(halves, halves, *results),
        in_specs=in_specs,
        out_specs=(half_spec, half_spec, *(fixed(r.shape) for r in results)),
        scratch_shapes=scratch,
        compiler_params=pltpu.CompilerParams(vmem_limit_bytes=limit),
        cost_estimate=pl.CostEstimate(
            flops=pairs * 12 * places * width * outs, bytes_accessed=pairs * 5_000_000, transcendentals=0
        ),
        name="slot_group",
    )(*args)


def halve_kernel(keep, came, *refs):
    outs = refs[-4:]
    for k in range(2):
        for half in range(2):
            total = keep[k, half].astype(F32) + came[k, half].astype(F32)
            outs[2 * half + k][...] = total.astype(BF16)


def halve(keep, came, after):
    part = jax.ShapeDtypeStruct(keep.shape[2:], BF16)
    vmem = pl.BlockSpec(memory_space=pltpu.VMEM)
    out = pl.pallas_call(
        halve_kernel,
        out_shape=(part,) * 4,
        in_specs=[vmem, vmem] + [pl.BlockSpec(memory_space=pl.ANY)] * len(after),
        out_specs=(vmem,) * 4,
        compiler_params=pltpu.CompilerParams(vmem_limit_bytes=24 * 1024 * 1024),
        cost_estimate=pl.CostEstimate(flops=2_000_000, bytes_accessed=6_000_000, transcendentals=0),
        name="halve",
    )(keep, came, *after)
    return out[0:2], out[2:4]


def join_kernel(norm, *refs):
    out = refs[-1]
    pairs = refs[:-1]
    slot = 0
    for i in range(0, len(pairs), 4):
        for k in range(pairs[i].shape[0]):
            for kept, came in (pairs[i : i + 2], pairs[i + 2 : i + 4]):
                out[slot] = (kept[k].astype(F32) + came[k].astype(F32)) * norm
                slot += 1


def join_heads(pairs, norm):
    flat = [array for pair in pairs for array in pair]
    slots = sum(kept.shape[0] for kept, _ in pairs)
    _, outs, piece = flat[0].shape
    vmem = pl.BlockSpec(memory_space=pltpu.VMEM)
    return pl.pallas_call(
        functools.partial(join_kernel, norm),
        out_shape=jax.ShapeDtypeStruct((slots, outs, piece), F32),
        in_specs=[vmem] * len(flat),
        out_specs=vmem,
        compiler_params=pltpu.CompilerParams(vmem_limit_bytes=VMEM_LIMIT),
        cost_estimate=pl.CostEstimate(flops=1_000_000, bytes_accessed=4_000_000, transcendentals=0),
        name="join_heads",
    )(*flat)


def fast_local(
    patches, norm_gain, input_proj, output_proj, level_scale, level_shift, head_weight, targets,
    level_counts, tile_dataset, slot_level,
):
    rows, cols, width = patches.shape
    lats, tiles = lax.axis_size("lat"), lax.axis_size("var")
    slots = head_weight.shape[0]
    lat, var = lax.axis_index("lat"), lax.axis_index("var")
    place = jnp.stack([lat, var]).astype(jnp.int32)
    gathered = lax.all_gather(jnp.transpose(head_weight, (0, 2, 1)), "lat", axis=0, tiled=False)

    right = [(i, (i + 1) % tiles) for i in range(tiles)]
    up = [(i, i + 1) for i in range(lats - 1)]
    down = [(i + 1, i) for i in range(lats - 1)]
    left = lax.ppermute(patches[:, cols - HC :], "var", right)
    shifted = jnp.concatenate([left, patches[:, : cols - HC]], axis=1)
    above = lax.ppermute(shifted[HR:], "lat", up)
    below = lax.ppermute(shifted[:HR], "lat", down)
    mine = attention(place, (shifted, above, below), norm_gain, input_proj, output_proj, lats)
    pieces = [mine]
    for s in range(1, tiles):
        pieces.append(lax.ppermute(mine, "var", [(i, (i + s) % tiles) for i in range(tiles)]))

    tile_of = jnp.asarray(np.arange(rows * tiles * cols)[:, None] % (tiles * cols) // cols, jnp.int32)
    scale3, shift3 = level_scale.reshape(slots, 1, width), level_shift.reshape(slots, 1, width)
    small = (level_counts, tile_dataset, slot_level)
    flip = lambda array, bit: lax.ppermute(array, "lat", [(i, i ^ bit) for i in range(lats)])
    add = lambda a, b: (a.astype(F32) + b.astype(F32)).astype(BF16)
    common = (lats, place, small, tile_of, scale3, shift3, gathered, targets)
    most = slots // 2 - 1
    bits = (2, 4)
    keep_a, send_a, so_far, band, latent = slot_group(0, most, *common, pieces, None)
    keep_b, send_b, terms = slot_group(most, slots // 2 - most, *common, None, (band, so_far))
    grad_latent = lax.psum_scatter(terms, "var", scatter_dimension=0, tiled=False)
    pairs, after = [], [terms]
    for keep, send in ((keep_a, send_a), (keep_b, send_b)):
        kept, sent = halve(keep, flip(send, 1), after)
        after = list(sent)
        came = [flip(sent[k], bits[k]) for k in range(2)]
        for k in range(2):
            last = flip(add(kept[k][1], came[k][1]), bits[1 - k])
            pairs.append((add(kept[k][0], came[k][0]), last))
    grad_head = join_heads(pairs, 1.0 / math.sqrt(lats * rows * tiles * cols))
    return (latent, grad_latent, jnp.transpose(grad_head, (0, 2, 1)))


def padded(array, sides, width, wrap):
    for axis, dim in sides:
        size, length = (lax.axis_size(axis), array.shape[dim])
        up = [(i, (i + 1) % size) for i in range(size if wrap else size - 1)]
        down = [(j, i) for i, j in up]
        last = lax.slice_in_dim(array, length - width, length, axis=dim)
        initial = lax.slice_in_dim(array, 0, width, axis=dim)
        before = lax.ppermute(last, axis, up)
        after = lax.ppermute(initial, axis, down)
        array = jnp.concatenate([before, array, after], axis=dim)
    return array


def layer_norm(values, gain):
    wide = values.astype(jnp.float32)
    average = jnp.mean(wide, axis=-1, keepdims=True)
    centred = wide - average
    variance = jnp.mean(centred * centred, axis=-1, keepdims=True)
    return (centred * lax.rsqrt(variance + EPS) * gain).astype(jnp.bfloat16)


def window_attention(query_ext, keyval, row_valid, heads):
    ext_rows, ext_cols, width = query_ext.shape
    head_size = width // heads
    win_rows = ext_rows // WH
    win_cols = ext_cols // WW

    def split(values, parts):
        shaped = values.reshape(win_rows, WH, win_cols, WW, parts, heads, head_size)
        return shaped.transpose(0, 2, 1, 3, 4, 5, 6).reshape(
            win_rows * win_cols, WH * WW, parts, heads, head_size
        )

    query_win = split(query_ext, 1)[:, :, 0]
    pairs = split(keyval, 2)
    key_win = pairs[:, :, 0]
    value_win = pairs[:, :, 1]
    key_mask = jnp.broadcast_to(
        row_valid.reshape(win_rows, 1, WH, 1), (win_rows, win_cols, WH, WW)
    ).reshape(win_rows * win_cols, WH * WW)
    scores = jnp.einsum(
        "wqhd,wkhd->whqk", query_win, key_win, preferred_element_type=jnp.float32
    ) / math.sqrt(head_size)
    scores = jnp.where(key_mask[:, None, None, :], scores, -jnp.inf)
    peak = jnp.max(scores, axis=-1, keepdims=True)
    weights = jnp.exp(scores - peak)
    probs = (weights / jnp.sum(weights, axis=-1, keepdims=True)).astype(jnp.bfloat16)
    mixed = jnp.einsum("whqk,wkhd->wqhd", probs, value_win, preferred_element_type=jnp.float32)
    return (
        mixed.reshape(win_rows, win_cols, WH, WW, width)
        .transpose(0, 2, 1, 3, 4)
        .reshape(ext_rows, ext_cols, width)
    )


def slot_terms(piece, target_rows, live_cols, level_scale, level_shift, heads_full):
    piece_wide = piece.astype(jnp.float32)
    rows = (
        piece_wide[None] * level_scale[:, None, None, :] + level_shift[:, None, None, :]
    ).astype(jnp.bfloat16)
    predicted = jnp.einsum("krnd,kdo->krno", rows, heads_full, preferred_element_type=jnp.float32)
    errors = ((predicted - target_rows.astype(jnp.float32)) * live_cols[:, None, :, None]).astype(
        jnp.bfloat16
    )
    back_grad = jnp.einsum("krno,kdo->krnd", errors, heads_full, preferred_element_type=jnp.float32)
    piece_grad = jnp.sum(back_grad * level_scale[:, None, None, :], axis=0)
    head_add = jnp.einsum("krnd,krno->dko", rows, errors, preferred_element_type=jnp.float32)
    return (piece_grad, head_add)


def local(
    patches,
    norm_gain,
    input_proj,
    output_proj,
    level_scale,
    level_shift,
    head_weight,
    targets,
    level_counts,
    tile_dataset,
    slot_level,
):
    band_rows, band_cols, width = patches.shape
    half_rows = WH // 2
    half_cols = WW // 2
    lat_count = lax.axis_size("lat")
    var_count = lax.axis_size("var")
    lat_place = lax.axis_index("lat")
    ext_rows = band_rows + WH
    ext_cols = band_cols + WW
    extended = padded(patches, (("lat", 0),), half_rows, False)
    extended = padded(extended, (("var", 1),), half_cols, True)
    normed_ext = layer_norm(extended, norm_gain)
    keyval = jnp.dot(
        normed_ext.reshape(-1, width), input_proj[:, width:], preferred_element_type=jnp.float32
    )
    keyval = keyval.astype(jnp.bfloat16).reshape(ext_rows, ext_cols, 2 * width)
    normed = normed_ext[half_rows : half_rows + band_rows, half_cols : half_cols + band_cols]
    queries = jnp.dot(
        normed.reshape(-1, width), input_proj[:, :width], preferred_element_type=jnp.float32
    )
    queries = queries.astype(jnp.bfloat16).reshape(band_rows, band_cols, width)
    query_ext = jnp.pad(queries, ((half_rows, WH - half_rows), (half_cols, WW - half_cols), (0, 0)))
    global_row = lat_place * band_rows - half_rows + jnp.arange(ext_rows, dtype=jnp.int32)
    row_valid = (global_row >= 0) & (global_row < lat_count * band_rows)
    mixed = window_attention(query_ext, keyval, row_valid, HEADS)
    attn = mixed[half_rows : half_rows + band_rows, half_cols : half_cols + band_cols].astype(
        jnp.bfloat16
    )
    update = jnp.dot(
        attn.reshape(-1, width), output_proj, preferred_element_type=jnp.float32
    ).reshape(band_rows, band_cols, width)
    latent = (patches.astype(jnp.float32) + update).astype(jnp.bfloat16)
    dataset_row = tile_dataset[0]
    dataset_ids = jnp.arange(level_counts.shape[0], dtype=jnp.int32)
    tile_levels = jnp.sum(
        jnp.where(dataset_row[:, None] == dataset_ids[None, :], level_counts[None, :], 0), axis=1
    )
    live_tiles = (slot_level[None, :] < tile_levels[:, None]).astype(jnp.float32)
    heads_full = lax.all_gather(head_weight, "lat", axis=1, tiled=True)
    tile_ids = jnp.arange(var_count, dtype=jnp.int32)
    piece = lax.all_gather(latent, "var", axis=1, tiled=True)
    piece_cols = piece.shape[1]
    column_tile = jnp.arange(piece_cols, dtype=jnp.int32) // band_cols
    onehot = (column_tile[:, None] == tile_ids[None, :]).astype(jnp.float32)
    column_live = jnp.dot(onehot, live_tiles)
    piece_grad, head_add = slot_terms(
        piece, targets, column_live.T, level_scale, level_shift, heads_full
    )
    latent_terms = piece_grad
    latent_terms, head_terms = (latent_terms, head_add)
    grad_latent = lax.psum_scatter(
        latent_terms.astype(jnp.bfloat16), "var", scatter_dimension=1, tiled=True
    )
    head_terms = head_terms * (1.0 / math.sqrt(lat_count * band_rows * var_count * band_cols))
    mine = lax.psum_scatter(
        head_terms.astype(jnp.bfloat16), "lat", scatter_dimension=0, tiled=True
    ).astype(jnp.float32)
    grad_head = jnp.transpose(mine, (1, 0, 2))
    return (latent, grad_latent, grad_head)


def solution(mesh):
    in_specs = (
        P("lat", "var", None),
        P(),
        P(),
        P(),
        P("var", None),
        P("var", None),
        P("var", "lat", None),
        P("var", "lat", None, None),
        P(),
        P("lat", None),
        P("var"),
    )
    fast = mesh.shape["lat"] == 8 and mesh.shape["var"] == 4
    body = fast_local if fast else local
    out_specs = (P("lat", "var", None), P("lat", "var", None), P("var", "lat", None))
    return jax.shard_map(body, mesh=mesh, in_specs=in_specs, out_specs=out_specs, check_vma=False)
```

```python
import functools
import math

import jax
import jax.numpy as jnp
import numpy as np
from jax import lax
from jax.experimental import pallas as pl
from jax.experimental.pallas import tpu as pltpu
from jax.sharding import PartitionSpec as P

HEADS = 16
WH = 6
WW = 12
EPS = 1e-05
HR = WH // 2
HC = WW // 2
QP = 48
VMEM_LIMIT = 48 * 1024 * 1024
F32 = jnp.float32
BF16 = jnp.bfloat16


def gather_maps(cols):
    win_cols = cols // WW
    windows = 2 * win_cols
    into = np.zeros((windows * 2 * QP, 2 * WH * cols), np.float32)
    back = np.zeros((WH * cols, windows * QP), np.float32)
    for win in range(windows):
        win_row, win_col = divmod(win, win_cols)
        for row in range(HR):
            for c in range(WW):
                own = (win_row * HR + row) * cols + win_col * WW + c
                slot = row * WW + c
                into[win * 2 * QP + slot, own] = 1
                into[win * 2 * QP + QP + slot, WH * cols + own] = 1
                back[own, win * QP + slot] = 1
    return into, back


def attention_kernel(
    bands,
    place,
    own,
    above,
    below,
    gain,
    maps_hbm,
    in_hbm,
    out_hbm,
    out,
    raw,
    qkv,
    attn,
    maps,
    proj_in,
    proj_out,
    sems,
):
    moves = [
        pltpu.make_async_copy(src, dst, sems.at[i])
        for i, (src, dst) in enumerate(((maps_hbm, maps), (in_hbm, proj_in), (out_hbm, proj_out)))
    ]
    for move in moves:
        move.start()
    cols, width = own.shape[1], own.shape[2]
    win_cols = cols // WW
    windows = 2 * win_cols
    slots = windows * 2 * QP
    head_size = width // HEADS
    quad = 256 // head_size
    size = WH * cols
    start = 0
    for ref in (own, above, below):
        count = ref.shape[0] * cols
        raw[start : start + count, :] = ref[...].astype(F32).reshape(count, width)
        start += count
    wide = raw[...]
    average = jnp.mean(wide, axis=-1, keepdims=True)
    centred = wide - average
    variance = jnp.mean(centred * centred, axis=-1, keepdims=True)
    normed = (centred * lax.rsqrt(variance + EPS) * gain[...]).astype(BF16)
    moves[0].wait()
    win_x = jnp.dot(maps[0:slots, :], normed, preferred_element_type=F32).astype(BF16)
    moves[1].wait()
    step = 512
    for j in range(3 * width // step):
        part = slice(j * step, (j + 1) * step)
        qkv[:, part] = jnp.dot(win_x, proj_in[:, part], preferred_element_type=F32).astype(BF16)
    lane = lax.broadcasted_iota(jnp.int32, (1, 256), 1) // head_size
    heads = [jnp.where(lane == h, 1.0, 0.0) for h in range(quad)]
    key_id = lax.broadcasted_iota(jnp.int32, (1, 2 * QP), 1)
    scale = 1.0 / math.sqrt(head_size)
    for win in range(windows):
        win_row = win // win_cols
        edge = 0 if win_row == 0 else bands - 1
        has_halo = place[0] != edge
        halo_keys = jnp.logical_and(key_id >= QP, key_id < QP + HR * WW)
        valid = jnp.logical_or(key_id < HR * WW, jnp.logical_and(halo_keys, has_halo))
        bias = jnp.where(valid, 0.0, -1e30)
        row0 = win * 2 * QP
        for g in range(width // 256):
            lanes = slice(g * 256, (g + 1) * 256)
            query = qkv[row0 : row0 + QP, lanes].astype(F32) * scale
            stacked = jnp.concatenate([query * h for h in heads], axis=0).astype(BF16)
            key = qkv[row0 : row0 + 2 * QP, width + g * 256 : width + (g + 1) * 256]
            value = qkv[row0 : row0 + 2 * QP, 2 * width + g * 256 : 2 * width + (g + 1) * 256]
            scores = (
                lax.dot_general(
                    stacked, key, (((1,), (1,)), ((), ())), preferred_element_type=F32
                )
                + bias
            )
            weights = jnp.exp(scores - jnp.max(scores, axis=-1, keepdims=True))
            probs = (weights / jnp.sum(weights, axis=-1, keepdims=True)).astype(BF16)
            mixed = jnp.dot(probs, value, preferred_element_type=F32)
            chosen = mixed[0:QP] * heads[0]
            for h in range(1, quad):
                chosen = chosen + mixed[h * QP : (h + 1) * QP] * heads[h]
            attn[win * QP : (win + 1) * QP, lanes] = chosen.astype(BF16)
    back = maps[slots : slots + size, 0 : windows * QP]
    ordered = jnp.dot(back, attn[...], preferred_element_type=F32).astype(BF16)
    moves[2].wait()
    update = jnp.dot(ordered, proj_out[...], preferred_element_type=F32)
    out[...] = (raw[0:size, :] + update).astype(BF16)


def attention(place, pieces, gain, proj_in, proj_out, bands):
    rows, cols, width = pieces[0].shape
    into, back = gather_maps(cols)
    total = into.shape[1]
    windows = 2 * (cols // WW)
    back = np.pad(back, ((0, 0), (0, total - back.shape[1])))
    maps = np.concatenate([into, back])
    vmem = pl.BlockSpec(memory_space=pltpu.VMEM)
    hbm = pl.BlockSpec(memory_space=pltpu.HBM)
    return pl.pallas_call(
        functools.partial(attention_kernel, bands),
        out_shape=jax.ShapeDtypeStruct((rows * cols, width), BF16),
        in_specs=[pl.BlockSpec(memory_space=pltpu.SMEM)] + [vmem] * 4 + [hbm] * 3,
        out_specs=vmem,
        scratch_shapes=[
            pltpu.VMEM((total, width), F32),
            pltpu.VMEM((windows * 2 * QP, 3 * width), BF16),
            pltpu.VMEM((windows * QP, width), BF16),
            pltpu.VMEM(maps.shape, BF16),
            pltpu.VMEM(proj_in.shape, BF16),
            pltpu.VMEM(proj_out.shape, BF16),
            pltpu.SemaphoreType.DMA((3,)),
        ],
        compiler_params=pltpu.CompilerParams(vmem_limit_bytes=53 * 1024 * 1024),
        cost_estimate=pl.CostEstimate(
            flops=6_000_000_000, bytes_accessed=12_000_000, transcendentals=400_000
        ),
        name="window_attention",
    )(
        place,
        *pieces,
        gain.reshape(1, width),
        jnp.asarray(maps, BF16),
        proj_in,
        proj_out,
    )


def band_map(tiles, cols):
    wide = tiles * cols
    chosen = np.zeros((WH * wide, WH * wide), np.float32)
    for r in range(WH):
        for c in range(wide):
            tile, at = divmod((c + HC) % wide, cols)
            chosen[r * wide + c, tile * WH * cols + r * cols + at] = 1
    return chosen


def order_band(tiles, cols, var, chosen, pieces, laid, wide, band, latent):
    size = WH * cols
    for s in range(tiles):
        tile = lax.rem(var + tiles - s, tiles)
        laid[pl.ds(pl.multiple_of(tile * size, 16), size), :] = pieces[s][...]
    wide[...] = jnp.dot(chosen[...], laid[...], preferred_element_type=F32)
    band[...] = wide[...].astype(BF16)
    for r in range(WH):
        start = pl.multiple_of(r * tiles * cols + var * cols, 8)
        latent[r] = wide[pl.ds(start, cols), :].astype(BF16)


def slot_errors(level, tile_counts, rows, weight, target):
    predicted = lax.dot_general(
        rows, weight, (((1,), (1,)), ((), ())), preferred_element_type=F32
    )
    live = jnp.where(level < tile_counts, 1.0, 0.0)
    diff = predicted - target.astype(F32).reshape(predicted.shape)
    return (diff * live).astype(BF16)


def head_halves(k, lats, lat, errors, rows, turned, keep, send):
    turned[k] = lax.dot_general(
        errors, rows, (((0,), (0,)), ((), ())), preferred_element_type=F32
    ).astype(BF16)
    piece = turned.shape[-1] // lats
    for q in range(lats):
        core, x, y = q & 1, (q >> 1) & 1, (q >> 2) & 1
        outer, inner = (x, y) if k == 0 else (y, x)
        start = pl.multiple_of(jnp.bitwise_xor(lat, q) * piece, piece)
        to = send if core else keep
        to[k, outer, inner, 0] = turned[k, :, pl.ds(start, piece)]


def add_back(lats, errs, gathered, scale, total):
    piece = gathered.shape[-1]
    for l in range(0, lats, 2):
        lanes = slice(l * piece, (l + 2) * piece)
        term = 0.0
        for k in range(2):
            weight = jnp.concatenate([gathered[l, k], gathered[l + 1, k]], axis=1)
            factor = scale[k][:, lanes]
            term = term + jnp.dot(errs[k], weight, preferred_element_type=F32) * factor
        total[:, lanes] += term


def slot_kernel(
    first_slot,
    lats,
    tiles,
    final,
    place,
    counts,
    datasets,
    levels,
    tile_of,
    scale,
    shift,
    gathered,
    target,
    *refs,
):
    if final:
        band, before, keep, send, out, total, rows0, rows1, errs, turned, tile_counts = refs
    else:
        chosen, pieces = refs[0], refs[1 : 1 + tiles]
        keep, send, total, band, latent, rows0, rows1, errs, turned, tile_counts = refs[1 + tiles :]
    rows = (rows0, rows1)
    step, steps = pl.program_id(0), pl.num_programs(0)
    slot = first_slot + 2 * step

    @pl.when(step == 0)
    def _():
        if final:
            total[...] = before[...]
        else:
            order_band(tiles, latent.shape[1], place[1], chosen, pieces, rows0, total, band, latent)
            total[...] = jnp.zeros_like(total)
        tile = tile_of[...]
        wanted = jnp.zeros_like(tile)
        for t in range(tiles):
            wanted = jnp.where(tile == t, counts[datasets[0, t]], wanted)
        tile_counts[...] = wanted

    for k in range(2):
        rows[k][...] = (band[...].astype(F32) * scale[k] + shift[k]).astype(BF16)
    for k in range(2):
        weight = jnp.concatenate([gathered[l, k] for l in range(lats)], axis=1)
        errs[k] = slot_errors(levels[slot + k], tile_counts[...], rows[k][...], weight, target[k])
    for k in range(2):
        head_halves(k, lats, place[0], errs[k], rows[k][...], turned, keep, send)
    add_back(lats, errs, gathered, scale, total)

    if final:

        @pl.when(step == steps - 1)
        def _():
            cols = out.shape[2]
            for s in range(tiles):
                for r in range(WH):
                    start = (r * tiles + s) * cols
                    out[s, r] = total[start : start + cols, :].astype(BF16)


def slot_group(pair, pairs, lats, place, small, tile_of, scale, shift, gathered, targets, pieces, before):
    places, width = tile_of.shape[0], scale.shape[-1]
    outs = targets.shape[-1]
    tiles = small[1].shape[1]
    piece = width // lats
    cols = places // (WH * tiles)
    smem = pl.BlockSpec(memory_space=pltpu.SMEM)
    fixed = lambda shape: pl.BlockSpec(shape, lambda i: (0,) * len(shape))
    halves = jax.ShapeDtypeStruct((2, 2, 2, pairs, outs, piece), BF16)
    half_spec = pl.BlockSpec((2, 2, 2, 1, outs, piece), lambda i: (0, 0, 0, i, 0, 0))
    level_spec = pl.BlockSpec((2, 1, width), lambda i: (i + pair, 0, 0))
    in_specs = [smem] * 4 + [
        fixed(tile_of.shape),
        level_spec,
        level_spec,
        pl.BlockSpec((lats, 2, outs, piece), lambda i: (0, i + pair, 0, 0)),
        pl.BlockSpec((2,) + targets.shape[1:], lambda i: (i + pair, 0, 0, 0)),
    ]
    args = [place, *small, tile_of, scale, shift, gathered, targets]
    final = before is not None
    scratch = [
        pltpu.VMEM((places, width), BF16),
        pltpu.VMEM((places, width), BF16),
        pltpu.VMEM((2, places, outs), BF16),
        pltpu.VMEM((2, outs, width), BF16),
        pltpu.VMEM((places, 1), jnp.int32),
    ]
    sums = jax.ShapeDtypeStruct((places, width), F32)
    if final:
        args.extend(before)
        scratch.insert(0, pltpu.VMEM(sums.shape, F32))
        results = [jax.ShapeDtypeStruct((tiles, WH, cols, width), BF16)]
    else:
        args.extend([jnp.asarray(band_map(tiles, cols), BF16), *pieces])
        results = [
            sums,
            jax.ShapeDtypeStruct((places, width), BF16),
            jax.ShapeDtypeStruct((WH, cols, width), BF16),
        ]
    in_specs.extend(fixed(arg.shape) for arg in args[len(in_specs) :])
    limit = (45 if final else 48) * 1024 * 1024
    return pl.pallas_call(
        functools.partial(slot_kernel, 2 * pair, lats, tiles, final),
        grid=(pairs,),
        out_shape=(halves, halves, *results),
        in_specs=in_specs,
        out_specs=(half_spec, half_spec, *(fixed(r.shape) for r in results)),
        scratch_shapes=scratch,
        compiler_params=pltpu.CompilerParams(vmem_limit_bytes=limit),
        cost_estimate=pl.CostEstimate(
            flops=pairs * 12 * places * width * outs, bytes_accessed=pairs * 5_000_000, transcendentals=0
        ),
        name="slot_group",
    )(*args)


def halve_kernel(keep, came, *refs):
    outs = refs[-4:]
    for k in range(2):
        for half in range(2):
            total = keep[k, half].astype(F32) + came[k, half].astype(F32)
            outs[2 * half + k][...] = total.astype(BF16)


def halve(keep, came, after):
    part = jax.ShapeDtypeStruct(keep.shape[2:], BF16)
    vmem = pl.BlockSpec(memory_space=pltpu.VMEM)
    out = pl.pallas_call(
        halve_kernel,
        out_shape=(part,) * 4,
        in_specs=[vmem, vmem] + [pl.BlockSpec(memory_space=pl.ANY)] * len(after),
        out_specs=(vmem,) * 4,
        compiler_params=pltpu.CompilerParams(vmem_limit_bytes=24 * 1024 * 1024),
        cost_estimate=pl.CostEstimate(flops=2_000_000, bytes_accessed=6_000_000, transcendentals=0),
        name="halve",
    )(keep, came, *after)
    return out[0:2], out[2:4]


def join_kernel(norm, *refs):
    out = refs[-1]
    pairs = refs[:-1]
    slot = 0
    for i in range(0, len(pairs), 4):
        for k in range(pairs[i].shape[0]):
            for kept, came in (pairs[i : i + 2], pairs[i + 2 : i + 4]):
                out[slot] = (kept[k].astype(F32) + came[k].astype(F32)) * norm
                slot += 1


def join_heads(pairs, norm):
    flat = [array for pair in pairs for array in pair]
    slots = sum(kept.shape[0] for kept, _ in pairs)
    _, outs, piece = flat[0].shape
    vmem = pl.BlockSpec(memory_space=pltpu.VMEM)
    return pl.pallas_call(
        functools.partial(join_kernel, norm),
        out_shape=jax.ShapeDtypeStruct((slots, outs, piece), F32),
        in_specs=[vmem] * len(flat),
        out_specs=vmem,
        compiler_params=pltpu.CompilerParams(vmem_limit_bytes=VMEM_LIMIT),
        cost_estimate=pl.CostEstimate(flops=1_000_000, bytes_accessed=4_000_000, transcendentals=0),
        name="join_heads",
    )(*flat)


def fast_local(
    patches, norm_gain, input_proj, output_proj, level_scale, level_shift, head_weight, targets,
    level_counts, tile_dataset, slot_level,
):
    rows, cols, width = patches.shape
    lats, tiles = lax.axis_size("lat"), lax.axis_size("var")
    slots = head_weight.shape[0]
    lat, var = lax.axis_index("lat"), lax.axis_index("var")
    place = jnp.stack([lat, var]).astype(jnp.int32)
    gathered = lax.all_gather(jnp.transpose(head_weight, (0, 2, 1)), "lat", axis=0, tiled=False)

    right = [(i, (i + 1) % tiles) for i in range(tiles)]
    up = [(i, i + 1) for i in range(lats - 1)]
    down = [(i + 1, i) for i in range(lats - 1)]
    left = lax.ppermute(patches[:, cols - HC :], "var", right)
    shifted = jnp.concatenate([left, patches[:, : cols - HC]], axis=1)
    above = lax.ppermute(shifted[HR:], "lat", up)
    below = lax.ppermute(shifted[:HR], "lat", down)
    mine = attention(place, (shifted, above, below), norm_gain, input_proj, output_proj, lats)
    pieces = [mine]
    for s in range(1, tiles):
        pieces.append(lax.ppermute(mine, "var", [(i, (i + s) % tiles) for i in range(tiles)]))

    tile_of = jnp.asarray(np.arange(rows * tiles * cols)[:, None] % (tiles * cols) // cols, jnp.int32)
    scale3, shift3 = level_scale.reshape(slots, 1, width), level_shift.reshape(slots, 1, width)
    small = (level_counts, tile_dataset, slot_level)
    flip = lambda array, bit: lax.ppermute(array, "lat", [(i, i ^ bit) for i in range(lats)])
    add = lambda a, b: (a.astype(F32) + b.astype(F32)).astype(BF16)
    common = (lats, place, small, tile_of, scale3, shift3, gathered, targets)
    most = slots // 4 + 1
    bits = (2, 4)
    keep_a, send_a, so_far, band, latent = slot_group(0, most, *common, pieces, None)
    keep_b, send_b, terms = slot_group(most, slots // 2 - most, *common, None, (band, so_far))
    grad_latent = lax.psum_scatter(terms, "var", scatter_dimension=0, tiled=False)
    pairs, after = [], [terms]
    for keep, send in ((keep_a, send_a), (keep_b, send_b)):
        kept, sent = halve(keep, flip(send, 1), after)
        after = list(sent)
        came = [flip(sent[k], bits[k]) for k in range(2)]
        for k in range(2):
            last = flip(add(kept[k][1], came[k][1]), bits[1 - k])
            pairs.append((add(kept[k][0], came[k][0]), last))
    grad_head = join_heads(pairs, 1.0 / math.sqrt(lats * rows * tiles * cols))
    return (latent, grad_latent, jnp.transpose(grad_head, (0, 2, 1)))


def padded(array, sides, width, wrap):
    for axis, dim in sides:
        size, length = (lax.axis_size(axis), array.shape[dim])
        up = [(i, (i + 1) % size) for i in range(size if wrap else size - 1)]
        down = [(j, i) for i, j in up]
        last = lax.slice_in_dim(array, length - width, length, axis=dim)
        initial = lax.slice_in_dim(array, 0, width, axis=dim)
        before = lax.ppermute(last, axis, up)
        after = lax.ppermute(initial, axis, down)
        array = jnp.concatenate([before, array, after], axis=dim)
    return array


def layer_norm(values, gain):
    wide = values.astype(jnp.float32)
    average = jnp.mean(wide, axis=-1, keepdims=True)
    centred = wide - average
    variance = jnp.mean(centred * centred, axis=-1, keepdims=True)
    return (centred * lax.rsqrt(variance + EPS) * gain).astype(jnp.bfloat16)


def window_attention(query_ext, keyval, row_valid, heads):
    ext_rows, ext_cols, width = query_ext.shape
    head_size = width // heads
    win_rows = ext_rows // WH
    win_cols = ext_cols // WW

    def split(values, parts):
        shaped = values.reshape(win_rows, WH, win_cols, WW, parts, heads, head_size)
        return shaped.transpose(0, 2, 1, 3, 4, 5, 6).reshape(
            win_rows * win_cols, WH * WW, parts, heads, head_size
        )

    query_win = split(query_ext, 1)[:, :, 0]
    pairs = split(keyval, 2)
    key_win = pairs[:, :, 0]
    value_win = pairs[:, :, 1]
    key_mask = jnp.broadcast_to(
        row_valid.reshape(win_rows, 1, WH, 1), (win_rows, win_cols, WH, WW)
    ).reshape(win_rows * win_cols, WH * WW)
    scores = jnp.einsum(
        "wqhd,wkhd->whqk", query_win, key_win, preferred_element_type=jnp.float32
    ) / math.sqrt(head_size)
    scores = jnp.where(key_mask[:, None, None, :], scores, -jnp.inf)
    peak = jnp.max(scores, axis=-1, keepdims=True)
    weights = jnp.exp(scores - peak)
    probs = (weights / jnp.sum(weights, axis=-1, keepdims=True)).astype(jnp.bfloat16)
    mixed = jnp.einsum("whqk,wkhd->wqhd", probs, value_win, preferred_element_type=jnp.float32)
    return (
        mixed.reshape(win_rows, win_cols, WH, WW, width)
        .transpose(0, 2, 1, 3, 4)
        .reshape(ext_rows, ext_cols, width)
    )


def slot_terms(piece, target_rows, live_cols, level_scale, level_shift, heads_full):
    piece_wide = piece.astype(jnp.float32)
    rows = (
        piece_wide[None] * level_scale[:, None, None, :] + level_shift[:, None, None, :]
    ).astype(jnp.bfloat16)
    predicted = jnp.einsum("krnd,kdo->krno", rows, heads_full, preferred_element_type=jnp.float32)
    errors = ((predicted - target_rows.astype(jnp.float32)) * live_cols[:, None, :, None]).astype(
        jnp.bfloat16
    )
    back_grad = jnp.einsum("krno,kdo->krnd", errors, heads_full, preferred_element_type=jnp.float32)
    piece_grad = jnp.sum(back_grad * level_scale[:, None, None, :], axis=0)
    head_add = jnp.einsum("krnd,krno->dko", rows, errors, preferred_element_type=jnp.float32)
    return (piece_grad, head_add)


def local(
    patches,
    norm_gain,
    input_proj,
    output_proj,
    level_scale,
    level_shift,
    head_weight,
    targets,
    level_counts,
    tile_dataset,
    slot_level,
):
    band_rows, band_cols, width = patches.shape
    half_rows = WH // 2
    half_cols = WW // 2
    lat_count = lax.axis_size("lat")
    var_count = lax.axis_size("var")
    lat_place = lax.axis_index("lat")
    ext_rows = band_rows + WH
    ext_cols = band_cols + WW
    extended = padded(patches, (("lat", 0),), half_rows, False)
    extended = padded(extended, (("var", 1),), half_cols, True)
    normed_ext = layer_norm(extended, norm_gain)
    keyval = jnp.dot(
        normed_ext.reshape(-1, width), input_proj[:, width:], preferred_element_type=jnp.float32
    )
    keyval = keyval.astype(jnp.bfloat16).reshape(ext_rows, ext_cols, 2 * width)
    normed = normed_ext[half_rows : half_rows + band_rows, half_cols : half_cols + band_cols]
    queries = jnp.dot(
        normed.reshape(-1, width), input_proj[:, :width], preferred_element_type=jnp.float32
    )
    queries = queries.astype(jnp.bfloat16).reshape(band_rows, band_cols, width)
    query_ext = jnp.pad(queries, ((half_rows, WH - half_rows), (half_cols, WW - half_cols), (0, 0)))
    global_row = lat_place * band_rows - half_rows + jnp.arange(ext_rows, dtype=jnp.int32)
    row_valid = (global_row >= 0) & (global_row < lat_count * band_rows)
    mixed = window_attention(query_ext, keyval, row_valid, HEADS)
    attn = mixed[half_rows : half_rows + band_rows, half_cols : half_cols + band_cols].astype(
        jnp.bfloat16
    )
    update = jnp.dot(
        attn.reshape(-1, width), output_proj, preferred_element_type=jnp.float32
    ).reshape(band_rows, band_cols, width)
    latent = (patches.astype(jnp.float32) + update).astype(jnp.bfloat16)
    dataset_row = tile_dataset[0]
    dataset_ids = jnp.arange(level_counts.shape[0], dtype=jnp.int32)
    tile_levels = jnp.sum(
        jnp.where(dataset_row[:, None] == dataset_ids[None, :], level_counts[None, :], 0), axis=1
    )
    live_tiles = (slot_level[None, :] < tile_levels[:, None]).astype(jnp.float32)
    heads_full = lax.all_gather(head_weight, "lat", axis=1, tiled=True)
    tile_ids = jnp.arange(var_count, dtype=jnp.int32)
    piece = lax.all_gather(latent, "var", axis=1, tiled=True)
    piece_cols = piece.shape[1]
    column_tile = jnp.arange(piece_cols, dtype=jnp.int32) // band_cols
    onehot = (column_tile[:, None] == tile_ids[None, :]).astype(jnp.float32)
    column_live = jnp.dot(onehot, live_tiles)
    piece_grad, head_add = slot_terms(
        piece, targets, column_live.T, level_scale, level_shift, heads_full
    )
    latent_terms = piece_grad
    latent_terms, head_terms = (latent_terms, head_add)
    grad_latent = lax.psum_scatter(
        latent_terms.astype(jnp.bfloat16), "var", scatter_dimension=1, tiled=True
    )
    head_terms = head_terms * (1.0 / math.sqrt(lat_count * band_rows * var_count * band_cols))
    mine = lax.psum_scatter(
        head_terms.astype(jnp.bfloat16), "lat", scatter_dimension=0, tiled=True
    ).astype(jnp.float32)
    grad_head = jnp.transpose(mine, (1, 0, 2))
    return (latent, grad_latent, grad_head)


def solution(mesh):
    in_specs = (
        P("lat", "var", None),
        P(),
        P(),
        P(),
        P("var", None),
        P("var", None),
        P("var", "lat", None),
        P("var", "lat", None, None),
        P(),
        P("lat", None),
        P("var"),
    )
    fast = mesh.shape["lat"] == 8 and mesh.shape["var"] == 4
    body = fast_local if fast else local
    out_specs = (P("lat", "var", None), P("lat", "var", None), P("var", "lat", None))
    return jax.shard_map(body, mesh=mesh, in_specs=in_specs, out_specs=out_specs, check_vma=False)
```
